32 devices in a mesh: replica: 8 (over z, x), shard: 4 (over y, core).
Axes of the slice: x: 2, y: 2, z: 4, core: 2. Of those that a mesh axis runs over, the one named last changes fastest.
Arguments:
- tokens: bfloat16 [16, 1024, 1024], P('replica', 'shard'), may hold values from -6 to 6
- qkv_weight: bfloat16 [1024, 3072], P('shard'), may hold values from -0.25 to 0.25
- qv_bias: bfloat16 [2048], P('shard'), may hold values from -3 to 3
- proj_weight: bfloat16 [1024, 1024], P('shard'), may hold values from -0.5 to 0.5
- proj_bias: bfloat16 [1024], P('shard'), may hold values from -3 to 3
- up_weight: bfloat16 [1024, 4096], P('shard'), may hold values from -0.1875 to 0.1875
- up_bias: bfloat16 [4096], P('shard'), may hold values from -3 to 3
- down_weight: bfloat16 [4096, 1024], P('shard'), may hold values from -0.09375 to 0.09375
- down_bias: bfloat16 [1024], P('shard'), may hold values from -3 to 3
- attn_gain: bfloat16 [1024], P('shard'), may hold values from 0.5 to 1.5
- attn_shift: bfloat16 [1024], P('shard'), may hold values from -3 to 3
- mlp_gain: bfloat16 [1024], P('shard'), may hold values from 0.5 to 1.5
- mlp_shift: bfloat16 [1024], P('shard'), may hold values from -3 to 3
- attn_scale: bfloat16 [1024], P('shard'), may hold values from 0.25 to 1.75
- mlp_scale: bfloat16 [1024], P('shard'), may hold values from 0.25 to 1.75
- cotangent: bfloat16 [16, 1024, 1024], P('replica', 'shard'), may hold values from -6 to 6
- image_count: int32 [8], replicated, may hold values from 1 to 2, 10 in all
Outputs:
- output: bfloat16 [16, 1024, 1024], P('replica', 'shard')
- grad_tokens: float32 [16, 1024, 1024], P('replica', 'shard')
- grad_qkv_weight: float32 [1024, 3072], P('shard')
- grad_qv_bias: float32 [2048], P('shard')
- grad_proj_weight: float32 [1024, 1024], P('shard')
- grad_proj_bias: float32 [1024], P('shard')
- grad_up_weight: float32 [1024, 4096], P('shard')
- grad_up_bias: float32 [4096], P('shard')
- grad_down_weight: float32 [4096, 1024], P('shard')
- grad_down_bias: float32 [1024], P('shard')
- grad_attn_gain: float32 [1024], P('shard')
- grad_attn_shift: float32 [1024], P('shard')
- grad_mlp_gain: float32 [1024], P('shard')
- grad_mlp_shift: float32 [1024], P('shard')
- grad_attn_scale: float32 [1024], P('shard')
- grad_mlp_scale: float32 [1024], P('shard')
The draws below stay inside these ranges and needn't reach their ends.
Inputs may be any that keep to these rules, and one draw needn't show every extreme that they name: image_count[g] images are live in group g, in its first slots; the busiest group holds exactly 2; the counts sum to 10.
All inputs are finite; a program needn't handle non-finite values.
Results may differ from the reference program's by a relative error of at most 0.012.
The reference program's roundings to bfloat16 on the way count: a program that leaves them out, or rounds other values in their place, can miss the bound.
Values may be sent and summed in bfloat16 or wider, within the bound.
A program may use at most 320 MiB of HBM per device.

```python
import math
import jax
import jax.numpy as jnp
import numpy as np
from jax import lax

D = 1024
HEADS = 16
HEAD_DIM = 64
FF = 4096
SEQ = 1024
CAP = 2
SLOTS = 16
IMAGES = 10
N_REPLICA = 8


def shard_levels(own_key, extent, split, smallest, top_value):
    def one(position, shards_of):
        steps = jax.random.uniform(jax.random.fold_in(jax.random.fold_in(own_key, 6), position), (shards_of,), jnp.float32, smallest / len(split), top_value / len(split))
        return jnp.repeat(jnp.exp(steps), extent[position] // shards_of).reshape((-1,) + (1,) * (len(extent) - position - 1))

    loudness = one(*split[0])
    for cut in split[1:]:
        loudness = loudness * one(*cut)
    return loudness


def profile(number_of, total, reach, lean):
    portions = [(1 << 20) // math.isqrt(grade ** lean) + 1 for grade in range(2, number_of + 1)]
    surplus, holding = total - reach - (number_of - 1), [1] * (number_of - 1)
    while surplus > 0:
        movable = [i for i in range(number_of - 1) if holding[i] < reach]
        pool, left = sum([portions[i] for i in movable]), surplus
        for i in movable:
            more = min(reach - holding[i], max(1, left * portions[i] // pool), surplus)
            holding[i] = holding[i] + more
            surplus = surplus - more
    return np.array([reach] + holding)


def uneven(rng, amount, total, most, skew):
    if amount == 2:
        one = jax.random.randint(rng, (), max(1, total - most), min(most, total - 1) + 1)
        return jnp.stack([one, total - one])
    lengths = jnp.asarray(profile(amount, total, most, skew), jnp.int32)
    pairs = (amount - 1) // 2
    source_of, sink = lengths[1:1 + 2 * pairs:2], lengths[2:2 + 2 * pairs:2]
    slack = jnp.minimum(source_of - 1, most - sink)
    shifted = jax.random.randint(jax.random.fold_in(rng, 1), (pairs,), 0, 1 << 20) % (slack + 1)
    lengths = lengths.at[1:1 + 2 * pairs:2].set(source_of - shifted).at[2:2 + 2 * pairs:2].set(sink + shifted)
    return lengths[jax.random.permutation(jax.random.fold_in(rng, 2), amount)]


def centred(rng, dims, deviation, reach, shards=(), kind=jnp.bfloat16):
    level = shard_levels(rng, dims, shards, -0.22, 0.18) if shards else 1.0
    values = jax.random.normal(rng, dims, jnp.float32) * deviation * level
    return jnp.minimum(jnp.maximum(values, -reach), reach).astype(kind)


def setup_inputs(seed: int = 0) -> dict:
    key_list = jax.random.split(jax.random.key(seed), 18)
    tokens = centred(key_list[0], (SLOTS, SEQ, D), 1.0, 6.0, ((0, 8), (1, 4)))
    qkv_weight = centred(key_list[1], (D, 3 * D), (D // 2) ** -0.5, 0.25, ((0, 4),))
    qv_bias = centred(key_list[2], (2 * D,), 0.3, 3.0, ((0, 4),))
    proj_weight = centred(key_list[3], (D, D), (D // 8) ** -0.5, 0.5, ((0, 4),))
    proj_bias = centred(key_list[4], (D,), 0.3, 3.0, ((0, 4),))
    up_weight = centred(key_list[5], (D, FF), D ** -0.5, 0.1875, ((0, 4),))
    up_bias = centred(key_list[6], (FF,), 0.3, 3.0, ((0, 4),))
    down_weight = centred(key_list[7], (FF, D), FF ** -0.5, 0.09375, ((0, 4),))
    down_bias = centred(key_list[8], (D,), 0.3, 3.0, ((0, 4),))
    attn_gain = jnp.clip(1.0 + 0.1 * jax.random.normal(key_list[9], (D,), jnp.float32), 0.5, 1.5).astype(jnp.bfloat16)
    attn_shift = centred(key_list[10], (D,), 0.3, 3.0, ((0, 4),))
    mlp_gain = jnp.clip(1.0 + 0.1 * jax.random.normal(key_list[11], (D,), jnp.float32), 0.5, 1.5).astype(jnp.bfloat16)
    mlp_shift = centred(key_list[12], (D,), 0.3, 3.0, ((0, 4),))
    attn_scale = jnp.clip(1.0 + 0.15 * jax.random.normal(key_list[13], (D,), jnp.float32), 0.25, 1.75).astype(jnp.bfloat16)
    mlp_scale = jnp.clip(1.0 + 0.15 * jax.random.normal(key_list[14], (D,), jnp.float32), 0.25, 1.75).astype(jnp.bfloat16)
    cotangent = centred(key_list[15], (SLOTS, SEQ, D), 1.0, 6.0, ((0, 8), (1, 4)))
    image_count = uneven(key_list[16], N_REPLICA, IMAGES, CAP, 2).astype(jnp.int32)
    return dict(tokens=tokens, qkv_weight=qkv_weight, qv_bias=qv_bias, proj_weight=proj_weight, proj_bias=proj_bias, up_weight=up_weight, up_bias=up_bias, down_weight=down_weight, down_bias=down_bias, attn_gain=attn_gain, attn_shift=attn_shift, mlp_gain=mlp_gain, mlp_shift=mlp_shift, attn_scale=attn_scale, mlp_scale=mlp_scale, cotangent=cotangent, image_count=image_count)


EPS = 1e-06
HIGH = lax.Precision.HIGHEST

@jax.custom_vjp
def low(v):
    return lax.optimization_barrier(v.astype(jnp.bfloat16)).astype(jnp.float32)

@jax.custom_vjp
def low_back(v):
    return v

def low_keep(v):
    return (low(v), None)

def low_pass(kept, grad):
    return (grad,)

def back_keep(v):
    return (v, None)

def back_low(kept, grad):
    return (low(grad),)
low.defvjp(low_keep, low_pass)
low_back.defvjp(back_keep, back_low)

def matmul(left, right):
    return jnp.dot(left, right, precision=HIGH, preferred_element_type=jnp.float32)

def normalize(values, gain, shift):
    centre = values - lax.optimization_barrier(jnp.mean(values, axis=-1, keepdims=True))
    spread = lax.optimization_barrier(jnp.mean(centre * centre, axis=-1, keepdims=True))
    return centre * lax.rsqrt(spread + EPS) * gain + shift

def image_layer(inputs, params):
    qkv_weight, qv_bias, proj_weight, proj_bias, up_weight, up_bias, down_weight, down_bias, attn_gain, attn_shift, mlp_gain, mlp_shift, attn_scale, mlp_scale = params
    width = inputs.shape[1]
    normed_first = low(normalize(inputs, attn_gain, attn_shift))
    projected = matmul(normed_first, qkv_weight)
    queries = low_back(low(projected[:, :width] + qv_bias[:width]))
    keys = low_back(low(projected[:, width:2 * width]))
    values = low_back(low(projected[:, 2 * width:] + qv_bias[width:]))
    query_heads = queries.reshape(-1, HEADS, HEAD_DIM)
    key_heads = keys.reshape(-1, HEADS, HEAD_DIM)
    value_heads = values.reshape(-1, HEADS, HEAD_DIM)
    scores = low_back(jnp.einsum('qhd,khd->hqk', query_heads, key_heads, precision=HIGH) * HEAD_DIM ** (-0.5))
    probs = low(jax.nn.softmax(scores, axis=-1))
    attended = low_back(low(jnp.einsum('hqk,khd->qhd', probs, value_heads, precision=HIGH).reshape(-1, width)))
    branch = low_back(matmul(attended, proj_weight) + proj_bias)
    middle = inputs + attn_scale * branch
    normed_second = low(normalize(middle, mlp_gain, mlp_shift))
    hidden_pre = low_back(matmul(normed_second, up_weight) + up_bias)
    hidden_act = low(jax.nn.gelu(hidden_pre, approximate=False))
    feed = low_back(matmul(hidden_act, down_weight) + down_bias)
    return middle + mlp_scale * feed

def reference(tokens, qkv_weight, qv_bias, proj_weight, proj_bias, up_weight, up_bias, down_weight, down_bias, attn_gain, attn_shift, mlp_gain, mlp_shift, attn_scale, mlp_scale, cotangent, image_count):
    params = tuple((array.astype(jnp.float32) for array in (qkv_weight, qv_bias, proj_weight, proj_bias, up_weight, up_bias, down_weight, down_bias, attn_gain, attn_shift, mlp_gain, mlp_shift, attn_scale, mlp_scale)))
    inputs = tokens.astype(jnp.float32)
    upstream = cotangent.astype(jnp.float32)
    slot_index = jnp.arange(inputs.shape[0], dtype=jnp.int32)
    live = (slot_index % CAP < image_count[slot_index // CAP]).astype(jnp.float32)

    def forward(everything, weights):

        def one_image(carry, image):
            return (carry, image_layer(image, weights))
        _, results = lax.scan(jax.checkpoint(one_image), jnp.zeros((), jnp.float32), everything)
        return results * live[:, None, None]
    result, backward = jax.vjp(forward, inputs, params)
    grad_inputs, grads = backward(upstream)
    return (result.astype(jnp.bfloat16), grad_inputs, grads[0], grads[1], grads[2], grads[3], grads[4], grads[5], grads[6], grads[7], grads[8], grads[9], grads[10], grads[11], grads[12], grads[13])
```

```python
import functools

import jax
import jax.numpy as jnp
from jax import lax
from jax.experimental import pallas as pl
from jax.experimental.pallas import tpu as pltpu
from jax.sharding import PartitionSpec as P

HEAD_DIM = 64
EPS = 1e-06
BF = jnp.bfloat16
F32 = jnp.float32
MESH = pl.DeviceIdType.MESH
MIB = 1024 * 1024
SLOTS = 4


def matmul(left, right, dims=((1,), (0,))):
    return lax.dot_general(left, right, (dims, ((), ())), preferred_element_type=F32)


def column_sum(values):
    return jnp.sum(values.astype(F32), axis=0)


def attend_forward(q_ref, k_ref, v_ref, out_ref, lse_ref):
    lane = lax.broadcasted_iota(jnp.int32, (1, 128), 1)
    query, key, value = q_ref[...], k_ref[...], v_ref[...]
    value_t = value.T
    parts = []
    for head in range(2):
        mine = (lane < HEAD_DIM) if head == 0 else (lane >= HEAD_DIM)
        own = jnp.where(mine, query * BF(HEAD_DIM**-0.5), BF(0))
        scores = matmul(key, own, ((1,), (1,)))
        highest = jnp.max(scores, axis=0, keepdims=True)
        expos = jnp.exp(scores - highest)
        denom = jnp.sum(expos, axis=0, keepdims=True)
        probs = (expos * (1.0 / denom)).astype(BF)
        lse_ref[0, head : head + 1, :] = highest + jnp.log(denom)
        rows = slice(head * HEAD_DIM, (head + 1) * HEAD_DIM)
        parts.append(matmul(value_t[rows, :], probs))
    out_ref[...] = jnp.concatenate(parts, axis=0).T.astype(BF)


def attend_backward(q_ref, k_ref, v_ref, g_ref, lse_ref, gq_ref, gk_ref, gv_ref):
    lane = lax.broadcasted_iota(jnp.int32, (1, 128), 1)
    query, key, value, grad = q_ref[...], k_ref[...], v_ref[...], g_ref[...]
    key_t = key.T
    parts = []
    for head in range(2):
        mine = (lane < HEAD_DIM) if head == 0 else (lane >= HEAD_DIM)
        own = jnp.where(mine, query * BF(HEAD_DIM**-0.5), BF(0))
        own_grad = jnp.where(mine, grad, BF(0))
        scores = matmul(key, own, ((1,), (1,)))
        probs = jnp.exp(scores - lse_ref[0, head : head + 1, :])
        grad_probs = matmul(value, own_grad, ((1,), (1,)))
        centre = jnp.sum(grad_probs * probs, axis=0, keepdims=True)
        grad_scores = (probs * (grad_probs - centre)).astype(BF)
        gv = matmul(probs.astype(BF), own_grad)
        gk = matmul(grad_scores, own)
        if head == 0:
            gv_ref[...], gk_ref[...] = gv, gk
        else:
            gv_ref[...] += gv
            gk_ref[...] += gk
        rows = slice(head * HEAD_DIM, (head + 1) * HEAD_DIM)
        parts.append(matmul(key_t[rows, :], grad_scores))
    whole = jnp.concatenate(parts, axis=0) * (HEAD_DIM**-0.5)
    gq_ref[...] = whole.T.astype(BF)


def attention_forward(query, key, value):
    rows, width = query.shape
    keys = key.shape[0]
    pairs = width // 128
    part = lambda n: pl.BlockSpec((n, 128), lambda i: (0, i))
    return pl.pallas_call(
        attend_forward,
        grid=(pairs,),
        in_specs=[part(rows), part(keys), part(keys)],
        out_specs=[part(rows), pl.BlockSpec((1, 2, rows), lambda i: (i, 0, 0))],
        out_shape=[
            jax.ShapeDtypeStruct((rows, width), BF),
            jax.ShapeDtypeStruct((pairs, 2, rows), F32),
        ],
        compiler_params=pltpu.CompilerParams(vmem_limit_bytes=48 * MIB),
    )(query, key, value)


def attention_backward(query, key, value, grad, lse):
    rows, width = query.shape
    keys = key.shape[0]
    pairs = width // 128
    part = lambda n: pl.BlockSpec((n, 128), lambda i: (0, i))
    return pl.pallas_call(
        attend_backward,
        grid=(pairs,),
        in_specs=[
            part(rows),
            part(keys),
            part(keys),
            part(rows),
            pl.BlockSpec((1, 2, rows), lambda i: (i, 0, 0)),
        ],
        out_specs=[part(rows), part(keys), part(keys)],
        out_shape=[
            jax.ShapeDtypeStruct((rows, width), BF),
            jax.ShapeDtypeStruct((keys, width), F32),
            jax.ShapeDtypeStruct((keys, width), F32),
        ],
        compiler_params=pltpu.CompilerParams(vmem_limit_bytes=48 * MIB),
    )(query, key, value, grad, lse)


class Place:
    def __init__(self, replicas, shards):
        self.Z, self.Y = replicas // 2, shards // 2
        self.shards = shards
        replica, shard = lax.axis_index("replica"), lax.axis_index("shard")
        self.x, self.z = lax.rem(replica, 2), lax.div(replica, 2)
        self.c, self.y = lax.rem(shard, 2), lax.div(shard, 2)
        self.s = shard

    def part(self, y, c):
        return y * 2 + c

    def at(self, x=None, z=None, y=None, c=None):
        x = self.x if x is None else x
        z = self.z if z is None else z
        y = self.y if y is None else y
        c = self.c if c is None else c
        return (z * 2 + x, y * 2 + c)

    def ahead_z(self, k):
        return lax.rem(self.z + k, self.Z)

    def behind_z(self, k):
        return lax.rem(self.z + self.Z - k, self.Z)

    def ahead_y(self, k):
        return lax.rem(self.y + k, self.Y)

    def behind_y(self, k):
        return lax.rem(self.y + self.Y - k, self.Y)

    def greet(self, extra=()):
        others = [self.at(c=1 - self.c), self.at(x=1 - self.x)]
        others += [self.at(y=self.ahead_y(k)) for k in range(1, self.Y)]
        others += [self.at(z=self.ahead_z(k)) for k in range(1, self.Z)]
        others += list(extra)
        barrier = pltpu.get_barrier_semaphore()
        for other in others:
            pl.semaphore_signal(barrier, inc=1, device_id=other, device_id_type=MESH)
        pl.semaphore_wait(barrier, len(others))


def send(src, dst, send_sem, recv_sem, device):
    return pltpu.make_async_remote_copy(
        src_ref=src,
        dst_ref=dst,
        send_sem=send_sem,
        recv_sem=recv_sem,
        device_id=device,
        device_id_type=MESH,
    )


def gather_kernel(replicas, shards, count, *refs):
    ins, outs = refs[: count + 1], refs[count + 1 : 2 * count + 2]
    (local, small_s, small_r, ys, yr, zs, zr, xs, xr, cs, cr, os, orr) = refs[2 * count + 2 :]
    place = Place(replicas, shards)
    Y, Z = place.Y, place.Z
    s = place.s
    diagonal = [
        place.at(y=place.ahead_y(k), c=1 - place.c) for k in range(1, Y)
    ]
    place.greet(diagonal)

    keep = [pltpu.make_async_copy(ins[w], outs[w].at[s], local.at[w]) for w in range(count + 1)]
    for copy in keep:
        copy.start()
    small = []
    for k in range(1, shards):
        peer = lax.rem(s + k, shards)
        small.append(
            send(ins[count], outs[count].at[s], small_s.at[k - 1], small_r.at[k - 1],
                 (lax.axis_index("replica"), peer))
        )
        small[-1].start()

    def piece(w, z):
        rows, cols = ins[w].shape
        half, step = rows // 2, cols // Z
        return (pl.ds(pl.multiple_of(place.x * half, half), half),
                pl.ds(pl.multiple_of(z * step, 128), step))

    def y_copy(w, k):
        rows, cols = piece(w, place.z)
        return send(ins[w].at[rows, cols], outs[w].at[s, rows, cols], ys.at[w, k - 1], yr.at[w, k - 1],
                    place.at(y=place.ahead_y(k)))

    def z_copy(w, k, j):
        owner = place.part(place.behind_y(k), place.c)
        rows, cols = piece(w, place.z)
        block = outs[w].at[owner, rows, cols]
        return send(block, block, zs.at[w, k - 1, j - 1], zr.at[w, k - 1, j - 1],
                    place.at(z=place.ahead_z(j)))

    def x_copy(w, k):
        owner = place.part(place.behind_y(k), place.c)
        half = ins[w].shape[0] // 2
        block = outs[w].at[owner, pl.ds(pl.multiple_of(place.x * half, half), half)]
        return send(block, block, xs.at[w, k - 1], xr.at[w, k - 1], place.at(x=1 - place.x))

    def c_copy(w, k):
        owner = place.part(place.behind_y(k), place.c)
        block = outs[w].at[owner]
        return send(block, block, cs.at[w, k - 1], cr.at[w, k - 1], place.at(c=1 - place.c))

    def own_copy(w):
        return send(ins[w], outs[w].at[s], os.at[w], orr.at[w], place.at(c=1 - place.c))

    for w in range(count):
        for k in range(1, Y):
            y_copy(w, k).start()
    for w in range(count):
        own_copy(w).start()
    for t in range(count + 3):
        if t < count:
            for k in range(1, Y):
                y_copy(t, k).wait()
                for j in range(1, Z):
                    z_copy(t, k, j).start()
        if 0 <= t - 1 < count:
            for k in range(1, Y):
                for j in range(1, Z):
                    z_copy(t - 1, k, j).wait()
                x_copy(t - 1, k).start()
        if 0 <= t - 2 < count:
            for k in range(1, Y):
                x_copy(t - 2, k).wait()
                c_copy(t - 2, k).start()
        if 0 <= t - 3 < count:
            for k in range(1, Y):
                c_copy(t - 3, k).wait()
            own_copy(t - 3).wait()
    for copy in small + keep:
        copy.wait()


def gather_weights(replicas, shards, weights, small):
    count = len(weights)
    Y, Z = shards // 2, replicas // 2
    dma = pltpu.SemaphoreType.DMA
    arrays = list(weights) + [small]
    any_spec = pl.BlockSpec(memory_space=pl.ANY)
    return pl.pallas_call(
        functools.partial(gather_kernel, replicas, shards, count),
        in_specs=[any_spec] * (count + 1),
        out_specs=[any_spec] * (count + 1),
        out_shape=[jax.ShapeDtypeStruct((shards,) + a.shape, a.dtype) for a in arrays],
        scratch_shapes=[
            dma((count + 1,)),
            dma((shards - 1,)), dma((shards - 1,)),
            dma((count, Y - 1)), dma((count, Y - 1)),
            dma((count, Y - 1, Z - 1)), dma((count, Y - 1, Z - 1)),
            dma((count, Y - 1)), dma((count, Y - 1)),
            dma((count, Y - 1)), dma((count, Y - 1)),
            dma((count,)), dma((count,)),
        ],
        compiler_params=pltpu.CompilerParams(collective_id=0, has_side_effects=True),
    )(*arrays)


def reduce_kernel(replicas, shards, plan, *refs):
    n_ops = 2 * len(plan)
    ops, small_ref = refs[:n_ops], refs[n_ops]
    out, small_out = refs[n_ops + 1 : n_ops + 3]
    (part, crecv, ysum, yrecv, xsum, xrecv, zsum, zrecv, small_buf, tile,
     cs, cr, ys, yr, xs, xr, zs, zr, gs, gr, hs, hr, ss, sr) = refs[n_ops + 3 :]
    place = Place(replicas, shards)
    Y, Z = place.Y, place.Z
    CB = part.shape[3]
    W = part.shape[4]
    total = sum(item[2] for item in plan)
    place.greet()

    def core_copy(i):
        a = lax.rem(i, SLOTS)
        return send(part.at[lax.rem(i, 2), 1 - place.c], crecv.at[a], cs.at[a], cr.at[a],
                    place.at(c=1 - place.c))

    def y_copy(i, k):
        a = lax.rem(i, SLOTS)
        return send(ysum.at[a, place.ahead_y(k)], yrecv.at[a, k - 1], ys.at[a, k - 1], yr.at[a, k - 1],
                    place.at(y=place.ahead_y(k)))

    def x_copy(i):
        a = lax.rem(i, SLOTS)
        return send(xsum.at[a, 1 - place.x], xrecv.at[a], xs.at[a], xr.at[a], place.at(x=1 - place.x))

    def z_copy(i, k):
        a = lax.rem(i, SLOTS)
        return send(zsum.at[a, place.ahead_z(k)], zrecv.at[a, k - 1], zs.at[a, k - 1], zr.at[a, k - 1],
                    place.at(z=place.ahead_z(k)))

    def zg_copy(i, k):
        a = lax.rem(i, SLOTS)
        block = out.at[i, place.x, place.z]
        return send(block, block, gs.at[a, k - 1], gr.at[a, k - 1], place.at(z=place.ahead_z(k)))

    def xg_copy(i):
        a = lax.rem(i, SLOTS)
        block = out.at[i, place.x]
        return send(block, block, hs.at[a], hr.at[a], place.at(x=1 - place.x))

    def add(*terms):
        whole = terms[0].astype(F32)
        for term in terms[1:]:
            whole = whole + term.astype(F32)
        return whole.astype(BF)

    def product(left, first, cols):
        if CB % 128 == 0:
            return matmul(left[:, pl.ds(first, CB)], cols, ((0,), (0,))).astype(BF)
        start = pl.multiple_of(lax.div(first, 128) * 128, 128)
        tile[...] = matmul(left[:, pl.ds(start, 128)], cols, ((0,), (0,)))
        return tile[pl.ds(pl.multiple_of(first - start, CB), CB)].astype(BF)

    def tick(i):
        def stage(lag):
            j = i - lag
            return j, (j >= 0) & (j < total)

        j1, ok1 = stage(1)

        @pl.when(ok1)
        def _():
            core_copy(j1).wait()
            a = lax.rem(j1, SLOTS)
            for y in range(Y):
                ysum[a, y] = add(part[lax.rem(j1, 2), place.c, y], crecv[a, y])
            for k in range(1, Y):
                y_copy(j1, k).start()

        j2, ok2 = stage(2)

        @pl.when(ok2)
        def _():
            a = lax.rem(j2, SLOTS)
            for k in range(1, Y):
                y_copy(j2, k).wait()
            for h in range(2):
                rows = slice(h * CB // 2, (h + 1) * CB // 2)
                xsum[a, h] = add(ysum[a, place.y, rows], *[yrecv[a, k - 1, rows] for k in range(1, Y)])
            x_copy(j2).start()

        j3, ok3 = stage(3)

        @pl.when(ok3)
        def _():
            a = lax.rem(j3, SLOTS)
            x_copy(j3).wait()
            for z in range(Z):
                cols = slice(z * W // Z, (z + 1) * W // Z)
                zsum[a, z] = add(xsum[a, place.x, :, cols], xrecv[a, :, cols])
            for k in range(1, Z):
                z_copy(j3, k).start()

        j4, ok4 = stage(4)

        @pl.when(ok4)
        def _():
            a = lax.rem(j4, SLOTS)
            for k in range(1, Z):
                z_copy(j4, k).wait()
            out[j4, place.x, place.z] = add(zsum[a, place.z], *[zrecv[a, k - 1] for k in range(1, Z)])
            for k in range(1, Z):
                zg_copy(j4, k).start()

        j5, ok5 = stage(5)

        @pl.when(ok5)
        def _():
            for k in range(1, Z):
                zg_copy(j5, k).wait()
            xg_copy(j5).start()

        j6, ok6 = stage(6)

        @pl.when(ok6)
        def _():
            xg_copy(j6).wait()

    def small_send(step, devices):
        copies = []
        for k, device in enumerate(devices):
            copies.append(send(small_buf.at[step, 0], small_buf.at[step, k + 1],
                               ss.at[step, k], sr.at[step, k], device))
        return copies

    small_steps = [
        [place.at(c=1 - place.c)],
        [place.at(y=place.ahead_y(k)) for k in range(1, Y)],
        [place.at(x=1 - place.x)],
        [place.at(z=place.ahead_z(k)) for k in range(1, Z)],
    ]
    small_buf[0, 0] = small_ref[...]
    for copy in small_send(0, small_steps[0]):
        copy.start()

    base = 0
    for number, (rows, n_cols, chunks) in enumerate(plan):
        left, right = ops[2 * number], ops[2 * number + 1]
        blocks = rows // CB

        def body(i, _, base=base, rows=rows, left=left, right=right, blocks=blocks):
            local = i - base
            b, n = lax.rem(local, blocks), lax.div(local, blocks)
            slot = lax.rem(i, 2)
            cols = right[:, pl.ds(pl.multiple_of(n * W, 128), W)]
            for turn in range(2):
                c = 1 - place.c if turn == 0 else place.c
                for y in range(Y):
                    first = pl.multiple_of(place.part(y, c) * rows + b * CB, CB)
                    part[slot, c, y] = product(left, first, cols)
                if turn == 0:
                    core_copy(i).start()
            tick(i)
            return 0

        lax.fori_loop(base, base + chunks, body, 0)
        base += chunks
        for copy in small_send(number, small_steps[number]):
            copy.wait()
        whole = small_buf[number, 0]
        for k in range(len(small_steps[number])):
            whole = whole + small_buf[number, k + 1]
        if number < 3:
            small_buf[number + 1, 0] = whole
            for copy in small_send(number + 1, small_steps[number + 1]):
                copy.start()
        else:
            small_out[...] = whole

    def drain(i, _):
        tick(i)
        return 0

    lax.fori_loop(total, total + 6, drain, 0)


def reduce_gradients(replicas, shards, pairs, small):
    Y, Z = shards // 2, replicas // 2
    dma = pltpu.SemaphoreType.DMA
    W = 1024
    CB = min(128, 1024 // shards)
    plan, flat = [], []
    for left, right in pairs:
        rows, n_cols = left.shape[1] // shards, right.shape[1] // W
        plan.append((rows, n_cols, (rows // CB) * n_cols))
        flat += [left, right]
    total = sum(item[2] for item in plan)
    vmem = pl.BlockSpec(memory_space=pltpu.VMEM)
    peers = max(Y, Z, 2)
    out, small_out = pl.pallas_call(
        functools.partial(reduce_kernel, replicas, shards, tuple(plan)),
        in_specs=[vmem] * (len(flat) + 1),
        out_specs=[vmem, vmem],
        out_shape=[
            jax.ShapeDtypeStruct((total, 2, Z, CB // 2, W // Z), BF),
            jax.ShapeDtypeStruct(small.shape, F32),
        ],
        scratch_shapes=[
            pltpu.VMEM((2, 2, Y, CB, W), BF),
            pltpu.VMEM((SLOTS, Y, CB, W), BF),
            pltpu.VMEM((SLOTS, Y, CB, W), BF),
            pltpu.VMEM((SLOTS, Y - 1, CB, W), BF),
            pltpu.VMEM((SLOTS, 2, CB // 2, W), BF),
            pltpu.VMEM((SLOTS, CB // 2, W), BF),
            pltpu.VMEM((SLOTS, Z, CB // 2, W // Z), BF),
            pltpu.VMEM((SLOTS, Z - 1, CB // 2, W // Z), BF),
            pltpu.VMEM((4, peers) + small.shape, F32),
            pltpu.VMEM((128, W), F32),
            dma((SLOTS,)), dma((SLOTS,)),
            dma((SLOTS, Y - 1)), dma((SLOTS, Y - 1)),
            dma((SLOTS,)), dma((SLOTS,)),
            dma((SLOTS, Z - 1)), dma((SLOTS, Z - 1)),
            dma((SLOTS, Z - 1)), dma((SLOTS, Z - 1)),
            dma((SLOTS,)), dma((SLOTS,)),
            dma((4, peers - 1)), dma((4, peers - 1)),
        ],
        compiler_params=pltpu.CompilerParams(
            collective_id=1, has_side_effects=True, vmem_limit_bytes=60 * MIB
        ),
    )(*flat, small)
    grads, base = [], 0
    for rows, n_cols, chunks in plan:
        block = out[base : base + chunks].reshape(n_cols, rows // CB, 2, Z, CB // 2, W // Z)
        block = block.transpose(1, 2, 4, 0, 3, 5).reshape(rows, n_cols * W)
        grads.append(block.astype(F32))
        base += chunks
    return grads, small_out


def norm_parts(values):
    centre = values - jnp.mean(values, axis=-1, keepdims=True)
    scale = lax.rsqrt(jnp.mean(centre * centre, axis=-1, keepdims=True) + EPS)
    return centre * scale, scale


def norm_back(grad, unit, scale, gain):
    inner = grad * gain
    return scale * (
        inner
        - jnp.mean(inner, axis=-1, keepdims=True)
        - unit * jnp.mean(inner * unit, axis=-1, keepdims=True)
    )


def on_device(replicas, shards, tokens, qkv_weight, qv_bias, proj_weight, proj_bias, up_weight, up_bias,
              down_weight, down_bias, attn_gain, attn_shift, mlp_gain, mlp_shift, attn_scale, mlp_scale,
              cotangent, image_count):
    vectors = (qv_bias, proj_bias, up_bias, down_bias, attn_gain, attn_shift, mlp_gain, mlp_shift,
               attn_scale, mlp_scale)
    lengths = [v.shape[0] for v in vectors]
    n_small = sum(lengths)
    padded = -(-n_small // 2048) * 2048
    packed = jnp.pad(jnp.concatenate(vectors), (0, padded - n_small)).reshape(16, padded // 16)
    qkv_all, proj_all, up_all, down_all, small_all = gather_weights(
        replicas, shards, (qkv_weight, proj_weight, up_weight, down_weight), packed
    )
    width = tokens.shape[2]
    qkv_full, proj_full = qkv_all.reshape(width, -1), proj_all.reshape(width, -1)
    up_full, down_full = up_all.reshape(width, -1), down_all.reshape(-1, width)
    small_flat = small_all.reshape(shards, padded)
    full, place = [], 0
    for n in lengths:
        full.append(small_flat[:, place : place + n].reshape(-1).astype(F32))
        place += n
    (qv_shift, proj_shift, up_shift, down_shift, gain_first, shift_first, gain_second, shift_second,
     scale_first, scale_second) = full

    half = shards // 2
    shard = lax.axis_index("shard")
    mine = lax.div(shard, half)
    swap = [(i, (i + half) % shards) for i in range(shards)]

    def join(array):
        keep = lax.dynamic_index_in_dim(array, mine, 0, keepdims=False)
        give = lax.dynamic_index_in_dim(array, 1 - mine, 0, keepdims=False)
        return jnp.concatenate([keep, lax.ppermute(give, "shard", swap)], axis=0)

    def split(array):
        rows = array.shape[0] // 2
        got = lax.ppermute(array[rows:], "shard", swap)
        first = jnp.where(mine == 0, array[:rows], got)
        second = jnp.where(mine == 0, got, array[:rows])
        return jnp.stack([first, second])

    inputs = join(tokens).astype(F32)
    upstream = join(cotangent).astype(F32)
    live = (mine < image_count[lax.axis_index("replica")]).astype(F32)
    rows = inputs.shape[0]

    groups = [list(range(half)), list(range(half, shards))]
    other = [(i, i ^ 1) for i in range(shards)]

    def all_rows(array):
        if half == 2:
            return jnp.concatenate([array, lax.ppermute(array, "shard", other)], axis=0)
        return lax.all_gather(array, "shard", axis=0, tiled=True, axis_index_groups=groups)

    def sum_rows(array):
        if half == 2:
            got = lax.ppermute(array[rows:].astype(BF), "shard", other)
            return array[:rows] + got.astype(F32)
        return lax.psum_scatter(array, "shard", scatter_dimension=0, tiled=True, axis_index_groups=groups)

    unit_first, rstd_first = norm_parts(inputs)
    normed_low = (unit_first * gain_first + shift_first).astype(BF)
    projected = matmul(normed_low, qkv_full)
    queries = (projected[:, :width] + qv_shift[:width]).astype(BF)
    keys = projected[:, width : 2 * width].astype(BF)
    values = (projected[:, 2 * width :] + qv_shift[width:]).astype(BF)
    keys_all, values_all = all_rows(keys), all_rows(values)
    attended, lse = attention_forward(queries, keys_all, values_all)
    branch = matmul(attended, proj_full) + proj_shift
    middle = inputs + scale_first * branch
    unit_second, rstd_second = norm_parts(middle)
    second_low = (unit_second * gain_second + shift_second).astype(BF)
    hidden = matmul(second_low, up_full) + up_shift
    gate = 0.5 * (1.0 + lax.erf(hidden * (0.5**0.5)))
    act = (hidden * gate).astype(BF)
    slope = gate + hidden * (jnp.exp(-0.5 * hidden * hidden) * 0.3989422804014327)
    feed = matmul(act, down_full) + down_shift
    result = middle + scale_second * feed
    output = split((result * live).astype(BF))

    grad_result = upstream * live
    grad_scale_second = jnp.sum(grad_result * feed, axis=0)
    grad_feed = (grad_result * scale_second).astype(BF)
    grad_down_shift = column_sum(grad_feed)
    grad_act = matmul(grad_feed, down_full, ((1,), (1,)))
    grad_pre = (grad_act * slope).astype(BF)
    grad_up_shift = column_sum(grad_pre)
    grad_second = matmul(grad_pre, up_full, ((1,), (1,)))
    grad_gain_second = jnp.sum(grad_second * unit_second, axis=0)
    grad_shift_second = jnp.sum(grad_second, axis=0)
    grad_middle = grad_result + norm_back(grad_second, unit_second, rstd_second, gain_second)
    grad_scale_first = jnp.sum(grad_middle * branch, axis=0)
    grad_branch = (grad_middle * scale_first).astype(BF)
    grad_proj_shift = column_sum(grad_branch)
    grad_attended = matmul(grad_branch, proj_full, ((1,), (1,))).astype(BF)
    grad_queries, keys_part, values_part = attention_backward(
        queries, keys_all, values_all, grad_attended, lse
    )
    grad_keys, grad_values = sum_rows(keys_part).astype(BF), sum_rows(values_part).astype(BF)
    grad_qkv = jnp.concatenate([grad_queries, grad_keys, grad_values], axis=1)
    grad_qv_shift = jnp.concatenate([column_sum(grad_queries), column_sum(grad_values)])
    grad_first = matmul(grad_qkv, qkv_full, ((1,), (1,)))
    grad_gain_first = jnp.sum(grad_first * unit_first, axis=0)
    grad_shift_first = jnp.sum(grad_first, axis=0)
    grad_inputs = grad_middle + norm_back(grad_first, unit_first, rstd_first, gain_first)
    grad_tokens = split(grad_inputs)

    sums = (grad_qv_shift, grad_proj_shift, grad_up_shift, grad_down_shift, grad_gain_first,
            grad_shift_first, grad_gain_second, grad_shift_second, grad_scale_first, grad_scale_second)
    small = jnp.concatenate([v.reshape(shards, -1) for v in sums], axis=1)
    small = jnp.pad(small, ((0, 0), (0, padded - n_small))).reshape(shards * padded // 1024, 1024)
    pairs = ((act, grad_feed), (second_low, grad_pre), (attended, grad_branch), (normed_low, grad_qkv))
    (grad_down, grad_up, grad_proj, grad_qkv_weight), small = reduce_gradients(
        replicas, shards, pairs, small
    )
    own = lax.dynamic_index_in_dim(small.reshape(shards, padded), shard, 0, keepdims=False)
    done, start = [], 0
    for n in lengths:
        done.append(own[start : start + n])
        start += n
    (g_qv, g_pb, g_ub, g_db, g_ag, g_as, g_mg, g_ms, g_sa, g_sm) = done
    return (output, grad_tokens, grad_qkv_weight, g_qv, grad_proj, g_pb, grad_up, g_ub, grad_down, g_db,
            g_ag, g_as, g_mg, g_ms, g_sa, g_sm)


def solution(mesh):
    rows, vector = P("shard", None), P("shard")
    image = P("replica", "shard", None)
    in_specs = (image, rows, vector, rows, vector, rows, vector, rows, vector, vector, vector, vector,
                vector, vector, vector, image, P())
    out_specs = (image, image, rows, vector, rows, vector, rows, vector, rows, vector, vector, vector,
                 vector, vector, vector, vector)
    return jax.shard_map(
        functools.partial(on_device, mesh.shape["replica"], mesh.shape["shard"]),
        mesh=mesh, in_specs=in_specs, out_specs=out_specs, check_vma=False,
    )
```

```python
import functools

import jax
import jax.numpy as jnp
from jax import lax
from jax.experimental import pallas as pl
from jax.experimental.pallas import tpu as pltpu
from jax.sharding import PartitionSpec as P

HEAD_DIM = 64
EPS = 1e-06
BF = jnp.bfloat16
F32 = jnp.float32
MESH = pl.DeviceIdType.MESH
MIB = 1024 * 1024
SLOTS = 4


def matmul(left, right, dims=((1,), (0,))):
    return lax.dot_general(left, right, (dims, ((), ())), preferred_element_type=F32)


def column_sum(values):
    return jnp.sum(values.astype(F32), axis=0)


def attend_forward(q_ref, k_ref, v_ref, out_ref, lse_ref):
    lane = lax.broadcasted_iota(jnp.int32, (1, 128), 1)
    query, key, value = q_ref[...], k_ref[...], v_ref[...]
    value_t = value.T
    parts = []
    for head in range(2):
        mine = (lane < HEAD_DIM) if head == 0 else (lane >= HEAD_DIM)
        own = jnp.where(mine, query * BF(HEAD_DIM**-0.5), BF(0))
        scores = matmul(key, own, ((1,), (1,)))
        highest = jnp.max(scores, axis=0, keepdims=True)
        expos = jnp.exp(scores - highest)
        denom = jnp.sum(expos, axis=0, keepdims=True)
        probs = (expos * (1.0 / denom)).astype(BF)
        lse_ref[0, head : head + 1, :] = highest + jnp.log(denom)
        rows = slice(head * HEAD_DIM, (head + 1) * HEAD_DIM)
        parts.append(matmul(value_t[rows, :], probs))
    out_ref[...] = jnp.concatenate(parts, axis=0).T.astype(BF)


def attention_forward(query, key, value):
    rows, width = query.shape
    keys = key.shape[0]
    pairs = width // 128
    part = lambda n: pl.BlockSpec((n, 128), lambda i: (0, i))
    return pl.pallas_call(
        attend_forward,
        grid=(pairs,),
        in_specs=[part(rows), part(keys), part(keys)],
        out_specs=[part(rows), pl.BlockSpec((1, 2, rows), lambda i: (i, 0, 0))],
        out_shape=[
            jax.ShapeDtypeStruct((rows, width), BF),
            jax.ShapeDtypeStruct((pairs, 2, rows), F32),
        ],
        compiler_params=pltpu.CompilerParams(vmem_limit_bytes=48 * MIB),
    )(query, key, value)


class Place:
    def __init__(self, replicas, shards):
        self.Z, self.Y = replicas // 2, shards // 2
        self.shards = shards
        replica, shard = lax.axis_index("replica"), lax.axis_index("shard")
        self.x, self.z = lax.rem(replica, 2), lax.div(replica, 2)
        self.c, self.y = lax.rem(shard, 2), lax.div(shard, 2)
        self.s = shard

    def part(self, y, c):
        return y * 2 + c

    def at(self, x=None, z=None, y=None, c=None):
        x = self.x if x is None else x
        z = self.z if z is None else z
        y = self.y if y is None else y
        c = self.c if c is None else c
        return (z * 2 + x, y * 2 + c)

    def ahead_z(self, k):
        return lax.rem(self.z + k, self.Z)

    def behind_z(self, k):
        return lax.rem(self.z + self.Z - k, self.Z)

    def ahead_y(self, k):
        return lax.rem(self.y + k, self.Y)

    def behind_y(self, k):
        return lax.rem(self.y + self.Y - k, self.Y)

    def greet(self, extra=()):
        others = [self.at(c=1 - self.c), self.at(x=1 - self.x)]
        others += [self.at(y=self.ahead_y(k)) for k in range(1, self.Y)]
        others += [self.at(z=self.ahead_z(k)) for k in range(1, self.Z)]
        others += list(extra)
        barrier = pltpu.get_barrier_semaphore()
        for other in others:
            pl.semaphore_signal(barrier, inc=1, device_id=other, device_id_type=MESH)
        pl.semaphore_wait(barrier, len(others))


def send(src, dst, send_sem, recv_sem, device):
    return pltpu.make_async_remote_copy(
        src_ref=src,
        dst_ref=dst,
        send_sem=send_sem,
        recv_sem=recv_sem,
        device_id=device,
        device_id_type=MESH,
    )


def gather_kernel(replicas, shards, count, *refs):
    ins, outs = refs[: count + 1], refs[count + 1 : 2 * count + 2]
    (local, small_s, small_r, ys, yr, zs, zr, xs, xr, cs, cr, os, orr) = refs[2 * count + 2 :]
    place = Place(replicas, shards)
    Y, Z = place.Y, place.Z
    s = place.s
    diagonal = [
        place.at(y=place.ahead_y(k), c=1 - place.c) for k in range(1, Y)
    ]
    place.greet(diagonal)

    keep = [pltpu.make_async_copy(ins[w], outs[w].at[s], local.at[w]) for w in range(count + 1)]
    for copy in keep:
        copy.start()
    small = []
    for k in range(1, shards):
        peer = lax.rem(s + k, shards)
        small.append(
            send(ins[count], outs[count].at[s], small_s.at[k - 1], small_r.at[k - 1],
                 (lax.axis_index("replica"), peer))
        )
        small[-1].start()

    def piece(w, z):
        rows, cols = ins[w].shape
        half, step = rows // 2, cols // Z
        return (pl.ds(pl.multiple_of(place.x * half, half), half),
                pl.ds(pl.multiple_of(z * step, 128), step))

    def y_copy(w, k):
        rows, cols = piece(w, place.z)
        return send(ins[w].at[rows, cols], outs[w].at[s, rows, cols], ys.at[w, k - 1], yr.at[w, k - 1],
                    place.at(y=place.ahead_y(k)))

    def z_copy(w, k, j):
        owner = place.part(place.behind_y(k), place.c)
        rows, cols = piece(w, place.z)
        block = outs[w].at[owner, rows, cols]
        return send(block, block, zs.at[w, k - 1, j - 1], zr.at[w, k - 1, j - 1],
                    place.at(z=place.ahead_z(j)))

    def x_copy(w, k):
        owner = place.part(place.behind_y(k), place.c)
        half = ins[w].shape[0] // 2
        block = outs[w].at[owner, pl.ds(pl.multiple_of(place.x * half, half), half)]
        return send(block, block, xs.at[w, k - 1], xr.at[w, k - 1], place.at(x=1 - place.x))

    def c_copy(w, k):
        owner = place.part(place.behind_y(k), place.c)
        block = outs[w].at[owner]
        return send(block, block, cs.at[w, k - 1], cr.at[w, k - 1], place.at(c=1 - place.c))

    def own_copy(w):
        return send(ins[w], outs[w].at[s], os.at[w], orr.at[w], place.at(c=1 - place.c))

    for w in range(count):
        for k in range(1, Y):
            y_copy(w, k).start()
    for w in range(count):
        own_copy(w).start()
    for t in range(count + 3):
        if t < count:
            for k in range(1, Y):
                y_copy(t, k).wait()
                for j in range(1, Z):
                    z_copy(t, k, j).start()
        if 0 <= t - 1 < count:
            for k in range(1, Y):
                for j in range(1, Z):
                    z_copy(t - 1, k, j).wait()
                x_copy(t - 1, k).start()
        if 0 <= t - 2 < count:
            for k in range(1, Y):
                x_copy(t - 2, k).wait()
                c_copy(t - 2, k).start()
        if 0 <= t - 3 < count:
            for k in range(1, Y):
                c_copy(t - 3, k).wait()
            own_copy(t - 3).wait()
    for copy in small + keep:
        copy.wait()


def gather_weights(replicas, shards, weights, small):
    count = len(weights)
    Y, Z = shards // 2, replicas // 2
    dma = pltpu.SemaphoreType.DMA
    arrays = list(weights) + [small]
    any_spec = pl.BlockSpec(memory_space=pl.ANY)
    return pl.pallas_call(
        functools.partial(gather_kernel, replicas, shards, count),
        in_specs=[any_spec] * (count + 1),
        out_specs=[any_spec] * (count + 1),
        out_shape=[jax.ShapeDtypeStruct((shards,) + a.shape, a.dtype) for a in arrays],
        scratch_shapes=[
            dma((count + 1,)),
            dma((shards - 1,)), dma((shards - 1,)),
            dma((count, Y - 1)), dma((count, Y - 1)),
            dma((count, Y - 1, Z - 1)), dma((count, Y - 1, Z - 1)),
            dma((count, Y - 1)), dma((count, Y - 1)),
            dma((count, Y - 1)), dma((count, Y - 1)),
            dma((count,)), dma((count,)),
        ],
        compiler_params=pltpu.CompilerParams(collective_id=0, has_side_effects=True),
    )(*arrays)


def norm_parts(values):
    centre = values - jnp.mean(values, axis=-1, keepdims=True)
    scale = lax.rsqrt(jnp.mean(centre * centre, axis=-1, keepdims=True) + EPS)
    return centre * scale, scale


def norm_back(grad, unit, scale, gain):
    inner = grad * gain
    return scale * (
        inner
        - jnp.mean(inner, axis=-1, keepdims=True)
        - unit * jnp.mean(inner * unit, axis=-1, keepdims=True)
    )


QV, PROJ_B, UP_B, DOWN_B, ATTN_GAIN, ATTN_SHIFT, MLP_GAIN, MLP_SHIFT, ATTN_SCALE, MLP_SCALE = (
    0, 2, 3, 7, 8, 9, 10, 11, 12, 13)
V_MLP_SCALE, V_MLP_GAIN, V_ATTN_SCALE, V_ATTN_GAIN, V_DOWN_B, V_LIVE = range(6)

HBM_INPUTS = ("act", "slope", "cot", "x", "branch", "second", "attended", "query", "key", "value",
              "first", "down", "up", "proj", "qkv")


def backward_kernel(replicas, shards, names, *refs):
    ref = dict(zip(names, refs))
    place = Place(replicas, shards)
    Y, Z = place.Y, place.Z
    half = shards // 2
    part, crecv, ysum, yrecv = ref["part"], ref["crecv"], ref["ysum"], ref["yrecv"]
    xsum, xrecv, zsum, zrecv = ref["xsum"], ref["xrecv"], ref["zsum"], ref["zrecv"]
    out, small, vec, lse = ref["out"], ref["small_buf"], ref["vec"], ref["lse"]
    CB, W = part.shape[3], part.shape[4]
    rows = ref["gfeed"].shape[0]
    R = rows // 2
    keys = half * rows
    FF = ref["slope_s"].shape[1]
    down_rows, other_rows = FF // shards, W // shards
    blocks_d, blocks = down_rows // CB, other_rows // CB
    n_down, n_up, n_proj, n_qkv = blocks_d, blocks * (FF // W), blocks, blocks * 3
    total = n_down + n_up + n_proj + n_qkv
    FB = FF // n_down
    mine = lax.div(place.s, half)
    j_half = lax.rem(place.s, half)
    replica = lax.axis_index("replica")

    def half_peer(k):
        return (replica, mine * half + lax.rem(j_half + k, half))

    swap_peer = (replica, lax.rem(place.s + half, shards))

    big, slope, cot, gfeed = ref["big"], ref["slope_s"], ref["cot_s"], ref["gfeed"]
    lsem = ref["lsem"]

    def load(src, dst, sem):
        return pltpu.make_async_copy(src, dst, sem)

    act_loads = [
        load(ref["act"].at[:, pl.ds(n * W, W)], big.at[pl.ds(n * rows, rows)], lsem.at[n])
        for n in range(FF // W)
    ]
    plain = {}
    for number, (name, target) in enumerate(
        [("cot", cot), ("slope", slope), ("x", ref["x_s"]), ("branch", ref["branch_s"]),
         ("second", ref["second_s"]), ("attended", ref["attended_s"]), ("query", ref["query_s"]),
         ("first", ref["first_s"]), ("proj", ref["proj_s"])]
    ):
        plain[name] = load(ref[name], target, lsem.at[8 + number])
    key_load = load(ref["key"], big.at[pl.ds(0, keys)], lsem.at[4])
    value_load = load(ref["value"], big.at[pl.ds(keys, keys)], lsem.at[5])

    def down_load(i):
        return load(ref["down"].at[pl.ds(pl.multiple_of(i * FB, FB), FB)], ref["wd"].at[lax.rem(i, 2)],
                    ref["wsem"].at[0, lax.rem(i, 2)])

    def up_load(i):
        return load(ref["up"].at[:, pl.ds(pl.multiple_of(i * FB, FB), FB)], ref["wu"].at[lax.rem(i, 2)],
                    ref["wsem"].at[1, lax.rem(i, 2)])

    def qkv_load(i):
        return load(ref["qkv"].at[:, pl.ds(pl.multiple_of(i * FB, FB), FB)], ref["wu"].at[lax.rem(i, 2)],
                    ref["wsem"].at[2, lax.rem(i, 2)])

    plain["cot"].start()
    for copy in act_loads:
        copy.start()
    plain["slope"].start()
    down_load(0).start()
    up_load(0).start()
    for name in ("second", "x", "branch", "proj", "attended", "query", "first"):
        plain[name].start()

    extra = [half_peer(k) for k in range(1, half)] if half > 2 else []
    place.greet(extra)

    def core_copy(i):
        a = lax.rem(i, SLOTS)
        return send(part.at[lax.rem(i, 2), 1 - place.c], crecv.at[a], ref["cs"].at[a], ref["cr"].at[a],
                    place.at(c=1 - place.c))

    def y_copy(i, k):
        a = lax.rem(i, SLOTS)
        return send(ysum.at[a, place.ahead_y(k)], yrecv.at[a, k - 1], ref["ys"].at[a, k - 1],
                    ref["yr"].at[a, k - 1], place.at(y=place.ahead_y(k)))

    def x_copy(i):
        a = lax.rem(i, SLOTS)
        return send(xsum.at[a, 1 - place.x], xrecv.at[a], ref["xs"].at[a], ref["xr"].at[a],
                    place.at(x=1 - place.x))

    def z_copy(i, k):
        a = lax.rem(i, SLOTS)
        return send(zsum.at[a, place.ahead_z(k)], zrecv.at[a, k - 1], ref["zs"].at[a, k - 1],
                    ref["zr"].at[a, k - 1], place.at(z=place.ahead_z(k)))

    HB, WZ = CB // 2, W // Z
    x_rows = pl.ds(pl.multiple_of(place.x * HB, HB), HB)
    z_cols = pl.ds(pl.multiple_of(place.z * WZ, WZ), WZ)

    def zg_copy(i, k):
        a = lax.rem(i, SLOTS)
        block = out.at[i, x_rows, z_cols]
        return send(block, block, ref["gs"].at[a, k - 1], ref["gr"].at[a, k - 1],
                    place.at(z=place.ahead_z(k)))

    def xg_copy(i):
        a = lax.rem(i, SLOTS)
        block = out.at[i, x_rows]
        return send(block, block, ref["hs"].at[a], ref["hr"].at[a], place.at(x=1 - place.x))

    def add(*terms):
        whole = terms[0].astype(F32)
        for term in terms[1:]:
            whole = whole + term.astype(F32)
        return whole.astype(BF)

    def tick(i):
        def stage(lag):
            j = i - lag
            return j, (j >= 0) & (j < total)

        j1, ok1 = stage(1)

        @pl.when(ok1)
        def _():
            core_copy(j1).wait()
            a = lax.rem(j1, SLOTS)
            for y in range(Y):
                ysum[a, y] = add(part[lax.rem(j1, 2), place.c, y], crecv[a, y])
            for k in range(1, Y):
                y_copy(j1, k).start()

        j2, ok2 = stage(2)

        @pl.when(ok2)
        def _():
            a = lax.rem(j2, SLOTS)
            for k in range(1, Y):
                y_copy(j2, k).wait()
            for h in range(2):
                piece = slice(h * HB, (h + 1) * HB)
                xsum[a, h] = add(ysum[a, place.y, piece], *[yrecv[a, k - 1, piece] for k in range(1, Y)])
            x_copy(j2).start()

        j3, ok3 = stage(3)

        @pl.when(ok3)
        def _():
            a = lax.rem(j3, SLOTS)
            x_copy(j3).wait()
            for z in range(Z):
                cols = slice(z * WZ, (z + 1) * WZ)
                zsum[a, z] = add(xsum[a, place.x, :, cols], xrecv[a, :, cols])
            for k in range(1, Z):
                z_copy(j3, k).start()

        j4, ok4 = stage(4)

        @pl.when(ok4)
        def _():
            a = lax.rem(j4, SLOTS)
            for k in range(1, Z):
                z_copy(j4, k).wait()
            out[j4, x_rows, z_cols] = add(zsum[a, place.z], *[zrecv[a, k - 1] for k in range(1, Z)])
            for k in range(1, Z):
                zg_copy(j4, k).start()

        j5, ok5 = stage(5)

        @pl.when(ok5)
        def _():
            for k in range(1, Z):
                zg_copy(j5, k).wait()
            xg_copy(j5).start()

        j6, ok6 = stage(6)

        @pl.when(ok6)
        def _():
            xg_copy(j6).wait()

    def produce(i, part_rows, left, b, cols):
        slot = lax.rem(i, 2)
        for turn in range(2):
            c = 1 - place.c if turn == 0 else place.c
            for y in range(Y):
                first = place.part(y, c) * part_rows + b * CB
                if CB % 128 == 0:
                    value = matmul(left(pl.multiple_of(first, 128), CB), cols, ((0,), (0,))).astype(BF)
                else:
                    start = pl.multiple_of(lax.div(first, 128) * 128, 128)
                    ref["tile"][...] = matmul(left(start, 128), cols, ((0,), (0,)))
                    value = ref["tile"][pl.ds(pl.multiple_of(first - start, CB), CB)].astype(BF)
                part[slot, c, y] = value
            if turn == 0:
                core_copy(i).start()

    def act_cols(first, size):
        n = lax.div(first, W)
        return big[pl.ds(pl.multiple_of(n * rows, rows), rows),
                   pl.ds(pl.multiple_of(lax.rem(first, W), 128), size)]

    def from_ref(array):
        return lambda first, size: array[:, pl.ds(first, size)]

    def vector(row):
        return vec[row : row + 1, :]

    def note(row, value):
        small[0, 0, row : row + 1, :] += value

    small[0, 0] = jnp.zeros_like(small[0, 0])
    plain["cot"].wait()
    TR = min(128, rows)

    def feed_tile(t, _):
        tile = pl.ds(pl.multiple_of(t * TR, TR), TR)
        value = (cot[tile, :].astype(F32) * vector(V_MLP_SCALE)).astype(BF)
        gfeed[tile, :] = value
        note(DOWN_B, jnp.sum(value.astype(F32), axis=0, keepdims=True))
        return 0

    lax.fori_loop(0, rows // TR, feed_tile, 0)
    for copy in act_loads:
        copy.wait()
    plain["slope"].wait()
    acc, gmid = ref["acc"], ref["gmid"]
    acc[...] = jnp.zeros_like(acc)
    gmid[...] = jnp.zeros_like(gmid)

    def down_step(i, _):
        slot = lax.rem(i, 2)
        produce(i, down_rows, act_cols, i, gfeed[...])
        tick(i)
        down_load(i).wait()
        up_load(i).wait()

        @pl.when(i + 1 < n_down)
        def _():
            down_load(i + 1).start()
            up_load(i + 1).start()

        cols = pl.ds(pl.multiple_of(i * FB, FB), FB)
        weight = ref["wd"][slot]
        grad = matmul(gfeed[...], weight, ((1,), (1,)))
        pre = (grad * slope[:, cols].astype(F32)).astype(BF)
        slope[:, cols] = pre
        row = UP_B + lax.div(i * FB, W)
        at = pl.ds(pl.multiple_of(lax.rem(i * FB, W), FB), FB)
        small[0, 0, pl.ds(row, 1), at] = jnp.sum(pre.astype(F32), axis=0, keepdims=True)
        acc[...] += matmul(act_cols(i * FB, FB), weight)
        gmid[...] += matmul(pre, ref["wu"][slot], ((1,), (1,)))
        return 0

    lax.fori_loop(0, n_down, down_step, 0)

    key_load.start()
    value_load.start()
    for name in ("x", "branch", "proj", "second", "attended", "query", "first"):
        plain[name].wait()
    x_s, branch, gbranch, gatt = ref["x_s"], ref["branch_s"], ref["gbranch"], ref["gatt"]
    tok_out, tok_send = ref["tok_out"], ref["tok_send"]

    def middle_tile(t, _):
        tile = pl.ds(pl.multiple_of(t * TR, TR), TR)
        low = branch[tile, :]
        middle = x_s[tile, :].astype(F32) + vector(V_ATTN_SCALE) * low
        feed = acc[tile, :] + vector(V_DOWN_B)
        result = ((middle + vector(V_MLP_SCALE) * feed) * vector(V_LIVE)).astype(BF)
        lower = pl.ds(pl.multiple_of(lax.rem(t * TR, R), TR), TR) if R >= TR else pl.ds(0, R)
        if R >= TR:
            @pl.when(t * TR < R)
            def _():
                tok_out[mine, lower, :] = result

            @pl.when(t * TR >= R)
            def _():
                tok_send[lower, :] = result
        else:
            tok_out[mine] = result[:R]
            tok_send[...] = result[R:]
        upstream = cot[tile, :].astype(F32)
        note(MLP_SCALE, jnp.sum(upstream * feed, axis=0, keepdims=True))
        unit, scale = norm_parts(middle)
        grad = gmid[tile, :]
        note(MLP_GAIN, jnp.sum(grad * unit, axis=0, keepdims=True))
        note(MLP_SHIFT, jnp.sum(grad, axis=0, keepdims=True))
        grad = upstream + norm_back(grad, unit, scale, vector(V_MLP_GAIN))
        gmid[tile, :] = grad
        note(ATTN_SCALE, jnp.sum(grad * low, axis=0, keepdims=True))
        grad = (grad * vector(V_ATTN_SCALE)).astype(BF)
        gbranch[tile, :] = grad
        note(PROJ_B, jnp.sum(grad.astype(F32), axis=0, keepdims=True))
        gatt[tile, :] = matmul(grad, ref["proj_s"][...], ((1,), (1,))).astype(BF)
        return 0

    lax.fori_loop(0, rows // TR, middle_tile, 0)
    tok_copy = send(tok_send, tok_out.at[mine], ref["ts"].at[0], ref["tr"].at[0], swap_peer)
    tok_copy.start()
    key_load.wait()
    value_load.wait()

    G, query = ref["G"], ref["query_s"]
    pown, psend, precv = ref["pown"], ref["psend"], ref["precv"]
    gk_acc, gv_acc = ref["gk_acc"], ref["gv_acc"]
    pairs = W // 128
    QT = min(256, rows)

    def pair_copy(p, k):
        a = lax.rem(p, SLOTS)
        return send(psend.at[a, k - 1], precv.at[a, k - 1], ref["ps"].at[a, k - 1], ref["pr"].at[a, k - 1],
                    half_peer(k))

    def pair_done(p):
        a = lax.rem(p, SLOTS)
        for k in range(1, half):
            pair_copy(p, k).wait()
        for which in range(2):
            whole = pown[a, which]
            for k in range(1, half):
                whole = whole + precv[a, k - 1, which].astype(F32)
            cols = pl.ds(pl.multiple_of((which + 1) * W + p * 128, 128), 128)
            G[:, cols] = whole.astype(BF)

    def pair_step(p):
        lane = lax.broadcasted_iota(jnp.int32, (1, 128), 1)
        cols = pl.ds(pl.multiple_of(p * 128, 128), 128)
        key = big[pl.ds(0, keys), cols]
        value = big[pl.ds(keys, keys), cols]
        key_t = key.T
        for t in range(rows // QT):
            tile = slice(t * QT, (t + 1) * QT)
            q_tile, g_tile = query[tile, cols], gatt[tile, cols]
            parts = []
            for head in range(2):
                owned = (lane < HEAD_DIM) if head == 0 else (lane >= HEAD_DIM)
                own = jnp.where(owned, q_tile * BF(HEAD_DIM**-0.5), BF(0))
                own_grad = jnp.where(owned, g_tile, BF(0))
                probs = jnp.exp(matmul(key, own, ((1,), (1,))) - lse[p, head : head + 1, tile])
                grad_probs = matmul(value, own_grad, ((1,), (1,)))
                centre = jnp.sum(grad_probs * probs, axis=0, keepdims=True)
                grad_scores = (probs * (grad_probs - centre)).astype(BF)
                gv = matmul(probs.astype(BF), own_grad)
                gk = matmul(grad_scores, own)
                if t == 0 and head == 0:
                    gv_acc[...], gk_acc[...] = gv, gk
                else:
                    gv_acc[...] += gv
                    gk_acc[...] += gk
                lanes = slice(head * HEAD_DIM, (head + 1) * HEAD_DIM)
                parts.append(matmul(key_t[lanes, :], grad_scores))
            whole = jnp.concatenate(parts, axis=0) * (HEAD_DIM**-0.5)
            G[tile, cols] = whole.T.astype(BF)
        a = lax.rem(p, SLOTS)
        pown[a, 0], pown[a, 1] = gk_acc[:rows], gv_acc[:rows]
        for k in range(1, half):
            psend[a, k - 1, 0] = gk_acc[k * rows : (k + 1) * rows].astype(BF)
            psend[a, k - 1, 1] = gv_acc[k * rows : (k + 1) * rows].astype(BF)
            pair_copy(p, k).start()

    per_tick = pairs // n_up

    def up_step(u, _):
        i = n_down + u
        b, n = lax.rem(u, blocks), lax.div(u, blocks)
        produce(i, other_rows, from_ref(ref["second_s"]), b,
                slope[:, pl.ds(pl.multiple_of(n * W, W), W)])
        tick(i)
        for m in range(per_tick):
            p = u * per_tick + m
            pair_step(p)

            @pl.when(p >= 1)
            def _():
                pair_done(p - 1)
        return 0

    lax.fori_loop(0, n_up, up_step, 0)

    qkv_load(0).start()

    def proj_step(u, _):
        i = n_down + n_up + u
        produce(i, other_rows, from_ref(ref["attended_s"]), u, gbranch[...])
        tick(i)

        @pl.when(u == 0)
        def _():
            pair_done(pairs - 1)
        return 0

    lax.fori_loop(0, n_proj, proj_step, 0)
    acc[...] = jnp.zeros_like(acc)

    def qkv_step(u, _):
        i = n_down + n_up + n_proj + u
        b, n = lax.rem(u, blocks), lax.div(u, blocks)
        produce(i, other_rows, from_ref(ref["first_s"]), b, G[:, pl.ds(pl.multiple_of(n * W, W), W)])
        tick(i)
        qkv_load(u).wait()

        @pl.when(u + 1 < n_qkv)
        def _():
            qkv_load(u + 1).start()

        acc[...] += matmul(G[:, pl.ds(pl.multiple_of(u * FB, FB), FB)], ref["wu"][lax.rem(u, 2)],
                           ((1,), (1,)))
        return 0

    lax.fori_loop(0, n_qkv, qkv_step, 0)

    gt_out, gt_send, gt_recv = ref["gt_out"], ref["gt_send"], ref["gt_recv"]

    def first_tile(t, _):
        tile = pl.ds(pl.multiple_of(t * TR, TR), TR)
        unit, scale = norm_parts(x_s[tile, :].astype(F32))
        grad = acc[tile, :]
        note(ATTN_GAIN, jnp.sum(grad * unit, axis=0, keepdims=True))
        note(ATTN_SHIFT, jnp.sum(grad, axis=0, keepdims=True))
        note(QV, jnp.sum(G[tile, :W].astype(F32), axis=0, keepdims=True))
        note(QV + 1, jnp.sum(G[tile, 2 * W :].astype(F32), axis=0, keepdims=True))
        whole = gmid[tile, :] + norm_back(grad, unit, scale, vector(V_ATTN_GAIN))
        if R >= TR:
            lower = pl.ds(pl.multiple_of(lax.rem(t * TR, R), TR), TR)

            @pl.when(t * TR < R)
            def _():
                gt_out[mine, lower, :] = whole

            @pl.when(t * TR >= R)
            def _():
                gt_send[lower, :] = whole.astype(BF)
        else:
            gt_out[mine] = whole[:R]
            gt_send[...] = whole[R:].astype(BF)
        return 0

    lax.fori_loop(0, rows // TR, first_tile, 0)

    small_steps = [
        [place.at(c=1 - place.c)],
        [place.at(y=place.ahead_y(k)) for k in range(1, Y)],
        [place.at(x=1 - place.x)],
        [place.at(z=place.ahead_z(k)) for k in range(1, Z)],
    ]

    def small_send(step):
        return [
            send(small.at[step, 0], small.at[step, k + 1], ref["ss"].at[step, k], ref["sr"].at[step, k], device)
            for k, device in enumerate(small_steps[step])
        ]

    for copy in small_send(0):
        copy.start()
    gt_copy = send(gt_send, gt_recv, ref["ts"].at[1], ref["tr"].at[1], swap_peer)
    for lag in range(6):
        tick(total + lag)
        if lag == 0:
            gt_copy.start()
        if lag < 4:
            for copy in small_send(lag):
                copy.wait()
            whole = small[lag, 0]
            for k in range(len(small_steps[lag])):
                whole = whole + small[lag, k + 1]
            if lag < 3:
                small[lag + 1, 0] = whole
                for copy in small_send(lag + 1):
                    copy.start()
            else:
                ref["small_out"][...] = whole
    tok_copy.wait()
    gt_copy.wait()
    gt_out[1 - mine] = gt_recv[...].astype(F32)


def backward(replicas, shards, hbm, vec, lse):
    Y, Z, half = shards // 2, replicas // 2, shards // 2
    W = hbm["cot"].shape[1]
    rows, FF = hbm["act"].shape
    R, keys = rows // 2, hbm["key"].shape[0]
    CB = min(128, W // shards)
    HB, WZ = CB // 2, W // Z
    counts = (FF // shards // CB, (W // shards // CB) * (FF // W), W // shards // CB, 3 * (W // shards // CB))
    total = sum(counts)
    FB = FF // counts[0]
    peers = max(Y, Z, 2)
    dma = pltpu.SemaphoreType.DMA
    vmem, anywhere = pl.BlockSpec(memory_space=pltpu.VMEM), pl.BlockSpec(memory_space=pl.ANY)
    scratch = {
        "part": pltpu.VMEM((2, 2, Y, CB, W), BF),
        "crecv": pltpu.VMEM((SLOTS, Y, CB, W), BF),
        "ysum": pltpu.VMEM((SLOTS, Y, CB, W), BF),
        "yrecv": pltpu.VMEM((SLOTS, Y - 1, CB, W), BF),
        "xsum": pltpu.VMEM((SLOTS, 2, HB, W), BF),
        "xrecv": pltpu.VMEM((SLOTS, HB, W), BF),
        "zsum": pltpu.VMEM((SLOTS, Z, HB, WZ), BF),
        "zrecv": pltpu.VMEM((SLOTS, Z - 1, HB, WZ), BF),
        "small_buf": pltpu.VMEM((4, peers, 16, W), F32),
        "big": pltpu.VMEM((max(rows * FF // W, 2 * keys), W), BF),
        "slope_s": pltpu.VMEM((rows, FF), BF),
        "cot_s": pltpu.VMEM((rows, W), BF),
        "gfeed": pltpu.VMEM((rows, W), BF),
        "x_s": pltpu.VMEM((rows, W), BF),
        "branch_s": pltpu.VMEM((rows, W), F32),
        "second_s": pltpu.VMEM((rows, W), BF),
        "attended_s": pltpu.VMEM((rows, W), BF),
        "query_s": pltpu.VMEM((rows, W), BF),
        "first_s": pltpu.VMEM((rows, W), BF),
        "proj_s": pltpu.VMEM((W, W), BF),
        "wd": pltpu.VMEM((2, FB, W), BF),
        "wu": pltpu.VMEM((2, W, FB), BF),
        "acc": pltpu.VMEM((rows, W), F32),
        "gmid": pltpu.VMEM((rows, W), F32),
        "gbranch": pltpu.VMEM((rows, W), BF),
        "gatt": pltpu.VMEM((rows, W), BF),
        "G": pltpu.VMEM((rows, 3 * W), BF),
        "pown": pltpu.VMEM((SLOTS, 2, rows, 128), F32),
        "psend": pltpu.VMEM((SLOTS, half - 1, 2, rows, 128), BF),
        "precv": pltpu.VMEM((SLOTS, half - 1, 2, rows, 128), BF),
        "gk_acc": pltpu.VMEM((keys, 128), F32),
        "gv_acc": pltpu.VMEM((keys, 128), F32),
        "tok_send": pltpu.VMEM((R, W), BF),
        "gt_send": pltpu.VMEM((R, W), BF),
        "gt_recv": pltpu.VMEM((R, W), BF),
        "lsem": dma((24,)), "wsem": dma((3, 2)),
        "cs": dma((SLOTS,)), "cr": dma((SLOTS,)),
        "ys": dma((SLOTS, Y - 1)), "yr": dma((SLOTS, Y - 1)),
        "xs": dma((SLOTS,)), "xr": dma((SLOTS,)),
        "zs": dma((SLOTS, Z - 1)), "zr": dma((SLOTS, Z - 1)),
        "gs": dma((SLOTS, Z - 1)), "gr": dma((SLOTS, Z - 1)),
        "hs": dma((SLOTS,)), "hr": dma((SLOTS,)),
        "ps": dma((SLOTS, half - 1)), "pr": dma((SLOTS, half - 1)),
        "ss": dma((4, peers - 1)), "sr": dma((4, peers - 1)),
        "ts": dma((2,)), "tr": dma((2,)),
    }
    if CB % 128:
        scratch["tile"] = pltpu.VMEM((128, W), F32)
    outs = {
        "out": jax.ShapeDtypeStruct((total, CB, W), BF),
        "small_out": jax.ShapeDtypeStruct((16, W), F32),
        "tok_out": jax.ShapeDtypeStruct((2, R, W), BF),
        "gt_out": jax.ShapeDtypeStruct((2, R, W), F32),
    }
    names = HBM_INPUTS + ("vec", "lse") + tuple(outs) + tuple(scratch)
    out, small_out, tok_out, gt_out = pl.pallas_call(
        functools.partial(backward_kernel, replicas, shards, names),
        in_specs=[anywhere] * len(HBM_INPUTS) + [vmem, vmem],
        out_specs=[vmem] * len(outs),
        out_shape=list(outs.values()),
        scratch_shapes=list(scratch.values()),
        compiler_params=pltpu.CompilerParams(
            collective_id=1, has_side_effects=True, vmem_limit_bytes=63 * MIB
        ),
    )(*[hbm[name] for name in HBM_INPUTS], vec, lse)
    grads, base = [], 0
    for chunks, n_cols in zip(counts, (1, FF // W, 1, 3)):
        block = out[base : base + chunks].reshape(n_cols, -1, W).swapaxes(0, 1)
        grads.append(block.reshape(-1, n_cols * W).astype(F32))
        base += chunks
    return grads, small_out, tok_out, gt_out


def on_device(replicas, shards, tokens, qkv_weight, qv_bias, proj_weight, proj_bias, up_weight, up_bias,
              down_weight, down_bias, attn_gain, attn_shift, mlp_gain, mlp_shift, attn_scale, mlp_scale,
              cotangent, image_count):
    vectors = (qv_bias, proj_bias, up_bias, down_bias, attn_gain, attn_shift, mlp_gain, mlp_shift,
               attn_scale, mlp_scale)
    lengths = [v.shape[0] for v in vectors]
    n_small = sum(lengths)
    padded = -(-n_small // 2048) * 2048
    packed = jnp.pad(jnp.concatenate(vectors), (0, padded - n_small)).reshape(16, padded // 16)
    qkv_all, proj_all, up_all, down_all, small_all = gather_weights(
        replicas, shards, (qkv_weight, proj_weight, up_weight, down_weight), packed
    )
    width = tokens.shape[2]
    qkv_full, proj_full = qkv_all.reshape(width, -1), proj_all.reshape(width, -1)
    up_full, down_full = up_all.reshape(width, -1), down_all.reshape(-1, width)
    small_flat = small_all.reshape(shards, padded)
    full, place = [], 0
    for n in lengths:
        full.append(small_flat[:, place : place + n].reshape(-1).astype(F32))
        place += n
    (qv_shift, proj_shift, up_shift, down_shift, gain_first, shift_first, gain_second, shift_second,
     scale_first, scale_second) = full

    half = shards // 2
    shard = lax.axis_index("shard")
    mine = lax.div(shard, half)
    swap = [(i, (i + half) % shards) for i in range(shards)]

    def join(array):
        keep = lax.dynamic_index_in_dim(array, mine, 0, keepdims=False)
        give = lax.dynamic_index_in_dim(array, 1 - mine, 0, keepdims=False)
        return jnp.concatenate([keep, lax.ppermute(give, "shard", swap)], axis=0)

    joined = join(tokens)
    inputs = joined.astype(F32)
    live = mine < image_count[lax.axis_index("replica")]
    upstream = jnp.where(live, join(cotangent), BF(0))
    groups = [list(range(half)), list(range(half, shards))]
    other = [(i, i ^ 1) for i in range(shards)]

    def all_rows(array):
        if half == 2:
            return jnp.concatenate([array, lax.ppermute(array, "shard", other)], axis=0)
        whole = lax.all_gather(array, "shard", axis=0, tiled=True, axis_index_groups=groups)
        return jnp.roll(whole, -lax.rem(shard, half) * array.shape[0], axis=0)

    unit_first, _ = norm_parts(inputs)
    normed_low = (unit_first * gain_first + shift_first).astype(BF)
    projected = matmul(normed_low, qkv_full)
    queries = (projected[:, :width] + qv_shift[:width]).astype(BF)
    keys = projected[:, width : 2 * width].astype(BF)
    values = (projected[:, 2 * width :] + qv_shift[width:]).astype(BF)
    keys_all, values_all = all_rows(keys), all_rows(values)
    attended, lse = attention_forward(queries, keys_all, values_all)
    branch = matmul(attended, proj_full) + proj_shift
    middle = inputs + scale_first * branch
    unit_second, _ = norm_parts(middle)
    second_low = (unit_second * gain_second + shift_second).astype(BF)
    hidden = matmul(second_low, up_full) + up_shift
    gate = 0.5 * (1.0 + lax.erf(hidden * (0.5**0.5)))
    act = (hidden * gate).astype(BF)
    slope = (gate + hidden * (jnp.exp(-0.5 * hidden * hidden) * 0.3989422804014327)).astype(BF)

    vec = jnp.stack([scale_second, gain_second, scale_first, gain_first, down_shift,
                     jnp.broadcast_to(live.astype(F32), (width,))])
    vec = jnp.concatenate([vec, jnp.zeros((2, width), F32)])
    hbm = dict(act=act, slope=slope, cot=upstream, x=joined, branch=branch, second=second_low,
               attended=attended, query=queries, key=keys_all, value=values_all, first=normed_low,
               down=down_full, up=up_full, proj=proj_full, qkv=qkv_full)
    grads, small, output, grad_tokens = backward(replicas, shards, hbm, vec, lse)
    grad_down, grad_up, grad_proj, grad_qkv = grads

    def own(row, count=1):
        whole = small[row : row + count].reshape(-1)
        size = whole.shape[0] // shards
        return lax.dynamic_slice_in_dim(whole, shard * size, size)

    return (output, grad_tokens, grad_qkv, own(QV, 2), grad_proj, own(PROJ_B), grad_up,
            own(UP_B, up_bias.shape[0] * shards // width), grad_down, own(DOWN_B), own(ATTN_GAIN),
            own(ATTN_SHIFT), own(MLP_GAIN), own(MLP_SHIFT), own(ATTN_SCALE), own(MLP_SCALE))


def solution(mesh):
    rows, vector = P("shard", None), P("shard")
    image = P("replica", "shard", None)
    in_specs = (image, rows, vector, rows, vector, rows, vector, rows, vector, vector, vector, vector,
                vector, vector, vector, image, P())
    out_specs = (image, image, rows, vector, rows, vector, rows, vector, rows, vector, vector, vector,
                 vector, vector, vector, vector)
    return jax.shard_map(
        functools.partial(on_device, mesh.shape["replica"], mesh.shape["shard"]),
        mesh=mesh, in_specs=in_specs, out_specs=out_specs, check_vma=False,
    )
```

```python
import functools

import jax
import jax.numpy as jnp
from jax import lax
from jax.experimental import pallas as pl
from jax.experimental.pallas import tpu as pltpu
from jax.sharding import PartitionSpec as P

HEAD_DIM = 64
EPS = 1e-06
BF = jnp.bfloat16
F32 = jnp.float32
MESH = pl.DeviceIdType.MESH
MIB = 1024 * 1024
SLOTS = 4


def matmul(left, right, dims=((1,), (0,))):
    return lax.dot_general(left, right, (dims, ((), ())), preferred_element_type=F32)


class Place:
    def __init__(self, replicas, shards):
        self.Z, self.Y = replicas // 2, shards // 2
        self.shards = shards
        replica, shard = lax.axis_index("replica"), lax.axis_index("shard")
        self.x, self.z = lax.rem(replica, 2), lax.div(replica, 2)
        self.c, self.y = lax.rem(shard, 2), lax.div(shard, 2)
        self.s = shard

    def part(self, y, c):
        return y * 2 + c

    def at(self, x=None, z=None, y=None, c=None):
        x = self.x if x is None else x
        z = self.z if z is None else z
        y = self.y if y is None else y
        c = self.c if c is None else c
        return (z * 2 + x, y * 2 + c)

    def ahead_z(self, k):
        return lax.rem(self.z + k, self.Z)

    def behind_z(self, k):
        return lax.rem(self.z + self.Z - k, self.Z)

    def ahead_y(self, k):
        return lax.rem(self.y + k, self.Y)

    def behind_y(self, k):
        return lax.rem(self.y + self.Y - k, self.Y)

    def greet(self, extra=()):
        others = [self.at(c=1 - self.c), self.at(x=1 - self.x)]
        others += [self.at(y=self.ahead_y(k)) for k in range(1, self.Y)]
        others += [self.at(z=self.ahead_z(k)) for k in range(1, self.Z)]
        others += list(extra)
        barrier = pltpu.get_barrier_semaphore()
        for other in others:
            pl.semaphore_signal(barrier, inc=1, device_id=other, device_id_type=MESH)
        pl.semaphore_wait(barrier, len(others))


def send(src, dst, send_sem, recv_sem, device):
    return pltpu.make_async_remote_copy(
        src_ref=src,
        dst_ref=dst,
        send_sem=send_sem,
        recv_sem=recv_sem,
        device_id=device,
        device_id_type=MESH,
    )


QV, PROJ_B, UP_B, DOWN_B, ATTN_GAIN, ATTN_SHIFT, MLP_GAIN, MLP_SHIFT, ATTN_SCALE, MLP_SCALE, LIVE = (
    0, 2, 3, 7, 8, 9, 10, 11, 12, 13, 14)
WEIGHTS = ("qkv", "proj", "up", "down")


def norm_parts(values):
    centre = values - jnp.mean(values, axis=-1, keepdims=True)
    scale = lax.rsqrt(jnp.mean(centre * centre, axis=-1, keepdims=True) + EPS)
    return centre * scale, scale


def norm_back(grad, unit, scale, gain):
    inner = grad * gain
    return scale * (
        inner
        - jnp.mean(inner, axis=-1, keepdims=True)
        - unit * jnp.mean(inner * unit, axis=-1, keepdims=True)
    )


def forward_kernel(replicas, shards, items, multiples, names, *refs):
    ref = dict(zip(names, refs))
    place = Place(replicas, shards)
    Y, Z, s = place.Y, place.Z, place.s
    half = shards // 2
    mine, j_half = lax.div(s, half), lax.rem(s, half)
    replica = lax.axis_index("replica")
    x_s, cot_s, first, query = ref["x_s"], ref["cot_s"], ref["first_s"], ref["query_s"]
    key, value, attended = ref["key_s"], ref["value_s"], ref["attended_s"]
    vec, lse = ref["vec"], ref["lse"]
    rows, W = x_s.shape
    R, keys = rows // 2, key.shape[0]
    weights = {name: ref["w_" + name] for name in WEIGHTS}
    shard_rows = {name: ref[name].shape[0] for name in WEIGHTS}
    FF = weights["up"].shape[1]

    def half_peer(k):
        return (replica, mine * half + lax.rem(j_half + k, half))

    swap_peer = (replica, lax.rem(s + half, shards))

    def own_rows(name):
        size = shard_rows[name]
        return weights[name].at[pl.ds(pl.multiple_of(s * size, size), size)]

    x_load = pltpu.make_async_copy(ref["tokens"].at[mine], x_s.at[pl.ds(0, R)], ref["lsem"].at[0])
    cot_load = pltpu.make_async_copy(ref["cotangent"].at[mine], cot_s.at[pl.ds(0, R)], ref["lsem"].at[1])
    own_loads = {
        name: pltpu.make_async_copy(ref[name], own_rows(name), ref["lsem"].at[2 + n])
        for n, name in enumerate(WEIGHTS)
    }
    small_load = pltpu.make_async_copy(ref["packed"], ref["small_s"].at[s], ref["lsem"].at[6])
    x_load.start()
    small_load.start()
    for name in WEIGHTS:
        own_loads[name].start()
    cot_load.start()
    extra = [(replica, lax.rem(s + k, shards)) for k in range(1, shards)]
    place.greet(extra)

    x_swap = send(ref["tokens"].at[1 - mine], x_s.at[pl.ds(R, R)], ref["ts"].at[0], ref["tr"].at[0], swap_peer)
    cot_swap = send(ref["cotangent"].at[1 - mine], cot_s.at[pl.ds(R, R)], ref["ts"].at[1], ref["tr"].at[1],
                    swap_peer)
    small_sends = [
        send(ref["packed"], ref["small_s"].at[s], ref["ss"].at[k - 1], ref["sr"].at[k - 1],
             (replica, lax.rem(s + k, shards)))
        for k in range(1, shards)
    ]
    own_sends = {
        name: send(ref[name], own_rows(name), ref["os"].at[n], ref["or"].at[n], place.at(c=1 - place.c))
        for n, name in enumerate(WEIGHTS)
    }

    def piece(m, owner, whole_rows=False, whole_cols=False):
        name, start, size, _ = items[m]
        at = owner * shard_rows[name] + start
        step = ref[name].shape[1] // Z
        if not whole_rows:
            at, size = at + place.x * (size // 2), size // 2
        at = pl.ds(pl.multiple_of(at, 16), size)
        if whole_cols:
            return at, slice(None)
        return at, pl.ds(pl.multiple_of(place.z * step, 128), step)

    def y_copy(m, k):
        name, _, _, direct = items[m]
        src = ref[name].at[piece(m, 0, direct, direct)]
        dst = weights[name].at[piece(m, s, direct, direct)]
        return send(src, dst, ref["ys"].at[m, k - 1], ref["yr"].at[m, k - 1], place.at(y=place.ahead_y(k)))

    def block(m, k, whole_rows, whole_cols):
        owner = place.part(place.behind_y(k), place.c)
        return weights[items[m][0]].at[piece(m, owner, whole_rows, whole_cols)]

    def z_copy(m, k, j):
        b = block(m, k, False, False)
        return send(b, b, ref["zs"].at[m, k - 1, j - 1], ref["zr"].at[m, k - 1, j - 1],
                    place.at(z=place.ahead_z(j)))

    def x_copy(m, k):
        b = block(m, k, False, True)
        return send(b, b, ref["xs"].at[m, k - 1], ref["xr"].at[m, k - 1], place.at(x=1 - place.x))

    def c_copy(m, k):
        b = block(m, k, True, True)
        return send(b, b, ref["cs"].at[m, k - 1], ref["cr"].at[m, k - 1], place.at(c=1 - place.c))

    def y_start(m):
        for k in range(1, Y):
            y_copy(m, k).start()

    def y_step(m):
        for k in range(1, Y):
            y_copy(m, k).wait()
            if items[m][3]:
                c_copy(m, k).start()
            else:
                for j in range(1, Z):
                    z_copy(m, k, j).start()

    def z_step(m):
        for k in range(1, Y):
            for j in range(1, Z):
                z_copy(m, k, j).wait()
            x_copy(m, k).start()

    def x_step(m):
        for k in range(1, Y):
            x_copy(m, k).wait()
            c_copy(m, k).start()

    def c_step(m):
        for k in range(1, Y):
            c_copy(m, k).wait()

    QKV_A, QKV_B, PROJ, UP_A, UP_B2, DOWN_A, DOWN_B2 = range(7)
    stores = []

    def store(src, dst):
        copy = pltpu.make_async_copy(src, dst, ref["osem"].at[len(stores)])
        stores.append(copy)
        copy.start()

    y_start(QKV_A)
    x_swap.start()
    for copy in small_sends:
        copy.start()
    y_start(QKV_B)
    for name in WEIGHTS:
        own_sends[name].start()

    small_load.wait()
    for copy in small_sends:
        copy.wait()
    vec[...] = jnp.zeros_like(vec)
    row = 0
    for count in multiples:
        pieces = [ref["small_s"][part, row + r : row + r + 1, :].astype(F32)
                  for part in range(shards) for r in range(count)]
        for r in range(count):
            vec[row + r : row + r + 1, :] = jnp.concatenate(pieces[r * shards : (r + 1) * shards], axis=1)
        row += count
    vec[LIVE : LIVE + 1, :] = ref["live"][0:1, :]

    def vector(at):
        return vec[at : at + 1, :]

    TR = min(128, R)

    def first_tile(t, _):
        tile = pl.ds(pl.multiple_of(t * TR, TR), TR)
        unit, _ = norm_parts(x_s[tile, :].astype(F32))
        first[tile, :] = (unit * vector(ATTN_GAIN) + vector(ATTN_SHIFT)).astype(BF)
        return 0

    x_load.wait()
    lax.fori_loop(0, R // TR, first_tile, 0)
    y_step(QKV_A)
    y_start(PROJ)
    y_start(UP_A)
    y_start(UP_B2)
    x_swap.wait()
    cot_swap.start()
    lax.fori_loop(R // TR, rows // TR, first_tile, 0)
    store(first, ref["o_first"])
    store(x_s, ref["o_x"])
    own_loads["qkv"].wait()
    own_sends["qkv"].wait()
    y_step(PROJ)
    y_step(UP_A)

    acc = ref["acc"]
    CT = min(512, W)
    chunk = 2 * shard_rows["qkv"]

    def project(y, cols):
        at = pl.ds(pl.multiple_of(y * chunk, chunk), chunk)
        return matmul(first[:, at], weights["qkv"][at, cols])

    def near_tile(n, _):
        cols = pl.ds(pl.multiple_of(n * CT, CT), CT)
        acc[:, cols] = project(place.y, cols)
        return 0

    lax.fori_loop(0, 3 * W // CT, near_tile, 0)
    z_step(QKV_A)
    y_start(DOWN_A)
    y_start(DOWN_B2)
    x_step(QKV_A)
    y_step(QKV_B)
    z_step(PROJ)
    c_step(QKV_A)
    c_step(QKV_B)

    def full_tile(n):
        cols = slice(n * CT, (n + 1) * CT)
        whole = acc[:, cols]
        for k in range(1, Y):
            whole = whole + project(place.ahead_y(k), cols)
        return whole

    per = W // CT

    def kv_copy(which, n, k):
        array = (key, value)[which]
        cols = pl.ds(n * CT, CT)
        return send(array.at[pl.ds(0, rows), cols], array.at[pl.ds((half - k) * rows, rows), cols],
                    ref["ks"].at[which, n, k - 1], ref["kr"].at[which, n, k - 1], half_peer(k))

    for n in range(per):
        here = slice(n * CT, (n + 1) * CT)
        key[:rows, here] = full_tile(per + n).astype(BF)
        for k in range(1, half):
            kv_copy(0, n, k).start()
        value[:rows, here] = (full_tile(2 * per + n) + vector(QV + 1)[:, here]).astype(BF)
        for k in range(1, half):
            kv_copy(1, n, k).start()
    for n in range(per):
        here = slice(n * CT, (n + 1) * CT)
        query[:, here] = (full_tile(n) + vector(QV)[:, here]).astype(BF)
    store(weights["qkv"], ref["o_qkv"])
    store(query, ref["o_query"])

    pairs = W // 128
    QT = min(256, rows)
    x_step(PROJ)
    y_step(UP_B2)

    def attend(p, _):
        for n in range(per):
            @pl.when(p == n * (pairs // per))
            def _():
                for k in range(1, half):
                    kv_copy(0, n, k).wait()
                    kv_copy(1, n, k).wait()

        for at, steps in (
            (1, ((z_step, UP_A), (c_step, PROJ), (y_step, DOWN_A))),
            (4, ((z_step, UP_B2), (x_step, UP_A))),
            (6, ((z_step, DOWN_A),)),
            (7, ((x_step, UP_B2), (c_step, UP_A))),
        ):
            @pl.when(p == at)
            def _():
                for step, m in steps:
                    step(m)

        lane = lax.broadcasted_iota(jnp.int32, (1, 128), 1)
        cols = pl.ds(pl.multiple_of(p * 128, 128), 128)
        key_p, value_p = key[:, cols], value[:, cols]
        value_t = value_p.T
        for t in range(rows // QT):
            tile = slice(t * QT, (t + 1) * QT)
            q_tile = query[tile, cols] * BF(HEAD_DIM**-0.5)
            parts = []
            for head in range(2):
                owned = (lane < HEAD_DIM) if head == 0 else (lane >= HEAD_DIM)
                scores = matmul(key_p, jnp.where(owned, q_tile, BF(0)), ((1,), (1,)))
                highest = jnp.max(scores, axis=0, keepdims=True)
                expos = jnp.exp(scores - highest)
                denom = jnp.sum(expos, axis=0, keepdims=True)
                probs = (expos * (1.0 / denom)).astype(BF)
                lse[p, head : head + 1, tile] = highest + jnp.log(denom)
                lanes = slice(head * HEAD_DIM, (head + 1) * HEAD_DIM)
                parts.append(matmul(value_t[lanes, :], probs))
            attended[tile, cols] = jnp.concatenate(parts, axis=0).T.astype(BF)
        return 0

    lax.fori_loop(0, pairs, attend, 0)
    store(key, ref["o_key"])
    store(value, ref["o_value"])
    store(attended, ref["o_attended"])
    own_loads["proj"].wait()
    own_sends["proj"].wait()
    store(weights["proj"], ref["o_proj"])

    branch, second = ref["branch_s"], ref["second_s"]
    MT = min(256, rows)

    def branch_tile(t, _):
        tile = pl.ds(pl.multiple_of(t * MT, MT), MT)
        low = matmul(attended[tile, :], weights["proj"][...]) + vector(PROJ_B)
        branch[tile, :] = low
        unit, _ = norm_parts(x_s[tile, :].astype(F32) + vector(ATTN_SCALE) * low)
        second[tile, :] = (unit * vector(MLP_GAIN) + vector(MLP_SHIFT)).astype(BF)
        return 0

    lax.fori_loop(0, rows // MT, branch_tile, 0)
    store(branch, ref["o_branch"])
    store(second, ref["o_second"])
    cot_load.wait()
    cot_swap.wait()
    store(cot_s, ref["o_cot"])
    x_step(DOWN_A)
    y_step(DOWN_B2)
    own_loads["up"].wait()
    own_sends["up"].wait()
    c_step(UP_B2)
    store(weights["up"], ref["o_up"])

    FT = ref["act_s"].shape[2]

    def act_store(i, which):
        name = ("act", "slope")[which]
        return pltpu.make_async_copy(
            ref[name + "_s"].at[lax.rem(i, 2)],
            ref["o_" + name].at[:, pl.ds(pl.multiple_of(i * FT, FT), FT)],
            ref["asem"].at[which, lax.rem(i, 2)],
        )

    steps = FF // FT

    def up_tile(i, _):
        @pl.when(i >= 2)
        def _():
            act_store(i - 2, 0).wait()
            act_store(i - 2, 1).wait()

        cols = pl.ds(pl.multiple_of(i * FT, FT), FT)
        bias = vec[pl.ds(UP_B + lax.div(i * FT, W), 1), pl.ds(pl.multiple_of(lax.rem(i * FT, W), FT), FT)]
        for t in range(rows // MT):
            tile = slice(t * MT, (t + 1) * MT)
            hidden = matmul(second[tile, :], weights["up"][:, cols]) + bias
            gate = 0.5 * (1.0 + lax.erf(hidden * (0.5**0.5)))
            ref["act_s"][lax.rem(i, 2), tile, :] = (hidden * gate).astype(BF)
            bell = jnp.exp(-0.5 * hidden * hidden) * 0.3989422804014327
            ref["slope_s"][lax.rem(i, 2), tile, :] = (gate + hidden * bell).astype(BF)
        act_store(i, 0).start()
        act_store(i, 1).start()
        return 0

    lax.fori_loop(0, steps, up_tile, 0)
    c_step(DOWN_A)
    c_step(DOWN_B2)
    own_loads["down"].wait()
    own_sends["down"].wait()
    store(weights["down"], ref["o_down"])
    for i in range(steps - 2, steps):
        act_store(i, 0).wait()
        act_store(i, 1).wait()
    for copy in stores:
        copy.wait()


def forward(replicas, shards, tokens, cotangent, shards_of, packed, live, multiples):
    Y, Z, half = shards // 2, replicas // 2, shards // 2
    _, R, W = tokens.shape
    rows, keys = 2 * R, half * 2 * R
    FF = shards_of["up"].shape[1]
    size = {name: shards_of[name].shape[0] for name in WEIGHTS}
    q, p, u, d = (size[name] for name in WEIGHTS)
    items = (
        ("qkv", 0, q // 2, False), ("qkv", q // 2, q // 2, True), ("proj", 0, p, False),
        ("up", 0, u // 2, False), ("up", u // 2, u // 2, False),
        ("down", 0, d // 2, False), ("down", d // 2, d // 2, True),
    )
    FT = min(512, FF)
    dma = pltpu.SemaphoreType.DMA
    vmem, anywhere = pl.BlockSpec(memory_space=pltpu.VMEM), pl.BlockSpec(memory_space=pl.ANY)
    inputs = dict(tokens=tokens, cotangent=cotangent, packed=packed, live=live, **shards_of)
    outs = {
        "o_qkv": ((W, 3 * W), BF), "o_proj": ((W, W), BF), "o_up": ((W, FF), BF), "o_down": ((FF, W), BF),
        "o_act": ((rows, FF), BF), "o_slope": ((rows, FF), BF), "o_cot": ((rows, W), BF),
        "o_x": ((rows, W), BF), "o_branch": ((rows, W), F32), "o_second": ((rows, W), BF),
        "o_attended": ((rows, W), BF), "o_query": ((rows, W), BF), "o_key": ((keys, W), BF),
        "o_value": ((keys, W), BF), "o_first": ((rows, W), BF),
        "vec": ((16, W), F32), "lse": ((W // 128, 2, rows), F32),
    }
    m, per = len(items), W // min(512, W)
    scratch = {
        "w_qkv": pltpu.VMEM((W, 3 * W), BF), "w_proj": pltpu.VMEM((W, W), BF),
        "w_up": pltpu.VMEM((W, FF), BF), "w_down": pltpu.VMEM((FF, W), BF),
        "x_s": pltpu.VMEM((rows, W), BF), "cot_s": pltpu.VMEM((rows, W), BF),
        "first_s": pltpu.VMEM((rows, W), BF), "acc": pltpu.VMEM((rows, 3 * W), F32),
        "query_s": pltpu.VMEM((rows, W), BF), "key_s": pltpu.VMEM((keys, W), BF),
        "value_s": pltpu.VMEM((keys, W), BF), "attended_s": pltpu.VMEM((rows, W), BF),
        "branch_s": pltpu.VMEM((rows, W), F32), "second_s": pltpu.VMEM((rows, W), BF),
        "act_s": pltpu.VMEM((2, rows, FT), BF), "slope_s": pltpu.VMEM((2, rows, FT), BF),
        "small_s": pltpu.VMEM((shards,) + packed.shape, BF),
        "lsem": dma((8,)), "osem": dma((16,)), "asem": dma((2, 2)),
        "ts": dma((2,)), "tr": dma((2,)),
        "ss": dma((shards - 1,)), "sr": dma((shards - 1,)),
        "os": dma((4,)), "or": dma((4,)),
        "ys": dma((m, Y - 1)), "yr": dma((m, Y - 1)),
        "zs": dma((m, Y - 1, Z - 1)), "zr": dma((m, Y - 1, Z - 1)),
        "xs": dma((m, Y - 1)), "xr": dma((m, Y - 1)),
        "cs": dma((m, Y - 1)), "cr": dma((m, Y - 1)),
        "ks": dma((2, per, half - 1)), "kr": dma((2, per, half - 1)),
    }
    names = tuple(inputs) + tuple(outs) + tuple(scratch)
    results = pl.pallas_call(
        functools.partial(forward_kernel, replicas, shards, items, multiples, names),
        in_specs=[vmem if name == "live" else anywhere for name in inputs],
        out_specs=[vmem if name in ("vec", "lse") else anywhere for name in outs],
        out_shape=[jax.ShapeDtypeStruct(*shape) for shape in outs.values()],
        scratch_shapes=list(scratch.values()),
        compiler_params=pltpu.CompilerParams(
            collective_id=0, has_side_effects=True, vmem_limit_bytes=63 * MIB
        ),
    )(*inputs.values())
    return dict(zip((name.removeprefix("o_") for name in outs), results))


HBM_INPUTS = ("act", "slope", "cot", "x", "branch", "second", "attended", "query", "key", "value",
              "first", "down", "up", "proj", "qkv")


def backward_kernel(replicas, shards, names, *refs):
    ref = dict(zip(names, refs))
    place = Place(replicas, shards)
    Y, Z = place.Y, place.Z
    half = shards // 2
    part, crecv, ysum, yrecv = ref["part"], ref["crecv"], ref["ysum"], ref["yrecv"]
    xsum, xrecv, zsum, zrecv = ref["xsum"], ref["xrecv"], ref["zsum"], ref["zrecv"]
    out, small, vec, lse = ref["out"], ref["small_buf"], ref["vec"], ref["lse"]
    CB, W = part.shape[3], part.shape[4]
    rows = ref["gfeed"].shape[0]
    R = rows // 2
    keys = half * rows
    FF = ref["slope_s"].shape[1]
    down_rows, other_rows = FF // shards, W // shards
    blocks_d, blocks = down_rows // CB, other_rows // CB
    n_down, n_up, n_proj, n_qkv = blocks_d, blocks * (FF // W), blocks, blocks * 3
    total = n_down + n_up + n_proj + n_qkv
    FB = FF // n_down
    mine = lax.div(place.s, half)
    j_half = lax.rem(place.s, half)
    replica = lax.axis_index("replica")

    def half_peer(k):
        return (replica, mine * half + lax.rem(j_half + k, half))

    swap_peer = (replica, lax.rem(place.s + half, shards))

    big, slope, cot, gfeed = ref["big"], ref["slope_s"], ref["cot_s"], ref["gfeed"]
    lsem = ref["lsem"]

    def load(src, dst, sem):
        return pltpu.make_async_copy(src, dst, sem)

    act_loads = [
        load(ref["act"].at[:, pl.ds(n * W, W)], big.at[pl.ds(n * rows, rows)], lsem.at[n])
        for n in range(FF // W)
    ]
    plain = {}
    for number, (name, target) in enumerate(
        [("cot", cot), ("slope", slope), ("x", ref["x_s"]), ("branch", ref["branch_s"]),
         ("second", ref["second_s"]), ("attended", ref["attended_s"]), ("query", ref["query_s"]),
         ("first", ref["first_s"]), ("proj", ref["proj_s"])]
    ):
        plain[name] = load(ref[name], target, lsem.at[8 + number])
    key_load = load(ref["key"], big.at[pl.ds(0, keys)], lsem.at[4])
    value_load = load(ref["value"], big.at[pl.ds(keys, keys)], lsem.at[5])

    def down_load(i):
        return load(ref["down"].at[pl.ds(pl.multiple_of(i * FB, FB), FB)], ref["wd"].at[lax.rem(i, 2)],
                    ref["wsem"].at[0, lax.rem(i, 2)])

    def up_load(i):
        return load(ref["up"].at[:, pl.ds(pl.multiple_of(i * FB, FB), FB)], ref["wu"].at[lax.rem(i, 2)],
                    ref["wsem"].at[1, lax.rem(i, 2)])

    def qkv_load(i):
        return load(ref["qkv"].at[:, pl.ds(pl.multiple_of(i * FB, FB), FB)], ref["wu"].at[lax.rem(i, 2)],
                    ref["wsem"].at[2, lax.rem(i, 2)])

    plain["cot"].start()
    for copy in act_loads:
        copy.start()
    plain["slope"].start()
    down_load(0).start()
    up_load(0).start()
    for name in ("second", "x", "branch", "proj", "attended", "query", "first"):
        plain[name].start()

    extra = [half_peer(k) for k in range(1, half)] if half > 2 else []
    place.greet(extra)

    def core_copy(i):
        a = lax.rem(i, SLOTS)
        return send(part.at[lax.rem(i, 2), 1 - place.c], crecv.at[a], ref["cs"].at[a], ref["cr"].at[a],
                    place.at(c=1 - place.c))

    def y_copy(i, k):
        a = lax.rem(i, SLOTS)
        return send(ysum.at[a, place.ahead_y(k)], yrecv.at[a, k - 1], ref["ys"].at[a, k - 1],
                    ref["yr"].at[a, k - 1], place.at(y=place.ahead_y(k)))

    def x_copy(i):
        a = lax.rem(i, SLOTS)
        return send(xsum.at[a, 1 - place.x], xrecv.at[a], ref["xs"].at[a], ref["xr"].at[a],
                    place.at(x=1 - place.x))

    def z_copy(i, k):
        a = lax.rem(i, SLOTS)
        return send(zsum.at[a, place.ahead_z(k)], zrecv.at[a, k - 1], ref["zs"].at[a, k - 1],
                    ref["zr"].at[a, k - 1], place.at(z=place.ahead_z(k)))

    HB, WZ = CB // 2, W // Z
    x_rows = pl.ds(pl.multiple_of(place.x * HB, HB), HB)
    z_cols = pl.ds(pl.multiple_of(place.z * WZ, WZ), WZ)

    def zg_copy(i, k):
        a = lax.rem(i, SLOTS)
        block = out.at[i, x_rows, z_cols]
        return send(block, block, ref["gs"].at[a, k - 1], ref["gr"].at[a, k - 1],
                    place.at(z=place.ahead_z(k)))

    def xg_copy(i):
        a = lax.rem(i, SLOTS)
        block = out.at[i, x_rows]
        return send(block, block, ref["hs"].at[a], ref["hr"].at[a], place.at(x=1 - place.x))

    def add(*terms):
        whole = terms[0].astype(F32)
        for term in terms[1:]:
            whole = whole + term.astype(F32)
        return whole.astype(BF)

    def tick(i):
        def stage(lag):
            j = i - lag
            return j, (j >= 0) & (j < total)

        j1, ok1 = stage(1)

        @pl.when(ok1)
        def _():
            core_copy(j1).wait()
            a = lax.rem(j1, SLOTS)
            for y in range(Y):
                ysum[a, y] = add(part[lax.rem(j1, 2), place.c, y], crecv[a, y])
            for k in range(1, Y):
                y_copy(j1, k).start()

        j2, ok2 = stage(2)

        @pl.when(ok2)
        def _():
            a = lax.rem(j2, SLOTS)
            for k in range(1, Y):
                y_copy(j2, k).wait()
            for h in range(2):
                piece = slice(h * HB, (h + 1) * HB)
                xsum[a, h] = add(ysum[a, place.y, piece], *[yrecv[a, k - 1, piece] for k in range(1, Y)])
            x_copy(j2).start()

        j3, ok3 = stage(3)

        @pl.when(ok3)
        def _():
            a = lax.rem(j3, SLOTS)
            x_copy(j3).wait()
            for z in range(Z):
                cols = slice(z * WZ, (z + 1) * WZ)
                zsum[a, z] = add(xsum[a, place.x, :, cols], xrecv[a, :, cols])
            for k in range(1, Z):
                z_copy(j3, k).start()

        j4, ok4 = stage(4)

        @pl.when(ok4)
        def _():
            a = lax.rem(j4, SLOTS)
            for k in range(1, Z):
                z_copy(j4, k).wait()
            out[j4, x_rows, z_cols] = add(zsum[a, place.z], *[zrecv[a, k - 1] for k in range(1, Z)])
            for k in range(1, Z):
                zg_copy(j4, k).start()

        j5, ok5 = stage(5)

        @pl.when(ok5)
        def _():
            for k in range(1, Z):
                zg_copy(j5, k).wait()
            xg_copy(j5).start()

        j6, ok6 = stage(6)

        @pl.when(ok6)
        def _():
            xg_copy(j6).wait()

    def produce(i, part_rows, left, b, cols):
        slot = lax.rem(i, 2)
        for turn in range(2):
            c = 1 - place.c if turn == 0 else place.c
            for y in range(Y):
                first = place.part(y, c) * part_rows + b * CB
                if CB % 128 == 0:
                    value = matmul(left(pl.multiple_of(first, 128), CB), cols, ((0,), (0,))).astype(BF)
                else:
                    start = pl.multiple_of(lax.div(first, 128) * 128, 128)
                    ref["tile"][...] = matmul(left(start, 128), cols, ((0,), (0,)))
                    value = ref["tile"][pl.ds(pl.multiple_of(first - start, CB), CB)].astype(BF)
                part[slot, c, y] = value
            if turn == 0:
                core_copy(i).start()

    def act_cols(first, size):
        n = lax.div(first, W)
        return big[pl.ds(pl.multiple_of(n * rows, rows), rows),
                   pl.ds(pl.multiple_of(lax.rem(first, W), 128), size)]

    def from_ref(array):
        return lambda first, size: array[:, pl.ds(first, size)]

    def vector(row):
        return vec[row : row + 1, :]

    def note(row, value):
        small[0, 0, row : row + 1, :] += value

    small[0, 0] = jnp.zeros_like(small[0, 0])
    plain["cot"].wait()
    TR = min(128, rows)

    def feed_tile(t, _):
        tile = pl.ds(pl.multiple_of(t * TR, TR), TR)
        value = (cot[tile, :].astype(F32) * vector(LIVE) * vector(MLP_SCALE)).astype(BF)
        gfeed[tile, :] = value
        note(DOWN_B, jnp.sum(value.astype(F32), axis=0, keepdims=True))
        return 0

    lax.fori_loop(0, rows // TR, feed_tile, 0)
    for copy in act_loads:
        copy.wait()
    plain["slope"].wait()
    acc, gmid = ref["acc"], ref["gmid"]
    acc[...] = jnp.zeros_like(acc)
    gmid[...] = jnp.zeros_like(gmid)

    def down_step(i, _):
        slot = lax.rem(i, 2)
        produce(i, down_rows, act_cols, i, gfeed[...])
        tick(i)
        down_load(i).wait()
        up_load(i).wait()

        @pl.when(i + 1 < n_down)
        def _():
            down_load(i + 1).start()
            up_load(i + 1).start()

        cols = pl.ds(pl.multiple_of(i * FB, FB), FB)
        weight = ref["wd"][slot]
        grad = matmul(gfeed[...], weight, ((1,), (1,)))
        pre = (grad * slope[:, cols].astype(F32)).astype(BF)
        slope[:, cols] = pre
        row = UP_B + lax.div(i * FB, W)
        at = pl.ds(pl.multiple_of(lax.rem(i * FB, W), FB), FB)
        small[0, 0, pl.ds(row, 1), at] = jnp.sum(pre.astype(F32), axis=0, keepdims=True)
        acc[...] += matmul(act_cols(i * FB, FB), weight)
        gmid[...] += matmul(pre, ref["wu"][slot], ((1,), (1,)))
        return 0

    lax.fori_loop(0, n_down, down_step, 0)

    key_load.start()
    value_load.start()
    for name in ("x", "branch", "proj", "second", "attended", "query", "first"):
        plain[name].wait()
    x_s, branch, gbranch, gatt = ref["x_s"], ref["branch_s"], ref["gbranch"], ref["gatt"]
    tok_out, tok_send = ref["tok_out"], ref["tok_send"]

    def middle_tile(t, _):
        tile = pl.ds(pl.multiple_of(t * TR, TR), TR)
        low = branch[tile, :]
        middle = x_s[tile, :].astype(F32) + vector(ATTN_SCALE) * low
        feed = acc[tile, :] + vector(DOWN_B)
        result = ((middle + vector(MLP_SCALE) * feed) * vector(LIVE)).astype(BF)
        lower = pl.ds(pl.multiple_of(lax.rem(t * TR, R), TR), TR) if R >= TR else pl.ds(0, R)
        if R >= TR:
            @pl.when(t * TR < R)
            def _():
                tok_out[mine, lower, :] = result

            @pl.when(t * TR >= R)
            def _():
                tok_send[lower, :] = result
        else:
            tok_out[mine] = result[:R]
            tok_send[...] = result[R:]
        upstream = cot[tile, :].astype(F32) * vector(LIVE)
        note(MLP_SCALE, jnp.sum(upstream * feed, axis=0, keepdims=True))
        unit, scale = norm_parts(middle)
        grad = gmid[tile, :]
        note(MLP_GAIN, jnp.sum(grad * unit, axis=0, keepdims=True))
        note(MLP_SHIFT, jnp.sum(grad, axis=0, keepdims=True))
        grad = upstream + norm_back(grad, unit, scale, vector(MLP_GAIN))
        gmid[tile, :] = grad
        note(ATTN_SCALE, jnp.sum(grad * low, axis=0, keepdims=True))
        grad = (grad * vector(ATTN_SCALE)).astype(BF)
        gbranch[tile, :] = grad
        note(PROJ_B, jnp.sum(grad.astype(F32), axis=0, keepdims=True))
        gatt[tile, :] = matmul(grad, ref["proj_s"][...], ((1,), (1,))).astype(BF)
        return 0

    lax.fori_loop(0, rows // TR, middle_tile, 0)
    tok_copy = send(tok_send, tok_out.at[mine], ref["ts"].at[0], ref["tr"].at[0], swap_peer)
    tok_copy.start()
    key_load.wait()
    value_load.wait()

    G, query = ref["G"], ref["query_s"]
    pown, psend, precv = ref["pown"], ref["psend"], ref["precv"]
    gk_acc, gv_acc = ref["gk_acc"], ref["gv_acc"]
    pairs = W // 128
    QT = min(256, rows)

    def pair_copy(p, k):
        a = lax.rem(p, SLOTS)
        return send(psend.at[a, k - 1], precv.at[a, k - 1], ref["ps"].at[a, k - 1], ref["pr"].at[a, k - 1],
                    half_peer(k))

    def pair_done(p):
        a = lax.rem(p, SLOTS)
        for k in range(1, half):
            pair_copy(p, k).wait()
        for which in range(2):
            whole = pown[a, which]
            for k in range(1, half):
                whole = whole + precv[a, k - 1, which].astype(F32)
            cols = pl.ds(pl.multiple_of((which + 1) * W + p * 128, 128), 128)
            G[:, cols] = whole.astype(BF)

    def pair_step(p):
        lane = lax.broadcasted_iota(jnp.int32, (1, 128), 1)
        cols = pl.ds(pl.multiple_of(p * 128, 128), 128)
        key = big[pl.ds(0, keys), cols]
        value = big[pl.ds(keys, keys), cols]
        key_t = key.T
        for t in range(rows // QT):
            tile = slice(t * QT, (t + 1) * QT)
            q_tile, g_tile = query[tile, cols], gatt[tile, cols]
            parts = []
            for head in range(2):
                owned = (lane < HEAD_DIM) if head == 0 else (lane >= HEAD_DIM)
                own = jnp.where(owned, q_tile * BF(HEAD_DIM**-0.5), BF(0))
                own_grad = jnp.where(owned, g_tile, BF(0))
                probs = jnp.exp(matmul(key, own, ((1,), (1,))) - lse[p, head : head + 1, tile])
                grad_probs = matmul(value, own_grad, ((1,), (1,)))
                centre = jnp.sum(grad_probs * probs, axis=0, keepdims=True)
                grad_scores = (probs * (grad_probs - centre)).astype(BF)
                gv = matmul(probs.astype(BF), own_grad)
                gk = matmul(grad_scores, own)
                if t == 0 and head == 0:
                    gv_acc[...], gk_acc[...] = gv, gk
                else:
                    gv_acc[...] += gv
                    gk_acc[...] += gk
                lanes = slice(head * HEAD_DIM, (head + 1) * HEAD_DIM)
                parts.append(matmul(key_t[lanes, :], grad_scores))
            whole = jnp.concatenate(parts, axis=0) * (HEAD_DIM**-0.5)
            G[tile, cols] = whole.T.astype(BF)
        a = lax.rem(p, SLOTS)
        pown[a, 0], pown[a, 1] = gk_acc[:rows], gv_acc[:rows]
        for k in range(1, half):
            psend[a, k - 1, 0] = gk_acc[k * rows : (k + 1) * rows].astype(BF)
            psend[a, k - 1, 1] = gv_acc[k * rows : (k + 1) * rows].astype(BF)
            pair_copy(p, k).start()

    per_tick = pairs // n_up

    def up_step(u, _):
        i = n_down + u
        b, n = lax.rem(u, blocks), lax.div(u, blocks)
        produce(i, other_rows, from_ref(ref["second_s"]), b,
                slope[:, pl.ds(pl.multiple_of(n * W, W), W)])
        tick(i)
        for m in range(per_tick):
            p = u * per_tick + m
            pair_step(p)

            @pl.when(p >= 1)
            def _():
                pair_done(p - 1)
        return 0

    lax.fori_loop(0, n_up, up_step, 0)

    qkv_load(0).start()

    def proj_step(u, _):
        i = n_down + n_up + u
        produce(i, other_rows, from_ref(ref["attended_s"]), u, gbranch[...])
        tick(i)

        @pl.when(u == 0)
        def _():
            pair_done(pairs - 1)
        return 0

    lax.fori_loop(0, n_proj, proj_step, 0)
    acc[...] = jnp.zeros_like(acc)

    def qkv_step(u, _):
        i = n_down + n_up + n_proj + u
        b, n = lax.rem(u, blocks), lax.div(u, blocks)
        produce(i, other_rows, from_ref(ref["first_s"]), b, G[:, pl.ds(pl.multiple_of(n * W, W), W)])
        tick(i)
        qkv_load(u).wait()

        @pl.when(u + 1 < n_qkv)
        def _():
            qkv_load(u + 1).start()

        acc[...] += matmul(G[:, pl.ds(pl.multiple_of(u * FB, FB), FB)], ref["wu"][lax.rem(u, 2)],
                           ((1,), (1,)))
        return 0

    lax.fori_loop(0, n_qkv, qkv_step, 0)

    gt_out, gt_send, gt_recv = ref["gt_out"], ref["gt_send"], ref["gt_recv"]

    def first_tile(t, _):
        tile = pl.ds(pl.multiple_of(t * TR, TR), TR)
        unit, scale = norm_parts(x_s[tile, :].astype(F32))
        grad = acc[tile, :]
        note(ATTN_GAIN, jnp.sum(grad * unit, axis=0, keepdims=True))
        note(ATTN_SHIFT, jnp.sum(grad, axis=0, keepdims=True))
        note(QV, jnp.sum(G[tile, :W].astype(F32), axis=0, keepdims=True))
        note(QV + 1, jnp.sum(G[tile, 2 * W :].astype(F32), axis=0, keepdims=True))
        whole = gmid[tile, :] + norm_back(grad, unit, scale, vector(ATTN_GAIN))
        if R >= TR:
            lower = pl.ds(pl.multiple_of(lax.rem(t * TR, R), TR), TR)

            @pl.when(t * TR < R)
            def _():
                gt_out[mine, lower, :] = whole

            @pl.when(t * TR >= R)
            def _():
                gt_send[lower, :] = whole.astype(BF)
        else:
            gt_out[mine] = whole[:R]
            gt_send[...] = whole[R:].astype(BF)
        return 0

    lax.fori_loop(0, rows // TR, first_tile, 0)

    small_steps = [
        [place.at(c=1 - place.c)],
        [place.at(y=place.ahead_y(k)) for k in range(1, Y)],
        [place.at(x=1 - place.x)],
        [place.at(z=place.ahead_z(k)) for k in range(1, Z)],
    ]

    def small_send(step):
        return [
            send(small.at[step, 0], small.at[step, k + 1], ref["ss"].at[step, k], ref["sr"].at[step, k], device)
            for k, device in enumerate(small_steps[step])
        ]

    for copy in small_send(0):
        copy.start()
    gt_copy = send(gt_send, gt_recv, ref["ts"].at[1], ref["tr"].at[1], swap_peer)
    for lag in range(6):
        tick(total + lag)
        if lag == 0:
            gt_copy.start()
        if lag < 4:
            for copy in small_send(lag):
                copy.wait()
            whole = small[lag, 0]
            for k in range(len(small_steps[lag])):
                whole = whole + small[lag, k + 1]
            if lag < 3:
                small[lag + 1, 0] = whole
                for copy in small_send(lag + 1):
                    copy.start()
            else:
                ref["small_out"][...] = whole
    tok_copy.wait()
    gt_copy.wait()
    gt_out[1 - mine] = gt_recv[...].astype(F32)


def backward(replicas, shards, hbm, vec, lse):
    Y, Z, half = shards // 2, replicas // 2, shards // 2
    W = hbm["cot"].shape[1]
    rows, FF = hbm["act"].shape
    R, keys = rows // 2, hbm["key"].shape[0]
    CB = min(128, W // shards)
    HB, WZ = CB // 2, W // Z
    counts = (FF // shards // CB, (W // shards // CB) * (FF // W), W // shards // CB, 3 * (W // shards // CB))
    total = sum(counts)
    FB = FF // counts[0]
    peers = max(Y, Z, 2)
    dma = pltpu.SemaphoreType.DMA
    vmem, anywhere = pl.BlockSpec(memory_space=pltpu.VMEM), pl.BlockSpec(memory_space=pl.ANY)
    scratch = {
        "part": pltpu.VMEM((2, 2, Y, CB, W), BF),
        "crecv": pltpu.VMEM((SLOTS, Y, CB, W), BF),
        "ysum": pltpu.VMEM((SLOTS, Y, CB, W), BF),
        "yrecv": pltpu.VMEM((SLOTS, Y - 1, CB, W), BF),
        "xsum": pltpu.VMEM((SLOTS, 2, HB, W), BF),
        "xrecv": pltpu.VMEM((SLOTS, HB, W), BF),
        "zsum": pltpu.VMEM((SLOTS, Z, HB, WZ), BF),
        "zrecv": pltpu.VMEM((SLOTS, Z - 1, HB, WZ), BF),
        "small_buf": pltpu.VMEM((4, peers, 16, W), F32),
        "big": pltpu.VMEM((max(rows * FF // W, 2 * keys), W), BF),
        "slope_s": pltpu.VMEM((rows, FF), BF),
        "cot_s": pltpu.VMEM((rows, W), BF),
        "gfeed": pltpu.VMEM((rows, W), BF),
        "x_s": pltpu.VMEM((rows, W), BF),
        "branch_s": pltpu.VMEM((rows, W), F32),
        "second_s": pltpu.VMEM((rows, W), BF),
        "attended_s": pltpu.VMEM((rows, W), BF),
        "query_s": pltpu.VMEM((rows, W), BF),
        "first_s": pltpu.VMEM((rows, W), BF),
        "proj_s": pltpu.VMEM((W, W), BF),
        "wd": pltpu.VMEM((2, FB, W), BF),
        "wu": pltpu.VMEM((2, W, FB), BF),
        "acc": pltpu.VMEM((rows, W), F32),
        "gmid": pltpu.VMEM((rows, W), F32),
        "gbranch": pltpu.VMEM((rows, W), BF),
        "gatt": pltpu.VMEM((rows, W), BF),
        "G": pltpu.VMEM((rows, 3 * W), BF),
        "pown": pltpu.VMEM((SLOTS, 2, rows, 128), F32),
        "psend": pltpu.VMEM((SLOTS, half - 1, 2, rows, 128), BF),
        "precv": pltpu.VMEM((SLOTS, half - 1, 2, rows, 128), BF),
        "gk_acc": pltpu.VMEM((keys, 128), F32),
        "gv_acc": pltpu.VMEM((keys, 128), F32),
        "tok_send": pltpu.VMEM((R, W), BF),
        "gt_send": pltpu.VMEM((R, W), BF),
        "gt_recv": pltpu.VMEM((R, W), BF),
        "lsem": dma((24,)), "wsem": dma((3, 2)),
        "cs": dma((SLOTS,)), "cr": dma((SLOTS,)),
        "ys": dma((SLOTS, Y - 1)), "yr": dma((SLOTS, Y - 1)),
        "xs": dma((SLOTS,)), "xr": dma((SLOTS,)),
        "zs": dma((SLOTS, Z - 1)), "zr": dma((SLOTS, Z - 1)),
        "gs": dma((SLOTS, Z - 1)), "gr": dma((SLOTS, Z - 1)),
        "hs": dma((SLOTS,)), "hr": dma((SLOTS,)),
        "ps": dma((SLOTS, half - 1)), "pr": dma((SLOTS, half - 1)),
        "ss": dma((4, peers - 1)), "sr": dma((4, peers - 1)),
        "ts": dma((2,)), "tr": dma((2,)),
    }
    if CB % 128:
        scratch["tile"] = pltpu.VMEM((128, W), F32)
    outs = {
        "out": jax.ShapeDtypeStruct((total, CB, W), BF),
        "small_out": jax.ShapeDtypeStruct((16, W), F32),
        "tok_out": jax.ShapeDtypeStruct((2, R, W), BF),
        "gt_out": jax.ShapeDtypeStruct((2, R, W), F32),
    }
    names = HBM_INPUTS + ("vec", "lse") + tuple(outs) + tuple(scratch)
    out, small_out, tok_out, gt_out = pl.pallas_call(
        functools.partial(backward_kernel, replicas, shards, names),
        in_specs=[anywhere] * len(HBM_INPUTS) + [vmem, vmem],
        out_specs=[vmem] * len(outs),
        out_shape=list(outs.values()),
        scratch_shapes=list(scratch.values()),
        compiler_params=pltpu.CompilerParams(
            collective_id=1, has_side_effects=True, vmem_limit_bytes=63 * MIB
        ),
    )(*[hbm[name] for name in HBM_INPUTS], vec, lse)
    grads, base = [], 0
    for chunks, n_cols in zip(counts, (1, FF // W, 1, 3)):
        block = out[base : base + chunks].reshape(n_cols, -1, W).swapaxes(0, 1)
        grads.append(block.reshape(-1, n_cols * W).astype(F32))
        base += chunks
    return grads, small_out, tok_out, gt_out


def on_device(replicas, shards, tokens, qkv_weight, qv_bias, proj_weight, proj_bias, up_weight, up_bias,
              down_weight, down_bias, attn_gain, attn_shift, mlp_gain, mlp_shift, attn_scale, mlp_scale,
              cotangent, image_count):
    vectors = (qv_bias, proj_bias, up_bias, down_bias, attn_gain, attn_shift, mlp_gain, mlp_shift,
               attn_scale, mlp_scale)
    width = tokens.shape[2]
    piece = width // shards
    multiples = tuple(v.shape[0] // piece for v in vectors)
    packed = jnp.pad(jnp.concatenate(vectors).reshape(-1, piece), ((0, 16 - sum(multiples)), (0, 0)))
    shard = lax.axis_index("shard")
    live = lax.div(shard, shards // 2) < image_count[lax.axis_index("replica")]
    live = jnp.broadcast_to(live.astype(F32), (8, width))
    shards_of = dict(qkv=qkv_weight, proj=proj_weight, up=up_weight, down=down_weight)
    kept = forward(replicas, shards, tokens, cotangent, shards_of, packed, live, multiples)
    hbm = {name: kept[name] for name in HBM_INPUTS}
    grads, small, output, grad_tokens = backward(replicas, shards, hbm, kept["vec"], kept["lse"])
    grad_down, grad_up, grad_proj, grad_qkv = grads

    def own(row, count=1):
        whole = small[row : row + count].reshape(-1)
        size = whole.shape[0] // shards
        return lax.dynamic_slice_in_dim(whole, shard * size, size)

    return (output, grad_tokens, grad_qkv, own(QV, 2), grad_proj, own(PROJ_B), grad_up,
            own(UP_B, DOWN_B - UP_B), grad_down, own(DOWN_B), own(ATTN_GAIN), own(ATTN_SHIFT), own(MLP_GAIN),
            own(MLP_SHIFT), own(ATTN_SCALE), own(MLP_SCALE))


def solution(mesh):
    rows, vector = P("shard", None), P("shard")
    image = P("replica", "shard", None)
    in_specs = (image, rows, vector, rows, vector, rows, vector, rows, vector, vector, vector, vector,
                vector, vector, vector, image, P())
    out_specs = (image, image, rows, vector, rows, vector, rows, vector, rows, vector, vector, vector,
                 vector, vector, vector, vector)
    return jax.shard_map(
        functools.partial(on_device, mesh.shape["replica"], mesh.shape["shard"]),
        mesh=mesh, in_specs=in_specs, out_specs=out_specs, check_vma=False,
    )
```

```python
import functools
import types

import jax
import jax.numpy as jnp
from jax import lax
from jax.experimental import pallas as pl
from jax.experimental.pallas import tpu as pltpu
from jax.sharding import PartitionSpec as P

HEAD_DIM = 64
EPS = 1e-06
BF = jnp.bfloat16
F32 = jnp.float32
MESH = pl.DeviceIdType.MESH
MIB = 1024 * 1024
SLOTS = 6
PAIR_SLOTS = 4
CORE_SLOTS = 4
LAG = 2
GLAG = 2


def matmul(left, right, dims=((1,), (0,))):
    return lax.dot_general(left, right, (dims, ((), ())), preferred_element_type=F32)


class Place:
    def __init__(self, replicas, shards):
        self.Z, self.Y = replicas // 2, shards // 2
        self.shards = shards
        replica, shard = lax.axis_index("replica"), lax.axis_index("shard")
        self.x, self.z = lax.rem(replica, 2), lax.div(replica, 2)
        self.c, self.y = lax.rem(shard, 2), lax.div(shard, 2)
        self.s = shard

    def part(self, y, c):
        return y * 2 + c

    def at(self, x=None, z=None, y=None, c=None):
        x = self.x if x is None else x
        z = self.z if z is None else z
        y = self.y if y is None else y
        c = self.c if c is None else c
        return (z * 2 + x, y * 2 + c)

    def ahead_z(self, k):
        return lax.rem(self.z + k, self.Z)

    def behind_z(self, k):
        return lax.rem(self.z + self.Z - k, self.Z)

    def ahead_y(self, k):
        return lax.rem(self.y + k, self.Y)

    def behind_y(self, k):
        return lax.rem(self.y + self.Y - k, self.Y)

    def greet(self, extra=()):
        others = [self.at(c=1 - self.c), self.at(x=1 - self.x)]
        others += [self.at(y=self.ahead_y(k)) for k in range(1, self.Y)]
        others += [self.at(z=self.ahead_z(k)) for k in range(1, self.Z)]
        others += list(extra)
        barrier = pltpu.get_barrier_semaphore()
        for other in others:
            pl.semaphore_signal(barrier, inc=1, device_id=other, device_id_type=MESH)
        pl.semaphore_wait(barrier, len(others))


def send(src, dst, send_sem, recv_sem, device):
    return pltpu.make_async_remote_copy(
        src_ref=src,
        dst_ref=dst,
        send_sem=send_sem,
        recv_sem=recv_sem,
        device_id=device,
        device_id_type=MESH,
    )


QV, PROJ_B, UP_B, DOWN_B, ATTN_GAIN, ATTN_SHIFT, MLP_GAIN, MLP_SHIFT, ATTN_SCALE, MLP_SCALE, LIVE = (
    0, 2, 3, 7, 8, 9, 10, 11, 12, 13, 14)
QKV, PROJ, UP, DOWN = range(4)


def norm_parts(values):
    centre = values - jnp.mean(values, axis=-1, keepdims=True)
    scale = lax.rsqrt(jnp.mean(centre * centre, axis=-1, keepdims=True) + EPS)
    return centre * scale, scale


def norm_back(grad, unit, scale, gain):
    inner = grad * gain
    return scale * (
        inner
        - jnp.mean(inner, axis=-1, keepdims=True)
        - unit * jnp.mean(inner * unit, axis=-1, keepdims=True)
    )


BW = 128


def gather_items(replicas, shards, width, hidden):
    Z = replicas // 2
    step = max(512, 128 * Z)
    size, down = width // shards, hidden // shards
    staged = [(QKV, 0, size, (1 + n) * width + h * step, step) for h in range(width // step) for n in range(2)]
    direct = [(QKV, 0, size, h * step, step) for h in range(width // step)]
    staged += [(PROJ, 0, size, h * step, step) for h in range(width // step)]
    need, known = [], set()
    for b in range(down // BW):
        for p in range(shards):
            c = (p * down + b * BW) // step
            if c not in known:
                known.add(c)
                staged.append((UP, 0, size, c * step, step))
        staged.append((DOWN, b * BW, BW, 0, width))
        need.append(len(staged))
    return staged, direct, need


def layer_kernel(replicas, shards, multiples, names, *refs):
    vector_refs, refs = refs[: len(multiples)], refs[len(multiples) :]
    ref = types.SimpleNamespace(**dict(zip(names, refs)))
    place = Place(replicas, shards)
    Y, Z, s = place.Y, place.Z, place.s
    half = shards // 2
    part, crecv, ysum, yrecv = ref.part, ref.crecv, ref.ysum, ref.yrecv
    xsum, xrecv, zsum, zrecv = ref.xsum, ref.xrecv, ref.zsum, ref.zrecv
    out, small, vec, lse = ref.out, ref.small_buf, ref.vec, ref.lse
    CB, CW = part.shape[3], part.shape[4]
    rows, W = ref.gfeed.shape
    R = rows // 2
    keys = half * rows
    FF = ref.gpre.shape[1]
    down_rows, other_rows = FF // shards, W // shards
    n_blocks, blocks = down_rows // BW, other_rows // CB
    per_block = (BW // CB) * (W // CW)
    n_down, n_up = n_blocks * per_block, blocks * (FF // CW)
    n_proj, n_qkv = blocks * (W // CW), blocks * (3 * W // CW)
    total = n_down + n_up + n_proj + n_qkv
    mine = lax.div(s, half)
    j_half = lax.rem(s, half)
    replica = lax.axis_index("replica")
    kv, gpre, cot, gfeed, G = ref.kv, ref.gpre, ref.cot_s, ref.gfeed, ref.G
    second, first, query, x_s = ref.second_s, ref.first_s, ref.query_s, ref.x_s
    attended, branch, gbranch, gatt = ref.attended_s, ref.branch_s, ref.gbranch, ref.gatt
    TR, MT, QT = min(128, R), min(256, rows), min(256, rows)
    pairs, tiles = W // 128, rows // QT

    def half_peer(k):
        return (replica, mine * half + lax.rem(j_half + k, half))

    swap_peer = (replica, lax.rem(s + half, shards))

    def load(src, dst, sem):
        return pltpu.make_async_copy(src, dst, sem)

    sources = (ref.qkv, ref.proj, ref.up, ref.down)
    weights = (ref.g_qkv, ref.g_proj, ref.g_up, ref.g_down)
    sizes = [source.shape[0] for source in sources]
    bounce = (G, gbranch, gpre, ref.proj_s)

    def own_rows(w):
        return weights[w].at[pl.ds(pl.multiple_of(s * sizes[w], sizes[w]), sizes[w])]

    own_loads = [load(sources[w], bounce[w].at[pl.ds(0, sizes[w])], ref.lsem.at[w]) for w in range(4)]
    own_stores = [load(bounce[w].at[pl.ds(0, sizes[w])], own_rows(w), ref.lsem.at[4 + w]) for w in range(4)]
    x_load = load(ref.tokens.at[mine], x_s.at[pl.ds(0, R)], ref.lsem.at[8])
    cot_load = load(ref.cotangent.at[mine], cot.at[pl.ds(0, R)], ref.lsem.at[9])
    x_load.start()
    for copy in own_loads:
        copy.start()
    cot_load.start()
    row = 0
    for vector_ref, count in zip(vector_refs, multiples):
        values = vector_ref[...].astype(F32).reshape(count, ref.small_s.shape[2])
        ref.small_s[s, row : row + count, :] = values
        row += count
    place.greet([(replica, lax.rem(s + k, shards)) for k in range(1, shards)])

    staged, direct, need = gather_items(replicas, shards, W, FF)
    items = staged + direct
    n_staged = len(staged)

    def piece(m, owner, whole_rows, whole_cols):
        w, row, size, col, width = items[m]
        at = owner * sizes[w] + row
        if not whole_rows:
            at, size = at + place.x * (size // 2), size // 2
        at = pl.ds(pl.multiple_of(at, 16), size)
        if whole_cols:
            return at, pl.ds(col, width)
        return at, pl.ds(pl.multiple_of(col + place.z * (width // Z), 128), width // Z)

    def gy_copy(m, k):
        w, whole = items[m][0], m >= n_staged
        return send(sources[w].at[piece(m, 0, whole, whole)], weights[w].at[piece(m, s, whole, whole)],
                    ref.gys.at[m, k - 1], ref.gyr.at[m, k - 1], place.at(y=place.ahead_y(k)))

    def gathered(m, k, whole_rows, whole_cols):
        owner = place.part(place.behind_y(k), place.c)
        return weights[items[m][0]].at[piece(m, owner, whole_rows, whole_cols)]

    def gz_copy(m, k, j):
        b = gathered(m, k, False, False)
        return send(b, b, ref.gzs.at[m, k - 1, j - 1], ref.gzr.at[m, k - 1, j - 1],
                    place.at(z=place.ahead_z(j)))

    def gx_copy(m, k):
        b = gathered(m, k, False, True)
        return send(b, b, ref.gxs.at[m, k - 1], ref.gxr.at[m, k - 1], place.at(x=1 - place.x))

    def gc_copy(m, k):
        b = gathered(m, k, True, True)
        return send(b, b, ref.gcs.at[m, k - 1], ref.gcr.at[m, k - 1], place.at(c=1 - place.c))

    def gy_start(m):
        for k in range(1, Y):
            gy_copy(m, k).start()

    def direct_arrived(h):
        for k in range(1, Y):
            gy_copy(n_staged + h, k).wait()
            gc_copy(n_staged + h, k).start()

    def arrived(m):
        for k in range(1, Y):
            gc_copy(m, k).wait()

    early = 2 * (W // CW)
    ahead = early + 2

    def gather_tick(t):
        if early <= t + ahead < n_staged:
            gy_start(t + ahead)
        if t < n_staged:
            for k in range(1, Y):
                gy_copy(t, k).wait()
                for j in range(1, Z):
                    gz_copy(t, k, j).start()
        m = t - GLAG
        if 0 <= m < n_staged:
            for k in range(1, Y):
                for j in range(1, Z):
                    gz_copy(m, k, j).wait()
                gx_copy(m, k).start()
        m = t - 2 * GLAG
        if 0 <= m < n_staged:
            for k in range(1, Y):
                gx_copy(m, k).wait()
                gc_copy(m, k).start()
        m = t - 3 * GLAG
        if 0 <= m < n_staged:
            arrived(m)

    ticked = [0]

    def gather_until(t):
        while ticked[0] < min(t + 3 * GLAG, n_staged + 3 * GLAG):
            gather_tick(ticked[0])
            ticked[0] += 1

    def gather_ticks(count):
        gather_until(ticked[0] + count - 3 * GLAG)

    x_swap = send(ref.tokens.at[1 - mine], x_s.at[pl.ds(R, R)], ref.ts.at[2], ref.tr.at[2], swap_peer)
    cot_swap = send(ref.cotangent.at[1 - mine], cot.at[pl.ds(R, R)], ref.ts.at[3], ref.tr.at[3], swap_peer)
    small_sends = [
        send(ref.small_s.at[s], ref.small_s.at[s], ref.vs.at[k - 1], ref.vr.at[k - 1],
             (replica, lax.rem(s + k, shards)))
        for k in range(1, shards)
    ]
    own_sends = [send(sources[w], own_rows(w), ref.os.at[w], ref.orr.at[w], place.at(c=1 - place.c))
                 for w in range(4)]
    for copy in small_sends:
        copy.start()
    for m in range(early):
        gy_start(m)
    x_swap.start()
    for h in range(W // CW):
        gy_start(n_staged + h)
    for m in range(early, early + 2):
        gy_start(m)
    for copy in own_sends:
        copy.start()

    for copy in small_sends:
        copy.wait()
    vec[...] = jnp.zeros_like(vec)
    row = 0
    for count in multiples:
        pieces = [ref.small_s[p, row + r : row + r + 1, :] for p in range(shards) for r in range(count)]
        for r in range(count):
            vec[row + r : row + r + 1, :] = jnp.concatenate(pieces[r * shards : (r + 1) * shards], axis=1)
        row += count
    live = (mine < ref.count[replica]).astype(F32)
    vec[LIVE : LIVE + 1, :] = jnp.full((1, W), live, F32)

    def vector(row):
        return vec[row : row + 1, :]

    def note(row, value):
        small[0, 0, row : row + 1, :] += value

    def norm_tile(t, _):
        tile = pl.ds(pl.multiple_of(t * TR, TR), TR)
        unit, _ = norm_parts(x_s[tile, :].astype(F32))
        first[tile, :] = (unit * vector(ATTN_GAIN) + vector(ATTN_SHIFT)).astype(BF)
        return 0

    x_load.wait()
    lax.fori_loop(0, R // TR, norm_tile, 0)
    for w in range(4):
        own_loads[w].wait()
        own_stores[w].start()
    gather_ticks(2)
    x_swap.wait()
    cot_swap.start()
    lax.fori_loop(R // TR, rows // TR, norm_tile, 0)
    gather_ticks(2)
    direct_arrived(0)
    gather_until(2)
    for w in (QKV, DOWN):
        own_stores[w].wait()
    own_sends[QKV].wait()

    def kv_copy(which, h, k):
        cols = pl.ds(h * CW, CW)
        return send(kv.at[which, pl.ds(0, rows), cols], kv.at[which, pl.ds((half - k) * rows, rows), cols],
                    ref.ks.at[which, h, k - 1], ref.kr.at[which, h, k - 1], half_peer(k))

    def qkv_tile(n, h, slot):
        return load(ref.g_qkv.at[:, pl.ds(n * W + h * CW, CW)], ref.wu.at[slot, :, pl.ds(0, CW)],
                    ref.qsem.at[slot])

    def project(h):
        here = slice(h * CW, (h + 1) * CW)
        tile_loads = [qkv_tile(1, h, 0), qkv_tile(2, h, 1), qkv_tile(0, h, 0)]
        tile_loads[0].start()
        tile_loads[1].start()
        for n in range(3):
            tile_loads[n].wait()
            for t in range(rows // MT):
                tile = slice(t * MT, (t + 1) * MT)
                value = matmul(first[tile, :], ref.wu[n % 2, :, :CW])
                if n == 0:
                    kv[0, tile, here] = value.astype(BF)
                elif n == 1:
                    kv[1, tile, here] = (value + vector(QV + 1)[:, here]).astype(BF)
                else:
                    query[tile, here] = (value + vector(QV)[:, here]).astype(BF)
            if n < 2:
                for k in range(1, half):
                    kv_copy(n, h, k).start()
            if n == 0:
                tile_loads[2].start()

    def exchanged(h):
        for which in range(2):
            for k in range(1, half):
                kv_copy(which, h, k).wait()

    for k in range(1, Y):
        gc_copy(n_staged, k).wait()
    project(0)

    halves = W // CW
    plan = {}

    def at_pair(p, act):
        plan.setdefault(p, []).append(act)

    if halves > 1:
        def second_half():
            direct_arrived(1)
            gather_until(early)
            arrived(n_staged + 1)
            project(1)

        at_pair(2, second_half)
        at_pair(4, lambda: exchanged(1))
    stop = 2 * halves + halves + 2
    at_pair(5, lambda: gather_until(early + 1))
    at_pair(6, lambda: gather_until(early + 2))
    at_pair(7, lambda: gather_until(stop))
    exchanged(0)

    def attend(p, _):
        for at in sorted(plan):
            @pl.when(p == at)
            def _(at=at):
                for act in plan[at]:
                    act()

        lane = lax.broadcasted_iota(jnp.int32, (1, 128), 1)
        cols = pl.ds(pl.multiple_of(p * 128, 128), 128)
        key, value_t = kv[0, :, cols], kv[1, :, cols].T
        for t in range(tiles):
            tile = slice(t * QT, (t + 1) * QT)
            q_tile = query[tile, cols] * BF(HEAD_DIM**-0.5)
            parts = []
            for head in range(2):
                owned = (lane < HEAD_DIM) if head == 0 else (lane >= HEAD_DIM)
                scores = matmul(key, jnp.where(owned, q_tile, BF(0)), ((1,), (1,)))
                highest = jnp.max(scores, axis=0, keepdims=True)
                expos = jnp.exp(scores - highest)
                denom = jnp.sum(expos, axis=0, keepdims=True)
                probs = (expos * (1.0 / denom)).astype(BF)
                lse[p, head : head + 1, tile] = highest + jnp.log(denom)
                lanes = slice(head * HEAD_DIM, (head + 1) * HEAD_DIM)
                parts.append(matmul(value_t[lanes, :], probs))
            attended[tile, cols] = jnp.concatenate(parts, axis=0).T.astype(BF)
        return 0

    lax.fori_loop(0, pairs, attend, 0)

    gather_until(3 * halves)
    own_stores[PROJ].wait()
    own_sends[PROJ].wait()
    proj_load = load(ref.g_proj, ref.proj_s, ref.lsem.at[10])
    proj_load.start()
    cot_load.wait()
    cot_swap.wait()
    small[0, 0] = jnp.zeros_like(small[0, 0])

    def feed_tile(t, _):
        tile = pl.ds(pl.multiple_of(t * TR, TR), TR)
        value = (cot[tile, :].astype(F32) * vector(LIVE) * vector(MLP_SCALE)).astype(BF)
        gfeed[tile, :] = value
        note(DOWN_B, jnp.sum(value.astype(F32), axis=0, keepdims=True))
        return 0

    lax.fori_loop(0, rows // TR, feed_tile, 0)
    proj_load.wait()

    def branch_tile(t, _):
        tile = pl.ds(pl.multiple_of(t * MT, MT), MT)
        low = matmul(attended[tile, :], ref.proj_s[...]) + vector(PROJ_B)
        branch[tile, :] = low
        unit, _ = norm_parts(x_s[tile, :].astype(F32) + vector(ATTN_SCALE) * low)
        second[tile, :] = (unit * vector(MLP_GAIN) + vector(MLP_SHIFT)).astype(BF)
        return 0

    lax.fori_loop(0, rows // MT, branch_tile, 0)
    for w in (UP, DOWN):
        own_sends[w].wait()
    own_stores[UP].wait()

    def block_loads(b):
        slot = lax.rem(b, 2)
        copies = []
        for p in range(shards):
            at = pl.ds(pl.multiple_of(p * down_rows + b * BW, BW), BW)
            to = pl.ds(p * BW, BW)
            copies.append(load(ref.g_up.at[:, at], ref.wu.at[slot, :, to], ref.wsem.at[0, slot, p]))
            copies.append(load(ref.g_down.at[at], ref.wd.at[slot, to], ref.wsem.at[1, slot, p]))
        return copies

    gather_until(need[0])
    for copy in block_loads(0):
        copy.start()

    def core_copy(i):
        a = lax.rem(i, CORE_SLOTS)
        return send(part.at[lax.rem(i, 2), 1 - place.c], crecv.at[a], ref.cs.at[a], ref.cr.at[a],
                    place.at(c=1 - place.c))

    def y_copy(i, k):
        a = lax.rem(i, SLOTS)
        return send(ysum.at[a, place.ahead_y(k)], yrecv.at[a, k - 1], ref.ys.at[a, k - 1],
                    ref.yr.at[a, k - 1], place.at(y=place.ahead_y(k)))

    def x_copy(i):
        a = lax.rem(i, SLOTS)
        return send(xsum.at[a, 1 - place.x], xrecv.at[a], ref.xs.at[a], ref.xr.at[a],
                    place.at(x=1 - place.x))

    def z_copy(i, k):
        a = lax.rem(i, SLOTS)
        return send(zsum.at[a, place.ahead_z(k)], zrecv.at[a, k - 1], ref.zs.at[a, k - 1],
                    ref.zr.at[a, k - 1], place.at(z=place.ahead_z(k)))

    HB, WZ = CB // 2, CW // Z
    x_rows = pl.ds(pl.multiple_of(place.x * HB, HB), HB)
    z_cols = pl.ds(pl.multiple_of(place.z * WZ, WZ), WZ)

    def zg_copy(i, k):
        a = lax.rem(i, SLOTS)
        block = out.at[i, x_rows, z_cols]
        return send(block, block, ref.gs.at[a, k - 1], ref.gr.at[a, k - 1],
                    place.at(z=place.ahead_z(k)))

    def xg_copy(i):
        a = lax.rem(i, SLOTS)
        block = out.at[i, x_rows]
        return send(block, block, ref.hs.at[a], ref.hr.at[a], place.at(x=1 - place.x))

    def for_store(i, act):
        a = lax.rem(i, SLOTS)
        base = 0
        plan = ((ref.o_down, n_down, False), (ref.o_up, n_up, True), (ref.o_proj, n_proj, False),
                (ref.o_qkv, n_qkv, True))
        for target, count, rows_first in plan:
            u = i - base
            if rows_first:
                r, c = lax.rem(u, blocks), lax.div(u, blocks)
            else:
                r, c = lax.div(u, W // CW), lax.rem(u, W // CW)
            at = (pl.ds(pl.multiple_of(r * CB, CB), CB), pl.ds(pl.multiple_of(c * CW, CW), CW))

            @pl.when((u >= 0) & (u < count))
            def _(target=target, at=at):
                act(load(out.at[i], target.at[at], ref.osem.at[a]))

            base += count

    def add(*terms):
        whole = terms[0].astype(F32)
        for term in terms[1:]:
            whole = whole + term.astype(F32)
        return whole.astype(BF)

    def tick(i):
        def stage(lag):
            j = i - lag
            return j, (j >= 0) & (j < total)

        j1, ok1 = stage(1)

        @pl.when(ok1)
        def _():
            core_copy(j1).wait()
            a = lax.rem(j1, SLOTS)
            for y in range(Y):
                ysum[a, y] = add(part[lax.rem(j1, 2), place.c, y], crecv[lax.rem(j1, CORE_SLOTS), y])
            for k in range(1, Y):
                y_copy(j1, k).start()

        j2, ok2 = stage(1 + LAG)

        @pl.when(ok2)
        def _():
            a = lax.rem(j2, SLOTS)
            for k in range(1, Y):
                y_copy(j2, k).wait()
            for h in range(2):
                piece = slice(h * HB, (h + 1) * HB)
                xsum[a, h] = add(ysum[a, place.y, piece], *[yrecv[a, k - 1, piece] for k in range(1, Y)])
            x_copy(j2).start()

        j3, ok3 = stage(1 + 2 * LAG)

        @pl.when(ok3)
        def _():
            a = lax.rem(j3, SLOTS)
            x_copy(j3).wait()
            for z in range(Z):
                cols = slice(z * WZ, (z + 1) * WZ)
                zsum[a, z] = add(xsum[a, place.x, :, cols], xrecv[a, :, cols])
            for k in range(1, Z):
                z_copy(j3, k).start()

        j4, ok4 = stage(1 + 3 * LAG)

        @pl.when(ok4)
        def _():
            a = lax.rem(j4, SLOTS)
            for k in range(1, Z):
                z_copy(j4, k).wait()
            out[j4, x_rows, z_cols] = add(zsum[a, place.z], *[zrecv[a, k - 1] for k in range(1, Z)])
            for k in range(1, Z):
                zg_copy(j4, k).start()

        j5, ok5 = stage(1 + 4 * LAG)

        @pl.when(ok5)
        def _():
            for k in range(1, Z):
                zg_copy(j5, k).wait()
            xg_copy(j5).start()

        j6, ok6 = stage(1 + 5 * LAG)

        @pl.when(ok6)
        def _():
            xg_copy(j6).wait()
            for_store(j6, lambda copy: copy.start())

        j7, ok7 = stage(2 + 5 * LAG)

        @pl.when(ok7)
        def _():
            for_store(j7, lambda copy: copy.wait())

    def produce(i, left, offset, cols):
        slot = lax.rem(i, 2)
        for turn in range(2):
            c = 1 - place.c if turn == 0 else place.c
            for y in range(Y):
                first = offset(place.part(y, c))
                if CB % 128 == 0:
                    first = pl.multiple_of(first, 128)
                    value = matmul(left[:, pl.ds(first, CB)], cols, ((0,), (0,))).astype(BF)
                else:
                    start = pl.multiple_of(lax.div(first, 128) * 128, 128)
                    ref.tile[...] = matmul(left[:, pl.ds(start, 128)], cols, ((0,), (0,)))
                    value = ref.tile[pl.ds(pl.multiple_of(first - start, CB), CB)].astype(BF)
                part[slot, c, y] = value
            if turn == 0:
                core_copy(i).start()

    def columns(array, n):
        return array[:, pl.ds(pl.multiple_of(n * CW, CW), CW)]

    acc, gmid, act, slope = ref.acc, ref.gmid, ref.act_s, ref.slope_s
    spread = []
    for b in range(n_blocks):
        goal = need[min(b + 1, n_blocks - 1)] + 3 * GLAG
        start = spread[-1][1] if spread else ticked[0]
        left = n_staged + 3 * GLAG - start
        stop = min(max(goal, start + -(-left // max(1, n_blocks - 1 - b))), n_staged + 3 * GLAG)
        spread.append((start, stop))

    def block_step(b, _):
        slot = lax.rem(b, 2)
        for copy in block_loads(b):
            copy.wait()

        for at, (start, stop) in enumerate(spread):
            @pl.when(b == at)
            def _(start=start, stop=stop):
                for t in range(start, stop):
                    gather_tick(t)

        @pl.when(b + 1 < n_blocks)
        def _():
            for copy in block_loads(b + 1):
                copy.start()

        spots = []
        for p in range(shards):
            row, col = UP_B + p * down_rows // W, p * down_rows % W
            spots.append((slice(row, row + 1), pl.ds(pl.multiple_of(col + b * BW, BW), BW)))
        bias = jnp.concatenate([vec[spot] for spot in spots], axis=1)
        for t in range(rows // MT):
            tile = slice(t * MT, (t + 1) * MT)
            hidden = matmul(second[tile, :], ref.wu[slot]) + bias
            gate = 0.5 * (1.0 + lax.erf(hidden * (0.5**0.5)))
            act[tile, :] = (hidden * gate).astype(BF)
            bell = jnp.exp(-0.5 * hidden * hidden) * 0.3989422804014327
            slope[tile, :] = gate + hidden * bell

        def chunk(n):
            r, c = n // (W // CW), n % (W // CW)
            produce(b * per_block + n, act, lambda p: p * BW + r * CB, columns(gfeed, c))
            tick(b * per_block + n)

        chunk(0)
        sums = [0.0] * shards
        for t in range(rows // MT):
            tile = slice(t * MT, (t + 1) * MT)
            pre = (matmul(gfeed[tile, :], ref.wd[slot], ((1,), (1,))) * slope[tile, :]).astype(BF)
            for p in range(shards):
                mid = pre[:, p * BW : (p + 1) * BW]
                gpre[tile, pl.ds(pl.multiple_of(p * down_rows + b * BW, BW), BW)] = mid
                sums[p] = sums[p] + jnp.sum(mid.astype(F32), axis=0, keepdims=True)
            more = matmul(pre, ref.wu[slot], ((1,), (1,)))
            feed = matmul(act[tile, :], ref.wd[slot])

            @pl.when(b == 0)
            def _():
                gmid[tile, :] = more
                acc[tile, :] = feed

            @pl.when(b > 0)
            def _():
                gmid[tile, :] += more
                acc[tile, :] += feed

            if t == 0:
                for n in range(1, per_block):
                    chunk(n)
        for p in range(shards):
            row, cols = spots[p]
            small[0, 0, row, cols] = sums[p]
        return 0

    lax.fori_loop(0, n_blocks, block_step, 0)

    tok_out, tok_send = ref.tok_out, ref.tok_send

    def to_owner(t, value, kept, given):
        if R >= TR:
            lower = pl.ds(pl.multiple_of(lax.rem(t * TR, R), TR), TR)

            @pl.when(t * TR < R)
            def _():
                kept[mine, lower, :] = value.astype(kept.dtype)

            @pl.when(t * TR >= R)
            def _():
                given[lower, :] = value.astype(BF)
        else:
            kept[mine] = value[:R].astype(kept.dtype)
            given[...] = value[R:].astype(BF)

    def middle_tile(t, _):
        tile = pl.ds(pl.multiple_of(t * TR, TR), TR)
        low = branch[tile, :]
        middle = x_s[tile, :].astype(F32) + vector(ATTN_SCALE) * low
        feed = acc[tile, :] + vector(DOWN_B)
        to_owner(t, (middle + vector(MLP_SCALE) * feed) * vector(LIVE), tok_out, tok_send)
        upstream = cot[tile, :].astype(F32) * vector(LIVE)
        note(MLP_SCALE, jnp.sum(upstream * feed, axis=0, keepdims=True))
        unit, scale = norm_parts(middle)
        grad = gmid[tile, :]
        note(MLP_GAIN, jnp.sum(grad * unit, axis=0, keepdims=True))
        note(MLP_SHIFT, jnp.sum(grad, axis=0, keepdims=True))
        grad = upstream + norm_back(grad, unit, scale, vector(MLP_GAIN))
        gmid[tile, :] = grad
        note(ATTN_SCALE, jnp.sum(grad * low, axis=0, keepdims=True))
        grad = (grad * vector(ATTN_SCALE)).astype(BF)
        gbranch[tile, :] = grad
        note(PROJ_B, jnp.sum(grad.astype(F32), axis=0, keepdims=True))
        gatt[tile, :] = matmul(grad, ref.proj_s[...], ((1,), (1,))).astype(BF)
        return 0

    lax.fori_loop(0, rows // TR, middle_tile, 0)
    tok_copy = send(tok_send, tok_out.at[mine], ref.ts.at[0], ref.tr.at[0], swap_peer)
    tok_copy.start()

    def qkv_load(n):
        slot = lax.rem(n, 2)
        return load(ref.g_qkv.at[:, pl.ds(pl.multiple_of(n * CW, CW), CW)], ref.wu.at[slot, :, pl.ds(0, CW)],
                    ref.qsem.at[slot])

    pown, psend, precv = ref.pown, ref.psend, ref.precv
    gk_acc, gv_acc = ref.gk_acc, ref.gv_acc

    def pair_copy(p, k):
        a = lax.rem(p, PAIR_SLOTS)
        return send(psend.at[a, k - 1], precv.at[a, k - 1], ref.ps.at[a, k - 1], ref.pr.at[a, k - 1],
                    half_peer(k))

    def pair_done(p):
        a = lax.rem(p, PAIR_SLOTS)
        for k in range(1, half):
            pair_copy(p, k).wait()
        for which in range(2):
            whole = pown[a, which]
            for k in range(1, half):
                whole = whole + precv[a, k - 1, which].astype(F32)
            cols = pl.ds(pl.multiple_of((which + 1) * W + p * 128, 128), 128)
            G[:, cols] = whole.astype(BF)

    def up_chunk(u):
        i = n_down + u
        b, n = lax.rem(u, blocks), lax.div(u, blocks)
        produce(i, second, lambda p: p * other_rows + b * CB, columns(gpre, n))
        tick(i)

    per_pair = n_up // pairs

    def pair_step(p, _):
        if per_pair:
            for m in range(max(1, per_pair - tiles + 1)):
                up_chunk(p * per_pair + m)
        else:
            @pl.when(lax.rem(p, pairs // n_up) == 0)
            def _():
                up_chunk(lax.div(p, pairs // n_up))

        lane = lax.broadcasted_iota(jnp.int32, (1, 128), 1)
        cols = pl.ds(pl.multiple_of(p * 128, 128), 128)
        key, value = kv[0, :, cols], kv[1, :, cols]
        key_t = key.T
        for t in range(tiles):
            tile = slice(t * QT, (t + 1) * QT)
            q_tile, g_tile = query[tile, cols], gatt[tile, cols]
            parts = []
            for head in range(2):
                owned = (lane < HEAD_DIM) if head == 0 else (lane >= HEAD_DIM)
                own = jnp.where(owned, q_tile * BF(HEAD_DIM**-0.5), BF(0))
                own_grad = jnp.where(owned, g_tile, BF(0))
                probs = jnp.exp(matmul(key, own, ((1,), (1,))) - lse[p, head : head + 1, tile])
                grad_probs = matmul(value, own_grad, ((1,), (1,)))
                centre = jnp.sum(grad_probs * probs, axis=0, keepdims=True)
                grad_scores = (probs * (grad_probs - centre)).astype(BF)
                gv = matmul(probs.astype(BF), own_grad)
                gk = matmul(grad_scores, own)
                if t == 0 and head == 0:
                    gv_acc[...], gk_acc[...] = gv, gk
                else:
                    gv_acc[...] += gv
                    gk_acc[...] += gk
                lanes = slice(head * HEAD_DIM, (head + 1) * HEAD_DIM)
                parts.append(matmul(key_t[lanes, :], grad_scores))
            whole = jnp.concatenate(parts, axis=0) * (HEAD_DIM**-0.5)
            G[tile, cols] = whole.T.astype(BF)
            if per_pair and t < tiles - 1:
                up_chunk(p * per_pair + max(1, per_pair - tiles + 1) + t)
        a = lax.rem(p, PAIR_SLOTS)
        pown[a, 0], pown[a, 1] = gk_acc[:rows], gv_acc[:rows]
        for k in range(1, half):
            psend[a, k - 1, 0] = gk_acc[k * rows : (k + 1) * rows].astype(BF)
            psend[a, k - 1, 1] = gv_acc[k * rows : (k + 1) * rows].astype(BF)
            pair_copy(p, k).start()

        @pl.when(p >= 1)
        def _():
            pair_done(p - 1)
        return 0

    lax.fori_loop(0, pairs, pair_step, 0)

    qkv_load(0).start()

    def proj_step(u, _):
        i = n_down + n_up + u
        r, c = lax.div(u, W // CW), lax.rem(u, W // CW)
        produce(i, attended, lambda p: p * other_rows + r * CB, columns(gbranch, c))
        tick(i)

        @pl.when(u == 0)
        def _():
            pair_done(pairs - 1)
        return 0

    lax.fori_loop(0, n_proj, proj_step, 0)

    def qkv_step(n, _):
        cols = columns(G, n)
        for b in range(blocks):
            i = n_down + n_up + n_proj + n * blocks + b
            produce(i, first, lambda p: p * other_rows + b * CB, cols)
            tick(i)
            if b == 0:
                qkv_load(n).wait()

                @pl.when(n + 1 < 3 * W // CW)
                def _():
                    qkv_load(n + 1).start()

                for t in range(rows // MT):
                    tile = slice(t * MT, (t + 1) * MT)
                    term = matmul(cols[tile, :], ref.wu[lax.rem(n, 2), :, :CW], ((1,), (1,)))

                    @pl.when(n == 0)
                    def _():
                        acc[tile, :] = term

                    @pl.when(n > 0)
                    def _():
                        acc[tile, :] += term
        return 0

    lax.fori_loop(0, 3 * W // CW, qkv_step, 0)

    gt_out, gt_send, gt_recv = ref.gt_out, ref.gt_send, ref.gt_recv

    def first_tile(t, _):
        tile = pl.ds(pl.multiple_of(t * TR, TR), TR)
        unit, scale = norm_parts(x_s[tile, :].astype(F32))
        grad = acc[tile, :]
        note(ATTN_GAIN, jnp.sum(grad * unit, axis=0, keepdims=True))
        note(ATTN_SHIFT, jnp.sum(grad, axis=0, keepdims=True))
        note(QV, jnp.sum(G[tile, :W].astype(F32), axis=0, keepdims=True))
        note(QV + 1, jnp.sum(G[tile, 2 * W :].astype(F32), axis=0, keepdims=True))
        to_owner(t, gmid[tile, :] + norm_back(grad, unit, scale, vector(ATTN_GAIN)), gt_out, gt_send)
        return 0

    lax.fori_loop(0, rows // TR, first_tile, 0)

    small_steps = [
        [place.at(c=1 - place.c)],
        [place.at(y=place.ahead_y(k)) for k in range(1, Y)],
        [place.at(x=1 - place.x)],
        [place.at(z=place.ahead_z(k)) for k in range(1, Z)],
    ]

    def small_send(step):
        return [
            send(small.at[step, 0], small.at[step, k + 1], ref.ss.at[step, k], ref.sr.at[step, k], device)
            for k, device in enumerate(small_steps[step])
        ]

    def small_step(step):
        for copy in small_send(step):
            copy.wait()
        whole = small[step, 0]
        for k in range(len(small_steps[step])):
            whole = whole + small[step, k + 1]
        if step < 3:
            small[step + 1, 0] = whole
            for copy in small_send(step + 1):
                copy.start()
        else:
            ref.small_out[...] = whole

    for copy in small_send(0):
        copy.start()
    gt_copy = send(gt_send, gt_recv, ref.ts.at[1], ref.tr.at[1], swap_peer)
    depth = 3 + 5 * LAG
    for lag in range(depth):
        tick(total + lag)
        if lag == 1:
            gt_copy.start()
        if lag % 2 == 1 and lag < 8:
            small_step(lag // 2)
    tok_copy.wait()
    gt_copy.wait()
    gt_out[1 - mine] = gt_recv[...].astype(F32)


def layer(replicas, shards, vectors, count, tokens, cotangent, weights):
    Y, Z, half = shards // 2, replicas // 2, shards // 2
    _, R, W = tokens.shape
    rows, keys = 2 * R, half * 2 * R
    FF = weights[UP].shape[1]
    CB, CW = min(128, W // shards), max(512, 128 * Z)
    HB, WZ = CB // 2, CW // Z
    total = (FF // shards // CB) * (W // CW) + (W // shards // CB) * ((FF + 4 * W) // CW)
    peers = max(Y, Z, 2)
    staged, direct, _ = gather_items(replicas, shards, W, FF)
    m = len(staged) + len(direct)
    multiples = tuple(v.shape[0] // (W // shards) for v in vectors)
    if (W // shards) % 128:
        vectors = [v.reshape(n, W // shards) for v, n in zip(vectors, multiples)]
    dma = pltpu.SemaphoreType.DMA
    vmem, anywhere = pl.BlockSpec(memory_space=pltpu.VMEM), pl.BlockSpec(memory_space=pl.ANY)
    inputs = dict(count=count, tokens=tokens, cotangent=cotangent, qkv=weights[QKV], proj=weights[PROJ],
                  up=weights[UP], down=weights[DOWN])
    scratch = dict(
        part=pltpu.VMEM((2, 2, Y, CB, CW), BF),
        crecv=pltpu.VMEM((CORE_SLOTS, Y, CB, CW), BF),
        ysum=pltpu.VMEM((SLOTS, Y, CB, CW), BF),
        yrecv=pltpu.VMEM((SLOTS, Y - 1, CB, CW), BF),
        xsum=pltpu.VMEM((SLOTS, 2, HB, CW), BF),
        xrecv=pltpu.VMEM((SLOTS, HB, CW), BF),
        zsum=pltpu.VMEM((SLOTS, Z, HB, WZ), BF),
        zrecv=pltpu.VMEM((SLOTS, Z - 1, HB, WZ), BF),
        out=pltpu.VMEM((total, CB, CW), BF),
        small_buf=pltpu.VMEM((4, peers, 16, W), F32),
        kv=pltpu.VMEM((2, keys, W), BF),
        gpre=pltpu.VMEM((rows, FF), BF),
        act_s=pltpu.VMEM((rows, shards * BW), BF),
        slope_s=pltpu.VMEM((rows, shards * BW), F32),
        cot_s=pltpu.VMEM((rows, W), BF),
        gfeed=pltpu.VMEM((rows, W), BF),
        x_s=pltpu.VMEM((rows, W), BF),
        branch_s=pltpu.VMEM((rows, W), F32),
        second_s=pltpu.VMEM((rows, W), BF),
        attended_s=pltpu.VMEM((rows, W), BF),
        query_s=pltpu.VMEM((rows, W), BF),
        first_s=pltpu.VMEM((rows, W), BF),
        proj_s=pltpu.VMEM((W, W), BF),
        wd=pltpu.VMEM((2, shards * BW, W), BF),
        wu=pltpu.VMEM((2, W, shards * BW), BF),
        acc=pltpu.VMEM((rows, W), F32),
        gmid=pltpu.VMEM((rows, W), F32),
        gbranch=pltpu.VMEM((rows, W), BF),
        gatt=pltpu.VMEM((rows, W), BF),
        G=pltpu.VMEM((rows, 3 * W), BF),
        pown=pltpu.VMEM((PAIR_SLOTS, 2, rows, 128), F32),
        psend=pltpu.VMEM((PAIR_SLOTS, half - 1, 2, rows, 128), BF),
        precv=pltpu.VMEM((PAIR_SLOTS, half - 1, 2, rows, 128), BF),
        gk_acc=pltpu.VMEM((keys, 128), F32),
        gv_acc=pltpu.VMEM((keys, 128), F32),
        tok_send=pltpu.VMEM((R, W), BF),
        gt_send=pltpu.VMEM((R, W), BF),
        gt_recv=pltpu.VMEM((R, W), BF),
        small_s=pltpu.VMEM((shards, 16, W // shards), F32),
        vec=pltpu.VMEM((16, W), F32),
        lse=pltpu.VMEM((W // 128, 2, rows), F32),
        lsem=dma((12,)), wsem=dma((2, 2, shards)), qsem=dma((2,)), osem=dma((SLOTS,)),
        gys=dma((m, Y - 1)), gyr=dma((m, Y - 1)),
        gzs=dma((m, Y - 1, Z - 1)), gzr=dma((m, Y - 1, Z - 1)),
        gxs=dma((m, Y - 1)), gxr=dma((m, Y - 1)),
        gcs=dma((m, Y - 1)), gcr=dma((m, Y - 1)),
        os=dma((4,)), orr=dma((4,)),
        vs=dma((shards - 1,)), vr=dma((shards - 1,)),
        ks=dma((2, W // CW, half - 1)), kr=dma((2, W // CW, half - 1)),
        cs=dma((CORE_SLOTS,)), cr=dma((CORE_SLOTS,)),
        ys=dma((SLOTS, Y - 1)), yr=dma((SLOTS, Y - 1)),
        xs=dma((SLOTS,)), xr=dma((SLOTS,)),
        zs=dma((SLOTS, Z - 1)), zr=dma((SLOTS, Z - 1)),
        gs=dma((SLOTS, Z - 1)), gr=dma((SLOTS, Z - 1)),
        hs=dma((SLOTS,)), hr=dma((SLOTS,)),
        ps=dma((PAIR_SLOTS, half - 1)), pr=dma((PAIR_SLOTS, half - 1)),
        ss=dma((4, peers - 1)), sr=dma((4, peers - 1)),
        ts=dma((4,)), tr=dma((4,)),
    )
    if CB % 128:
        scratch["tile"] = pltpu.VMEM((128, CW), F32)
    outs = dict(
        o_down=jax.ShapeDtypeStruct((FF // shards, W), BF),
        o_up=jax.ShapeDtypeStruct((W // shards, FF), BF),
        o_proj=jax.ShapeDtypeStruct((W // shards, W), BF),
        o_qkv=jax.ShapeDtypeStruct((W // shards, 3 * W), BF),
        small_out=jax.ShapeDtypeStruct((16, W), F32),
        tok_out=jax.ShapeDtypeStruct((2, R, W), BF),
        gt_out=jax.ShapeDtypeStruct((2, R, W), F32),
        g_qkv=jax.ShapeDtypeStruct((W, 3 * W), BF),
        g_proj=jax.ShapeDtypeStruct((W, W), BF),
        g_up=jax.ShapeDtypeStruct((W, FF), BF),
        g_down=jax.ShapeDtypeStruct((FF, W), BF),
    )
    names = tuple(inputs) + tuple(outs) + tuple(scratch)
    results = pl.pallas_call(
        functools.partial(layer_kernel, replicas, shards, multiples, names),
        in_specs=[vmem] * len(vectors) + [pl.BlockSpec(memory_space=pltpu.SMEM)] + [anywhere] * 6,
        out_specs=[anywhere] * 4 + [vmem] * 3 + [anywhere] * 4,
        out_shape=list(outs.values()),
        scratch_shapes=list(scratch.values()),
        compiler_params=pltpu.CompilerParams(
            collective_id=0, has_side_effects=True, vmem_limit_bytes=63 * MIB
        ),
    )(*vectors, *inputs.values())
    return results[:7]


def on_device(replicas, shards, tokens, qkv_weight, qv_bias, proj_weight, proj_bias, up_weight, up_bias,
              down_weight, down_bias, attn_gain, attn_shift, mlp_gain, mlp_shift, attn_scale, mlp_scale,
              cotangent, image_count):
    vectors = (qv_bias, proj_bias, up_bias, down_bias, attn_gain, attn_shift, mlp_gain, mlp_shift,
               attn_scale, mlp_scale)
    shard = lax.axis_index("shard")
    *grads, small, output, grad_tokens = layer(
        replicas, shards, vectors, image_count, tokens, cotangent,
        (qkv_weight, proj_weight, up_weight, down_weight),
    )
    grad_down, grad_up, grad_proj, grad_qkv = [grad.astype(F32) for grad in grads]

    def own(row, count=1):
        whole = small[row : row + count].reshape(-1)
        size = whole.shape[0] // shards
        return lax.dynamic_slice_in_dim(whole, shard * size, size)

    return (output, grad_tokens, grad_qkv, own(QV, 2), grad_proj, own(PROJ_B), grad_up,
            own(UP_B, DOWN_B - UP_B), grad_down, own(DOWN_B), own(ATTN_GAIN), own(ATTN_SHIFT), own(MLP_GAIN),
            own(MLP_SHIFT), own(ATTN_SCALE), own(MLP_SCALE))


def solution(mesh):
    rows, vector = P("shard", None), P("shard")
    image = P("replica", "shard", None)
    in_specs = (image, rows, vector, rows, vector, rows, vector, rows, vector, vector, vector, vector,
                vector, vector, vector, image, P())
    out_specs = (image, image, rows, vector, rows, vector, rows, vector, rows, vector, vector, vector,
                 vector, vector, vector, vector)
    return jax.shard_map(
        functools.partial(on_device, mesh.shape["replica"], mesh.shape["shard"]),
        mesh=mesh, in_specs=in_specs, out_specs=out_specs, check_vma=False,
    )
```

```python
import functools
import types

import jax
import jax.numpy as jnp
from jax import lax
from jax.experimental import pallas as pl
from jax.experimental.pallas import tpu as pltpu
from jax.sharding import PartitionSpec as P

HEAD_DIM = 64
EPS = 1e-06
BF = jnp.bfloat16
F32 = jnp.float32
MESH = pl.DeviceIdType.MESH
MIB = 1024 * 1024
SLOTS = 6
PAIR_SLOTS = 4
CORE_SLOTS = 4
LAG = 2


def matmul(left, right, dims=((1,), (0,))):
    return lax.dot_general(left, right, (dims, ((), ())), preferred_element_type=F32)


class Place:
    def __init__(self, replicas, shards):
        self.Z, self.Y = replicas // 2, shards // 2
        self.shards = shards
        replica, shard = lax.axis_index("replica"), lax.axis_index("shard")
        self.x, self.z = lax.rem(replica, 2), lax.div(replica, 2)
        self.c, self.y = lax.rem(shard, 2), lax.div(shard, 2)
        self.s = shard

    def part(self, y, c):
        return y * 2 + c

    def at(self, x=None, z=None, y=None, c=None):
        x = self.x if x is None else x
        z = self.z if z is None else z
        y = self.y if y is None else y
        c = self.c if c is None else c
        return (z * 2 + x, y * 2 + c)

    def near_z(self, k):
        z, bit = self.z, 1
        while bit < self.Z:
            if k & bit:
                z = z + bit - 2 * bit * lax.rem(lax.div(z, bit), 2)
            bit *= 2
        return z

    def z_order(self):
        return sorted(range(1, self.Z), key=lambda k: (-(k.bit_length()), k))

    def ahead_y(self, k):
        return lax.rem(self.y + k, self.Y)

    def behind_y(self, k):
        return lax.rem(self.y + self.Y - k, self.Y)

    def greet(self, extra=()):
        others = [self.at(c=1 - self.c), self.at(x=1 - self.x)]
        others += [self.at(y=self.ahead_y(k)) for k in range(1, self.Y)]
        others += [self.at(z=self.near_z(k)) for k in range(1, self.Z)]
        others += list(extra)
        barrier = pltpu.get_barrier_semaphore()
        for other in others:
            pl.semaphore_signal(barrier, inc=1, device_id=other, device_id_type=MESH)
        pl.semaphore_wait(barrier, len(others))


def send(src, dst, send_sem, recv_sem, device):
    return pltpu.make_async_remote_copy(
        src_ref=src,
        dst_ref=dst,
        send_sem=send_sem,
        recv_sem=recv_sem,
        device_id=device,
        device_id_type=MESH,
    )


QV, PROJ_B, UP_B, DOWN_B, ATTN_GAIN, ATTN_SHIFT, MLP_GAIN, MLP_SHIFT, ATTN_SCALE, MLP_SCALE, LIVE = (
    0, 2, 3, 7, 8, 9, 10, 11, 12, 13, 14)
SMALL_ROWS = ((QV, 2), (PROJ_B, 1), (UP_B, 4), (DOWN_B, 1), (ATTN_GAIN, 1), (ATTN_SHIFT, 1), (MLP_GAIN, 1),
              (MLP_SHIFT, 1), (ATTN_SCALE, 1), (MLP_SCALE, 1))
QKV, PROJ, UP, DOWN = range(4)


def norm_parts(values):
    centre = values - jnp.mean(values, axis=-1, keepdims=True)
    scale = lax.rsqrt(jnp.mean(centre * centre, axis=-1, keepdims=True) + EPS)
    return centre * scale, scale


def norm_back(grad, unit, scale, gain):
    inner = grad * gain
    return scale * (
        inner
        - jnp.mean(inner, axis=-1, keepdims=True)
        - unit * jnp.mean(inner * unit, axis=-1, keepdims=True)
    )


BW = 128


FIRST = 6
TAIL = 4


def gather_items(replicas, shards, width, hidden):
    Z = replicas // 2
    step = max(512, 128 * Z)
    size, down = width // shards, hidden // shards
    halves = width // step
    items = [(QKV, 0, size, n * width + h * step, step) for h in range(halves) for n in (1, 2, 0)]
    items += [(PROJ, 0, size, h * step, step) for h in range(halves)]
    upto, known = [], set()
    for b in range(down // BW):
        for p in range(shards):
            c = (p * down + b * BW) // step
            if c not in known:
                known.add(c)
                items.append((UP, 0, size, c * step, step))
        items.append((DOWN, b * BW, BW, 0, width))
        upto.append(len(items))
    straight = set(range(len(items) - TAIL, len(items)))
    staged = [item for n, item in enumerate(items) if n not in straight]
    direct = [item for n, item in enumerate(items) if n in straight]
    need = []
    for n in upto:
        over = len([m for m in straight if m < n])
        need.append((n - over, over))
    return staged, direct, need


def layer_kernel(replicas, shards, multiples, names, *refs):
    vector_refs, refs = refs[: len(multiples)], refs[len(multiples) :]
    ref = types.SimpleNamespace(**dict(zip(names, refs)))
    place = Place(replicas, shards)
    Y, Z, s = place.Y, place.Z, place.s
    half = shards // 2
    part, crecv, ysum, yrecv = ref.part, ref.crecv, ref.ysum, ref.yrecv
    xsum, xrecv, zsum, zrecv = ref.xsum, ref.xrecv, ref.zsum, ref.zrecv
    out, small, vec, lse = ref.out, ref.small_buf, ref.vec, ref.lse
    CB, CW = part.shape[3], part.shape[4]
    rows, W = ref.gfeed.shape
    R = rows // 2
    keys = half * rows
    FF = ref.gpre.shape[1]
    down_rows, other_rows = FF // shards, W // shards
    n_blocks, blocks = down_rows // BW, other_rows // CB
    per_block = (BW // CB) * (W // CW)
    n_down, n_up = n_blocks * per_block, blocks * (FF // CW)
    n_proj, n_qkv = blocks * (W // CW), blocks * (3 * W // CW)
    total = n_down + n_up + n_proj + n_qkv
    mine = lax.div(s, half)
    j_half = lax.rem(s, half)
    replica = lax.axis_index("replica")
    kv, gpre, cot, gfeed, G = ref.kv, ref.gpre, ref.cot_s, ref.gfeed, ref.G
    second, first, query, x_s = ref.second_s, ref.first_s, ref.query_s, ref.x_s
    attended, branch, gbranch, gatt = ref.attended_s, ref.branch_s, ref.gbranch, ref.gatt
    TR, MT, QT, TM = min(128, R), min(256, rows), min(256, rows), min(256, R)
    pairs, tiles = W // 128, rows // QT

    def half_peer(k):
        return (replica, mine * half + lax.rem(j_half + k, half))

    swap_peer = (replica, lax.rem(s + half, shards))

    def load(src, dst, sem):
        return pltpu.make_async_copy(src, dst, sem)

    sources = (ref.qkv, ref.proj, ref.up, ref.down)
    weights = (ref.g_qkv, ref.g_proj, ref.g_up, ref.g_down)
    sizes = [source.shape[0] for source in sources]
    bounce = (G, gbranch, gpre, ref.proj_s)

    def own_rows(w):
        return weights[w].at[pl.ds(pl.multiple_of(s * sizes[w], sizes[w]), sizes[w])]

    own_loads = [load(sources[w], bounce[w].at[pl.ds(0, sizes[w])], ref.lsem.at[w]) for w in range(4)]
    own_stores = [load(bounce[w].at[pl.ds(0, sizes[w])], own_rows(w), ref.lsem.at[4 + w]) for w in range(4)]
    x_load = load(ref.tokens.at[mine], x_s.at[pl.ds(0, R)], ref.lsem.at[8])
    cot_load = load(ref.cotangent.at[mine], cot.at[pl.ds(0, R)], ref.lsem.at[9])
    x_load.start()
    for copy in own_loads:
        copy.start()
    cot_load.start()
    row = 0
    for vector_ref, count in zip(vector_refs, multiples):
        values = vector_ref[...].astype(F32).reshape(count, ref.small_s.shape[2])
        ref.small_s[s, row : row + count, :] = values
        row += count
    place.greet([(replica, lax.rem(s + k, shards)) for k in range(1, shards)])

    staged, direct, need = gather_items(replicas, shards, W, FF)
    items = staged + direct
    n_staged = len(staged)

    def piece(m, owner, whole_rows, whole_cols):
        w, row, size, col, width = items[m]
        at, cols = owner * sizes[w] + row, pl.ds(col, width)
        if not whole_rows:
            size //= 2
            at = at + place.x * size
        if not whole_cols:
            if size % (16 * Z):
                cols = pl.ds(pl.multiple_of(col + place.z * (width // Z), 128), width // Z)
            else:
                size //= Z
                at = at + place.z * size
        return pl.ds(pl.multiple_of(at, 16), size), cols

    def gy_copy(m, k):
        w, whole = items[m][0], m >= n_staged
        return send(sources[w].at[piece(m, 0, whole, whole)], weights[w].at[piece(m, s, whole, whole)],
                    ref.gys.at[m, k - 1], ref.gyr.at[m, k - 1], place.at(y=place.ahead_y(k)))

    def gathered(m, k, whole_rows, whole_cols):
        owner = place.part(place.behind_y(k), place.c)
        return weights[items[m][0]].at[piece(m, owner, whole_rows, whole_cols)]

    def gz_copy(m, k, j):
        b = gathered(m, k, False, False)
        return send(b, b, ref.gzs.at[m, k - 1, j - 1], ref.gzr.at[m, k - 1, j - 1],
                    place.at(z=place.near_z(j)))

    def gx_copy(m, k):
        b = gathered(m, k, False, True)
        return send(b, b, ref.gxs.at[m, k - 1], ref.gxr.at[m, k - 1], place.at(x=1 - place.x))

    def gc_copy(m, k):
        b = gathered(m, k, True, True)
        return send(b, b, ref.gcs.at[m, k - 1], ref.gcr.at[m, k - 1], place.at(c=1 - place.c))

    def gy_start(m):
        for k in range(1, Y):
            gy_copy(m, k).start()

    def direct_arrived(h):
        for k in range(1, Y):
            gy_copy(n_staged + h, k).wait()
            gc_copy(n_staged + h, k).start()

    def arrived(m):
        for k in range(1, Y):
            gc_copy(m, k).wait()

    halves = W // CW
    early = 3 * halves

    def gather_y_step(m):
        for k in range(1, Y):
            gy_copy(m, k).wait()
            for j in place.z_order():
                gz_copy(m, k, j).start()

    def gather_x_step(m):
        if 0 <= m - 2 < n_staged:
            for k in range(1, Y):
                gx_copy(m - 2, k).wait()
                gc_copy(m - 2, k).start()
        if m < n_staged:
            for k in range(1, Y):
                for j in range(1, Z):
                    gz_copy(m, k, j).wait()
                gx_copy(m, k).start()
        if 0 <= m - 4 < n_staged and m - 4 >= done[2]:
            gather_c_step(m - 4)

    def gather_c_step(m):
        for k in range(1, Y):
            gc_copy(m, k).wait()
        done[2] = m + 1

    last_step = n_staged + 4
    done = [0, 0, 0]

    def gather_y(n):
        while done[0] < min(n, n_staged):
            gather_y_step(done[0])
            done[0] += 1

    def gather_x(n, window=3):
        while done[1] < min(n, last_step):
            gather_y(done[1] + window)
            gather_x_step(done[1])
            done[1] += 1

    def gather_until(m):
        gather_x(m + 2)
        while done[2] < min(m, n_staged):
            gather_c_step(done[2])

    def direct_step(h):
        for k in range(1, Y):
            gy_copy(n_staged + h, k).wait()
            gc_copy(n_staged + h, k).start()

    def direct_arrived(h):
        for k in range(1, Y):
            gc_copy(n_staged + h, k).wait()

    x_swap = send(ref.tokens.at[1 - mine], x_s.at[pl.ds(R, R)], ref.ts.at[2], ref.tr.at[2], swap_peer)
    cot_swap = send(ref.cotangent.at[1 - mine], cot.at[pl.ds(R, R)], ref.ts.at[3], ref.tr.at[3], swap_peer)
    small_sends = [
        send(ref.small_s.at[s], ref.small_s.at[s], ref.vs.at[k - 1], ref.vr.at[k - 1],
             (replica, lax.rem(s + k, shards)))
        for k in range(1, shards)
    ]
    own_sends = [send(sources[w], own_rows(w), ref.os.at[w], ref.orr.at[w], place.at(c=1 - place.c))
                 for w in range(4)]
    for copy in small_sends:
        copy.start()
    for m in range(min(FIRST, n_staged)):
        gy_start(m)
    x_swap.start()
    for m in range(FIRST, n_staged):
        gy_start(m)
    for copy in own_sends:
        copy.start()

    for copy in small_sends:
        copy.wait()
    vec[...] = jnp.zeros_like(vec)
    row = 0
    for count in multiples:
        pieces = [ref.small_s[p, row + r : row + r + 1, :] for p in range(shards) for r in range(count)]
        for r in range(count):
            vec[row + r : row + r + 1, :] = jnp.concatenate(pieces[r * shards : (r + 1) * shards], axis=1)
        row += count
    live = (mine < ref.count[replica]).astype(F32)
    vec[LIVE : LIVE + 1, :] = jnp.full((1, W), live, F32)

    def vector(row):
        return vec[row : row + 1, :]

    def note(row, value):
        small[row : row + 1, :] += value

    def norm_tile(t, _):
        tile = pl.ds(pl.multiple_of(t * TR, TR), TR)
        unit, _ = norm_parts(x_s[tile, :].astype(F32))
        first[tile, :] = (unit * vector(ATTN_GAIN) + vector(ATTN_SHIFT)).astype(BF)
        return 0

    x_load.wait()
    lax.fori_loop(0, R // TR, norm_tile, 0)
    for w in range(4):
        own_loads[w].wait()
        own_stores[w].start()
    gather_x(3)
    x_swap.wait()
    lax.fori_loop(R // TR, rows // TR, norm_tile, 0)
    gather_until(2)
    own_stores[QKV].wait()
    own_sends[QKV].wait()

    def kv_copy(which, h, k):
        cols = pl.ds(h * CW, CW)
        return send(kv.at[which, pl.ds(0, rows), cols], kv.at[which, pl.ds((half - k) * rows, rows), cols],
                    ref.ks.at[which, h, k - 1], ref.kr.at[which, h, k - 1], half_peer(k))

    def qkv_slot(slot):
        if slot < 2:
            return ref.wu[slot, :, :CW]
        return ref.wq[...]

    def qkv_tile(n, h, slot):
        target = ref.wu.at[slot, :, pl.ds(0, CW)] if slot < 2 else ref.wq
        return load(ref.g_qkv.at[:, pl.ds(n * W + h * CW, CW)], target, ref.qsem.at[slot])

    def project(h, ready=None):
        here = slice(h * CW, (h + 1) * CW)
        tile_loads = [qkv_tile(1, h, 0), qkv_tile(2, h, 1), qkv_tile(0, h, 2)]
        tile_loads[0].start()
        tile_loads[1].start()
        for n in range(3):
            if n == 2:
                if ready:
                    ready()
                tile_loads[2].start()
            tile_loads[n].wait()
            for t in range(rows // MT):
                tile = slice(t * MT, (t + 1) * MT)
                value = matmul(first[tile, :], qkv_slot(n))
                if n == 0:
                    kv[0, tile, here] = value.astype(BF)
                elif n == 1:
                    kv[1, tile, here] = (value + vector(QV + 1)[:, here]).astype(BF)
                else:
                    query[tile, here] = (value + vector(QV)[:, here]).astype(BF)
            if n < 2:
                for k in range(1, half):
                    kv_copy(n, h, k).start()

    def exchanged(h):
        for which in range(2):
            for k in range(1, half):
                kv_copy(which, h, k).wait()

    project(0, lambda: gather_until(3))
    cot_swap.start()
    for h in range(len(direct)):
        gy_start(n_staged + h)

    plan = {}

    def at_pair(p, act):
        plan.setdefault(p, []).append(act)

    pace = (6, 7, 8, 9, 11, 12, 13, 14)
    for p in range(1, pairs):
        at_pair(p, lambda p=p: gather_x(pace[p], 5))
    if halves > 1:
        def second_half():
            gather_until(early)
            project(1)

        at_pair(pairs // 2 - 1, second_half)
        at_pair(pairs // 2, lambda: exchanged(1))
    gather_x(pace[0], 5)
    exchanged(0)

    def both_heads(array, lane):
        return jnp.concatenate([jnp.where(lane < HEAD_DIM, array, BF(0)), jnp.where(lane >= HEAD_DIM, array, BF(0))])

    def own_heads(array):
        n = array.shape[1] // 2
        return jnp.concatenate([array[:HEAD_DIM, :n], array[HEAD_DIM:, n:]])

    def attend(p, _):
        for at in sorted(plan):
            @pl.when(p == at)
            def _(at=at):
                for act in plan[at]:
                    act()

        lane = lax.broadcasted_iota(jnp.int32, (1, 128), 1)
        cols = pl.ds(pl.multiple_of(p * 128, 128), 128)
        key, value_t = kv[0, :, cols], kv[1, :, cols].T
        scores = matmul(key, both_heads(query[:, cols] * BF(HEAD_DIM**-0.5), lane), ((1,), (1,)))
        highest = jnp.max(scores, axis=0, keepdims=True)
        expos = jnp.exp(scores - highest)
        denom = jnp.sum(expos, axis=0, keepdims=True)
        probs = (expos * (1.0 / denom)).astype(BF)
        lse[p] = highest + jnp.log(denom)
        attended[:, cols] = own_heads(matmul(value_t, probs)).T.astype(BF)
        return 0

    lax.fori_loop(0, pairs, attend, 0)

    gather_until(early + halves)
    own_stores[PROJ].wait()
    own_stores[DOWN].wait()
    own_sends[PROJ].wait()
    proj_load = load(ref.g_proj, ref.proj_s, ref.lsem.at[10])
    proj_load.start()
    cot_load.wait()
    cot_swap.wait()
    small[...] = jnp.zeros_like(small)

    def feed_tile(t, _):
        tile = pl.ds(pl.multiple_of(t * TR, TR), TR)
        value = (cot[tile, :].astype(F32) * vector(LIVE) * vector(MLP_SCALE)).astype(BF)
        gfeed[tile, :] = value
        note(DOWN_B, jnp.sum(value.astype(F32), axis=0, keepdims=True))
        return 0

    lax.fori_loop(0, rows // TR, feed_tile, 0)
    proj_load.wait()

    def branch_tile(t, _):
        tile = pl.ds(pl.multiple_of(t * MT, MT), MT)
        low = matmul(attended[tile, :], ref.proj_s[...]) + vector(PROJ_B)
        branch[tile, :] = low
        unit, _ = norm_parts(x_s[tile, :].astype(F32) + vector(ATTN_SCALE) * low)
        second[tile, :] = (unit * vector(MLP_GAIN) + vector(MLP_SHIFT)).astype(BF)
        return 0

    lax.fori_loop(0, rows // MT, branch_tile, 0)
    gather_x(pace[-1] + 2, 5)
    for w in (UP, DOWN):
        own_sends[w].wait()
    own_stores[UP].wait()

    def block_loads(b):
        slot = lax.rem(b, 2)
        copies = []
        for p in range(shards):
            at = pl.ds(pl.multiple_of(p * down_rows + b * BW, BW), BW)
            to = pl.ds(p * BW, BW)
            copies.append(load(ref.g_up.at[:, at], ref.wu.at[slot, :, to], ref.wsem.at[0, slot, p]))
            copies.append(load(ref.g_down.at[at], ref.wd.at[slot, to], ref.wsem.at[1, slot, p]))
        return copies

    gather_until(need[0][0])
    for h in range(need[0][1]):
        direct_step(h)
        direct_arrived(h)
    for copy in block_loads(0):
        copy.start()

    def core_copy(i):
        a = lax.rem(i, CORE_SLOTS)
        return send(part.at[lax.rem(i, 2), 1 - place.c], crecv.at[a], ref.cs.at[a], ref.cr.at[a],
                    place.at(c=1 - place.c))

    def y_copy(i, k):
        a = lax.rem(i, SLOTS)
        return send(ysum.at[a, place.ahead_y(k)], yrecv.at[a, k - 1], ref.ys.at[a, k - 1],
                    ref.yr.at[a, k - 1], place.at(y=place.ahead_y(k)))

    def x_copy(i):
        a = lax.rem(i, SLOTS)
        return send(xsum.at[a, 1 - place.x], xrecv.at[a], ref.xs.at[a], ref.xr.at[a],
                    place.at(x=1 - place.x))

    def z_copy(i, k):
        a = lax.rem(i, SLOTS)
        return send(zsum.at[a, place.near_z(k)], zrecv.at[a, k - 1], ref.zs.at[a, k - 1],
                    ref.zr.at[a, k - 1], place.at(z=place.near_z(k)))

    HB, WZ = CB // 2, CW // Z
    x_rows = pl.ds(pl.multiple_of(place.x * HB, HB), HB)
    z_cols = pl.ds(pl.multiple_of(place.z * WZ, WZ), WZ)

    def zg_copy(i, k):
        a = lax.rem(i, SLOTS)
        block = out.at[i, x_rows, z_cols]
        return send(block, block, ref.gs.at[a, k - 1], ref.gr.at[a, k - 1],
                    place.at(z=place.near_z(k)))

    def xg_copy(i):
        a = lax.rem(i, SLOTS)
        block = out.at[i, x_rows]
        return send(block, block, ref.hs.at[a], ref.hr.at[a], place.at(x=1 - place.x))

    def for_store(i, act):
        a = lax.rem(i, SLOTS)
        base = 0
        plan = ((ref.o_down, n_down, False), (ref.o_up, n_up, True), (ref.o_proj, n_proj, False),
                (ref.o_qkv, n_qkv, True))
        for target, count, rows_first in plan:
            u = i - base
            if rows_first:
                r, c = lax.rem(u, blocks), lax.div(u, blocks)
            else:
                r, c = lax.div(u, W // CW), lax.rem(u, W // CW)
            at = (pl.ds(pl.multiple_of(r * CB, CB), CB), pl.ds(pl.multiple_of(c * CW, CW), CW))

            @pl.when((u >= 0) & (u < count))
            def _(target=target, at=at):
                act(load(out.at[i], target.at[at], ref.osem.at[a]))

            base += count

    def add(*terms):
        if len(terms) == 2:
            return terms[0] + terms[1]
        whole = terms[0].astype(F32)
        for term in terms[1:]:
            whole = whole + term.astype(F32)
        return whole.astype(BF)

    def tick(i):
        def stage(lag):
            j = i - lag
            return j, (j >= 0) & (j < total)

        j1, ok1 = stage(1)

        @pl.when(ok1)
        def _():
            core_copy(j1).wait()
            a = lax.rem(j1, SLOTS)
            for y in range(Y):
                ysum[a, y] = add(part[lax.rem(j1, 2), place.c, y], crecv[lax.rem(j1, CORE_SLOTS), y])
            for k in range(1, Y):
                y_copy(j1, k).start()

        j2, ok2 = stage(1 + LAG)

        @pl.when(ok2)
        def _():
            a = lax.rem(j2, SLOTS)
            for k in range(1, Y):
                y_copy(j2, k).wait()
            for h in range(2):
                piece = slice(h * HB, (h + 1) * HB)
                xsum[a, h] = add(ysum[a, place.y, piece], *[yrecv[a, k - 1, piece] for k in range(1, Y)])
            x_copy(j2).start()

        j3, ok3 = stage(1 + 2 * LAG)

        @pl.when(ok3)
        def _():
            a = lax.rem(j3, SLOTS)
            x_copy(j3).wait()
            for z in range(Z):
                cols = slice(z * WZ, (z + 1) * WZ)
                zsum[a, z] = add(xsum[a, place.x, :, cols], xrecv[a, :, cols])
            for k in place.z_order():
                z_copy(j3, k).start()

        j4, ok4 = stage(1 + 3 * LAG)

        @pl.when(ok4)
        def _():
            a = lax.rem(j4, SLOTS)
            for k in range(1, Z):
                z_copy(j4, k).wait()
            out[j4, x_rows, z_cols] = add(zsum[a, place.z], *[zrecv[a, k - 1] for k in range(1, Z)])
            for k in place.z_order():
                zg_copy(j4, k).start()

        j5, ok5 = stage(1 + 4 * LAG)

        @pl.when(ok5)
        def _():
            for k in range(1, Z):
                zg_copy(j5, k).wait()
            xg_copy(j5).start()

        j6, ok6 = stage(1 + 5 * LAG)

        @pl.when(ok6)
        def _():
            xg_copy(j6).wait()
            for_store(j6, lambda copy: copy.start())

        j7, ok7 = stage(2 + 5 * LAG)

        @pl.when(ok7)
        def _():
            for_store(j7, lambda copy: copy.wait())

    def produce(i, left, offset, cols):
        slot = lax.rem(i, 2)
        for turn in range(2):
            c = 1 - place.c if turn == 0 else place.c
            for y in range(Y):
                first = offset(place.part(y, c))
                if CB % 128 == 0:
                    first = pl.multiple_of(first, 128)
                    value = matmul(left[:, pl.ds(first, CB)], cols, ((0,), (0,))).astype(BF)
                else:
                    start = pl.multiple_of(lax.div(first, 128) * 128, 128)
                    ref.tile[...] = matmul(left[:, pl.ds(start, 128)], cols, ((0,), (0,)))
                    value = ref.tile[pl.ds(pl.multiple_of(first - start, CB), CB)].astype(BF)
                part[slot, c, y] = value
            if turn == 0:
                core_copy(i).start()

    def columns(array, n):
        return array[:, pl.ds(pl.multiple_of(n * CW, CW), CW)]

    acc, gmid, act, slope = ref.acc, ref.gmid, ref.act_s, ref.slope_s
    spread = []
    for b in range(n_blocks):
        start = spread[-1][1] if spread else done[1]
        goal, over = need[min(b + 1, n_blocks - 1)]
        soon = need[min(b + 2, n_blocks - 1)][1]
        spread.append((start, min(max(goal + 4, start + 2), last_step), over, soon))

    def block_step(b, _):
        slot = lax.rem(b, 2)
        for copy in block_loads(b):
            copy.wait()

        for at, (_, stop, over, soon) in enumerate(spread):
            @pl.when(b == at)
            def _(at=at, stop=stop, over=over, soon=soon):
                gather_x(stop, 5)
                for h in range(spread[at - 1][2] if at else need[0][1], over):
                    if at == 0:
                        direct_step(h)
                    direct_arrived(h)
                for h in range(spread[at - 1][3] if at else over, soon):
                    direct_step(h)

        @pl.when(b + 1 < n_blocks)
        def _():
            for copy in block_loads(b + 1):
                copy.start()

        spots = []
        for p in range(shards):
            row, col = UP_B + p * down_rows // W, p * down_rows % W
            spots.append((slice(row, row + 1), pl.ds(pl.multiple_of(col + b * BW, BW), BW)))
        bias = jnp.concatenate([vec[spot] for spot in spots], axis=1)
        for t in range(rows // MT):
            tile = slice(t * MT, (t + 1) * MT)
            hidden = matmul(second[tile, :], ref.wu[slot]) + bias
            gate = 0.5 * (1.0 + lax.erf(hidden * (0.5**0.5)))
            act[tile, :] = (hidden * gate).astype(BF)
            bell = jnp.exp(-0.5 * hidden * hidden) * 0.3989422804014327
            slope[tile, :] = gate + hidden * bell

        def chunk(n):
            r, c = n // (W // CW), n % (W // CW)
            produce(b * per_block + n, act, lambda p: p * BW + r * CB, columns(gfeed, c))
            tick(b * per_block + n)

        chunk(0)
        sums = [0.0] * shards
        for t in range(rows // MT):
            tile = slice(t * MT, (t + 1) * MT)
            pre = (matmul(gfeed[tile, :], ref.wd[slot], ((1,), (1,))) * slope[tile, :]).astype(BF)
            for p in range(shards):
                mid = pre[:, p * BW : (p + 1) * BW]
                gpre[tile, pl.ds(pl.multiple_of(p * down_rows + b * BW, BW), BW)] = mid
                sums[p] = sums[p] + jnp.sum(mid.astype(F32), axis=0, keepdims=True)
            more = matmul(pre, ref.wu[slot], ((1,), (1,)))
            feed = matmul(act[tile, :], ref.wd[slot])

            @pl.when(b == 0)
            def _():
                gmid[tile, :] = more
                acc[tile, :] = feed

            @pl.when(b > 0)
            def _():
                gmid[tile, :] += more
                acc[tile, :] += feed

            if t == 0:
                for n in range(1, per_block):
                    chunk(n)
        for p in range(shards):
            row, cols = spots[p]
            small[row, cols] = sums[p]
        return 0

    lax.fori_loop(0, n_blocks, block_step, 0)

    tok_out, tok_send = ref.tok_out, ref.tok_send

    def to_owner(t, value, kept, given):
        if R >= TM:
            lower = pl.ds(pl.multiple_of(lax.rem(t * TM, R), TM), TM)

            @pl.when(t * TM < R)
            def _():
                kept[mine, lower, :] = value.astype(kept.dtype)

            @pl.when(t * TM >= R)
            def _():
                given[lower, :] = value.astype(BF)
        else:
            kept[mine] = value[:R].astype(kept.dtype)
            given[...] = value[R:].astype(BF)

    def middle_tile(t, _):
        tile = pl.ds(pl.multiple_of(t * TM, TM), TM)
        low = branch[tile, :]
        middle = x_s[tile, :].astype(F32) + vector(ATTN_SCALE) * low
        feed = acc[tile, :] + vector(DOWN_B)
        to_owner(t, (middle + vector(MLP_SCALE) * feed) * vector(LIVE), tok_out, tok_send)
        upstream = cot[tile, :].astype(F32) * vector(LIVE)
        note(MLP_SCALE, jnp.sum(upstream * feed, axis=0, keepdims=True))
        unit, scale = norm_parts(middle)
        grad = gmid[tile, :]
        note(MLP_GAIN, jnp.sum(grad * unit, axis=0, keepdims=True))
        note(MLP_SHIFT, jnp.sum(grad, axis=0, keepdims=True))
        grad = upstream + norm_back(grad, unit, scale, vector(MLP_GAIN))
        gmid[tile, :] = grad
        note(ATTN_SCALE, jnp.sum(grad * low, axis=0, keepdims=True))
        grad = (grad * vector(ATTN_SCALE)).astype(BF)
        gbranch[tile, :] = grad
        note(PROJ_B, jnp.sum(grad.astype(F32), axis=0, keepdims=True))
        gatt[tile, :] = matmul(grad, ref.proj_s[...], ((1,), (1,))).astype(BF)
        return 0

    def up_chunk(u):
        i = n_down + u
        b, n = lax.rem(u, blocks), lax.div(u, blocks)
        produce(i, second, lambda p: p * other_rows + b * CB, columns(gpre, n))
        tick(i)

    early_up = rows // TM if n_up >= 2 * pairs else 0

    def middle_step(t, _):
        if early_up:
            up_chunk(t)
        return middle_tile(t, 0)

    lax.fori_loop(0, rows // TM, middle_step, 0)
    tok_copy = send(tok_send, tok_out.at[mine], ref.ts.at[0], ref.tr.at[0], swap_peer)

    def qkv_load(n):
        slot = lax.rem(n, 2)
        return load(ref.g_qkv.at[:, pl.ds(pl.multiple_of(n * CW, CW), CW)], ref.wu.at[slot, :, pl.ds(0, CW)],
                    ref.qsem.at[slot])

    pown, psend, precv = ref.pown, ref.psend, ref.precv
    gk_acc, gv_acc = ref.gk_acc, ref.gv_acc

    def pair_copy(p, k):
        a = lax.rem(p, PAIR_SLOTS)
        return send(psend.at[a, k - 1], precv.at[a, k - 1], ref.ps.at[a, k - 1], ref.pr.at[a, k - 1],
                    half_peer(k))

    def pair_done(p):
        a = lax.rem(p, PAIR_SLOTS)
        for k in range(1, half):
            pair_copy(p, k).wait()
        for which in range(2):
            whole = pown[a, which]
            for k in range(1, half):
                whole = whole + precv[a, k - 1, which].astype(F32)
            cols = pl.ds(pl.multiple_of((which + 1) * W + p * 128, 128), 128)
            G[:, cols] = whole.astype(BF)

    per_pair = n_up // pairs

    def pair_step(p, _):
        if per_pair:
            for m in range(max(1, per_pair - tiles + 1)):
                @pl.when(p * per_pair + m >= early_up)
                def _(m=m):
                    up_chunk(p * per_pair + m)
        else:
            @pl.when(lax.rem(p, pairs // n_up) == 0)
            def _():
                up_chunk(lax.div(p, pairs // n_up))

        lane = lax.broadcasted_iota(jnp.int32, (1, 128), 1)
        cols = pl.ds(pl.multiple_of(p * 128, 128), 128)
        key, value = kv[0, :, cols], kv[1, :, cols]
        key_t = key.T
        for t in range(tiles):
            tile = slice(t * QT, (t + 1) * QT)
            own = both_heads(query[tile, cols] * BF(HEAD_DIM**-0.5), lane)
            own_grad = both_heads(gatt[tile, cols], lane)
            logs = jnp.concatenate([lse[p, :, tile], lse[p, :, rows + t * QT : rows + (t + 1) * QT]], axis=1)
            probs = jnp.exp(matmul(key, own, ((1,), (1,))) - logs)
            grad_probs = matmul(value, own_grad, ((1,), (1,)))
            centre = jnp.sum(grad_probs * probs, axis=0, keepdims=True)
            grad_scores = (probs * (grad_probs - centre)).astype(BF)
            gv = matmul(probs.astype(BF), own_grad)
            gk = matmul(grad_scores, own)
            if t == 0:
                gv_acc[...], gk_acc[...] = gv, gk
            else:
                gv_acc[...] += gv
                gk_acc[...] += gk
            G[tile, cols] = (own_heads(matmul(key_t, grad_scores)) * HEAD_DIM**-0.5).T.astype(BF)
            if per_pair and t < tiles - 1:
                u = p * per_pair + max(1, per_pair - tiles + 1) + t

                @pl.when(u >= early_up)
                def _(u=u):
                    up_chunk(u)
        a = lax.rem(p, PAIR_SLOTS)
        pown[a, 0], pown[a, 1] = gk_acc[:rows], gv_acc[:rows]
        for k in range(1, half):
            psend[a, k - 1, 0] = gk_acc[k * rows : (k + 1) * rows].astype(BF)
            psend[a, k - 1, 1] = gv_acc[k * rows : (k + 1) * rows].astype(BF)
            pair_copy(p, k).start()

        @pl.when(p >= 1)
        def _():
            pair_done(p - 1)
        return 0

    lax.fori_loop(0, pairs, pair_step, 0)

    qkv_load(0).start()

    def proj_step(u, _):
        i = n_down + n_up + u
        r, c = lax.div(u, W // CW), lax.rem(u, W // CW)
        produce(i, attended, lambda p: p * other_rows + r * CB, columns(gbranch, c))
        tick(i)

        @pl.when(u == 0)
        def _():
            pair_done(pairs - 1)
        return 0

    lax.fori_loop(0, n_proj, proj_step, 0)

    def qkv_step(n, _):
        cols = columns(G, n)
        for b in range(blocks):
            i = n_down + n_up + n_proj + n * blocks + b
            produce(i, first, lambda p: p * other_rows + b * CB, cols)
            tick(i)
            if b == 0:
                qkv_load(n).wait()

                @pl.when(n + 1 < 3 * W // CW)
                def _():
                    qkv_load(n + 1).start()

                for t in range(rows // MT):
                    tile = slice(t * MT, (t + 1) * MT)
                    term = matmul(cols[tile, :], ref.wu[lax.rem(n, 2), :, :CW], ((1,), (1,)))

                    @pl.when(n == 0)
                    def _():
                        acc[tile, :] = term

                    @pl.when(n > 0)
                    def _():
                        acc[tile, :] += term
        return 0

    lax.fori_loop(0, 3 * W // CW, qkv_step, 0)

    gt_out, gt_send, gt_recv = ref.gt_out, ref.gt_send, ref.gt_recv

    def first_tile(t, _):
        tile = pl.ds(pl.multiple_of(t * TM, TM), TM)
        unit, scale = norm_parts(x_s[tile, :].astype(F32))
        grad = acc[tile, :]
        note(ATTN_GAIN, jnp.sum(grad * unit, axis=0, keepdims=True))
        note(ATTN_SHIFT, jnp.sum(grad, axis=0, keepdims=True))
        note(QV, jnp.sum(G[tile, :W].astype(F32), axis=0, keepdims=True))
        note(QV + 1, jnp.sum(G[tile, 2 * W :].astype(F32), axis=0, keepdims=True))
        to_owner(t, gmid[tile, :] + norm_back(grad, unit, scale, vector(ATTN_GAIN)), gt_out, gt_send)
        return 0

    lax.fori_loop(0, rows // TM, first_tile, 0)

    cw = W // shards
    packs = ref.packs
    for p in range(shards):
        at = 0
        for row, count in SMALL_ROWS:
            for r in range(count):
                t = p * count + r
                line, col = row + t // shards, t % shards * cw
                packs[p % 2, p // 2, at : at + 1, :] = small[line : line + 1, col : col + cw]
                at += 1

    sums = ref.sums
    core_small = send(packs.at[1 - place.c], ref.core_pack, ref.ss.at[0], ref.sr.at[0], place.at(c=1 - place.c))
    y_small = [send(packs.at[place.c, place.ahead_y(k)], sums.at[0, k], ref.ss.at[k], ref.sr.at[k],
                    place.at(y=place.ahead_y(k))) for k in range(1, Y)]
    x_small = [send(sums.at[1, 0], sums.at[1, 1], ref.ss.at[Y], ref.sr.at[Y], place.at(x=1 - place.x))]
    z_small = [send(sums.at[2, 0], sums.at[2, k], ref.ss.at[Y + k], ref.sr.at[Y + k],
                    place.at(z=place.near_z(k))) for k in range(1, Z)]

    def small_step(step):
        if step == 0:
            core_small.wait()
            for y in range(Y):
                packs[place.c, y] = packs[place.c, y] + ref.core_pack[y]
            for copy in y_small:
                copy.start()
            return
        copies = (y_small, x_small, z_small)[step - 1]
        for copy in copies:
            copy.wait()
        whole = packs[place.c, place.y] if step == 1 else sums[step - 1, 0]
        for k in range(len(copies)):
            whole = whole + sums[step - 1, k + 1]
        if step < 3:
            sums[step, 0] = whole
            for copy in (x_small, z_small)[step - 1]:
                copy.start()
        else:
            ref.small_out[...] = whole

    core_small.start()
    gt_copy = send(gt_send, gt_recv, ref.ts.at[1], ref.tr.at[1], swap_peer)
    depth = 3 + 5 * LAG
    small_after = {0: 0, 2 + LAG: 1, 2 + 2 * LAG: 2, 2 + 3 * LAG: 3}
    for lag in range(depth):
        tick(total + lag)
        if lag in small_after:
            small_step(small_after[lag])
        if lag == 0:
            gt_copy.start()
            tok_copy.start()
    tok_copy.wait()
    gt_copy.wait()
    gt_out[1 - mine] = gt_recv[...].astype(F32)


def layer(replicas, shards, vectors, count, tokens, cotangent, weights):
    Y, Z, half = shards // 2, replicas // 2, shards // 2
    _, R, W = tokens.shape
    rows, keys = 2 * R, half * 2 * R
    FF = weights[UP].shape[1]
    CB, CW = min(128, W // shards), max(512, 128 * Z)
    HB, WZ = CB // 2, CW // Z
    total = (FF // shards // CB) * (W // CW) + (W // shards // CB) * ((FF + 4 * W) // CW)
    peers = max(Y, Z, 2)
    staged, direct, _ = gather_items(replicas, shards, W, FF)
    m = len(staged) + len(direct)
    multiples = tuple(v.shape[0] // (W // shards) for v in vectors)
    if (W // shards) % 128:
        vectors = [v.reshape(n, W // shards) for v, n in zip(vectors, multiples)]
    dma = pltpu.SemaphoreType.DMA
    vmem, anywhere = pl.BlockSpec(memory_space=pltpu.VMEM), pl.BlockSpec(memory_space=pl.ANY)
    inputs = dict(count=count, tokens=tokens, cotangent=cotangent, qkv=weights[QKV], proj=weights[PROJ],
                  up=weights[UP], down=weights[DOWN])
    scratch = dict(
        part=pltpu.VMEM((2, 2, Y, CB, CW), BF),
        crecv=pltpu.VMEM((CORE_SLOTS, Y, CB, CW), BF),
        ysum=pltpu.VMEM((SLOTS, Y, CB, CW), BF),
        yrecv=pltpu.VMEM((SLOTS, Y - 1, CB, CW), BF),
        xsum=pltpu.VMEM((SLOTS, 2, HB, CW), BF),
        xrecv=pltpu.VMEM((SLOTS, HB, CW), BF),
        zsum=pltpu.VMEM((SLOTS, Z, HB, WZ), BF),
        zrecv=pltpu.VMEM((SLOTS, Z - 1, HB, WZ), BF),
        out=pltpu.VMEM((total, CB, CW), BF),
        small_buf=pltpu.VMEM((16, W), F32),
        packs=pltpu.VMEM((2, Y, 16, W // shards), F32),
        core_pack=pltpu.VMEM((Y, 16, W // shards), F32),
        sums=pltpu.VMEM((3, peers, 16, W // shards), F32),
        kv=pltpu.VMEM((2, keys, W), BF),
        gpre=pltpu.VMEM((rows, FF), BF),
        act_s=pltpu.VMEM((rows, shards * BW), BF),
        slope_s=pltpu.VMEM((rows, shards * BW), F32),
        cot_s=pltpu.VMEM((rows, W), BF),
        gfeed=pltpu.VMEM((rows, W), BF),
        x_s=pltpu.VMEM((rows, W), BF),
        branch_s=pltpu.VMEM((rows, W), F32),
        second_s=pltpu.VMEM((rows, W), BF),
        attended_s=pltpu.VMEM((rows, W), BF),
        query_s=pltpu.VMEM((rows, W), BF),
        first_s=pltpu.VMEM((rows, W), BF),
        proj_s=pltpu.VMEM((W, W), BF),
        wd=pltpu.VMEM((2, shards * BW, W), BF),
        wu=pltpu.VMEM((2, W, shards * BW), BF),
        wq=pltpu.VMEM((W, CW), BF),
        acc=pltpu.VMEM((rows, W), F32),
        gmid=pltpu.VMEM((rows, W), F32),
        gbranch=pltpu.VMEM((rows, W), BF),
        gatt=pltpu.VMEM((rows, W), BF),
        G=pltpu.VMEM((rows, 3 * W), BF),
        pown=pltpu.VMEM((PAIR_SLOTS, 2, rows, 128), F32),
        psend=pltpu.VMEM((PAIR_SLOTS, half - 1, 2, rows, 128), BF),
        precv=pltpu.VMEM((PAIR_SLOTS, half - 1, 2, rows, 128), BF),
        gk_acc=pltpu.VMEM((keys, 128), F32),
        gv_acc=pltpu.VMEM((keys, 128), F32),
        tok_send=pltpu.VMEM((R, W), BF),
        gt_send=pltpu.VMEM((R, W), BF),
        gt_recv=pltpu.VMEM((R, W), BF),
        small_s=pltpu.VMEM((shards, 16, W // shards), F32),
        vec=pltpu.VMEM((16, W), F32),
        lse=pltpu.VMEM((W // 128, 1, 2 * rows), F32),
        lsem=dma((12,)), wsem=dma((2, 2, shards)), qsem=dma((3,)), osem=dma((SLOTS,)),
        gys=dma((m, Y - 1)), gyr=dma((m, Y - 1)),
        gzs=dma((m, Y - 1, Z - 1)), gzr=dma((m, Y - 1, Z - 1)),
        gxs=dma((m, Y - 1)), gxr=dma((m, Y - 1)),
        gcs=dma((m, Y - 1)), gcr=dma((m, Y - 1)),
        os=dma((4,)), orr=dma((4,)),
        vs=dma((shards - 1,)), vr=dma((shards - 1,)),
        ks=dma((2, W // CW, half - 1)), kr=dma((2, W // CW, half - 1)),
        cs=dma((CORE_SLOTS,)), cr=dma((CORE_SLOTS,)),
        ys=dma((SLOTS, Y - 1)), yr=dma((SLOTS, Y - 1)),
        xs=dma((SLOTS,)), xr=dma((SLOTS,)),
        zs=dma((SLOTS, Z - 1)), zr=dma((SLOTS, Z - 1)),
        gs=dma((SLOTS, Z - 1)), gr=dma((SLOTS, Z - 1)),
        hs=dma((SLOTS,)), hr=dma((SLOTS,)),
        ps=dma((PAIR_SLOTS, half - 1)), pr=dma((PAIR_SLOTS, half - 1)),
        ss=dma((Y + Z,)), sr=dma((Y + Z,)),
        ts=dma((4,)), tr=dma((4,)),
    )
    if CB % 128:
        scratch["tile"] = pltpu.VMEM((128, CW), F32)
    outs = dict(
        o_down=jax.ShapeDtypeStruct((FF // shards, W), BF),
        o_up=jax.ShapeDtypeStruct((W // shards, FF), BF),
        o_proj=jax.ShapeDtypeStruct((W // shards, W), BF),
        o_qkv=jax.ShapeDtypeStruct((W // shards, 3 * W), BF),
        small_out=jax.ShapeDtypeStruct((16, W // shards), F32),
        tok_out=jax.ShapeDtypeStruct((2, R, W), BF),
        gt_out=jax.ShapeDtypeStruct((2, R, W), F32),
        g_qkv=jax.ShapeDtypeStruct((W, 3 * W), BF),
        g_proj=jax.ShapeDtypeStruct((W, W), BF),
        g_up=jax.ShapeDtypeStruct((W, FF), BF),
        g_down=jax.ShapeDtypeStruct((FF, W), BF),
    )
    names = tuple(inputs) + tuple(outs) + tuple(scratch)
    results = pl.pallas_call(
        functools.partial(layer_kernel, replicas, shards, multiples, names),
        in_specs=[vmem] * len(vectors) + [pl.BlockSpec(memory_space=pltpu.SMEM)] + [anywhere] * 6,
        out_specs=[anywhere] * 4 + [vmem] * 3 + [anywhere] * 4,
        out_shape=list(outs.values()),
        scratch_shapes=list(scratch.values()),
        compiler_params=pltpu.CompilerParams(
            collective_id=0, has_side_effects=True, vmem_limit_bytes=63 * MIB
        ),
    )(*vectors, *inputs.values())
    return results[:7]


def result_kernel(shards, n_vectors, *refs):
    small, *ins = refs[:7]
    outs = refs[7:13]
    vectors = refs[13 : 13 + n_vectors]
    low, wide, tok_s, gt_s, in_sem, out_sem = refs[13 + n_vectors :]
    size, width = low.shape[1:]
    blocks = []
    for source, target in zip(ins[2:], outs[2:]):
        for r in range(source.shape[0] // size):
            for c in range(source.shape[1] // width):
                at = (pl.ds(r * size, size), pl.ds(c * width, width))
                blocks.append((source.at[at], target.at[at]))
    n = len(blocks)
    loads = [pltpu.make_async_copy(src, low.at[i], in_sem.at[i]) for i, (src, _) in enumerate(blocks)]
    stores = [pltpu.make_async_copy(wide.at[i], dst, out_sem.at[i]) for i, (_, dst) in enumerate(blocks)]
    for i, (source, middle, target) in enumerate(((ins[0], tok_s, outs[0]), (ins[1], gt_s, outs[1]))):
        loads.append(pltpu.make_async_copy(source, middle, in_sem.at[n + i]))
        stores.append(pltpu.make_async_copy(middle, target, out_sem.at[n + i]))
    for copy in loads:
        copy.start()
    at = 0
    for (_, count), vector in zip(SMALL_ROWS, vectors):
        pieces = [small[at + r : at + r + 1, :] for r in range(count)]
        vector[...] = jnp.concatenate(pieces, axis=1).reshape(vector.shape)
        at += count
    for i in range(n + 2):
        loads[i].wait()
        if i < n:
            wide[i] = low[i].astype(F32)
        stores[i].start()
    for copy in stores:
        copy.wait()


def results(shards, small, tok, gt, grads):
    _, R, W = tok.shape
    size = W // shards
    count = sum(grad.shape[0] * grad.shape[1] for grad in grads) // (size * W)
    vmem, anywhere = pl.BlockSpec(memory_space=pltpu.VMEM), pl.BlockSpec(memory_space=pl.ANY)
    shapes = [jax.ShapeDtypeStruct(tok.shape, BF), jax.ShapeDtypeStruct(gt.shape, F32)]
    shapes += [jax.ShapeDtypeStruct(grad.shape, F32) for grad in grads]
    n_vectors = len(SMALL_ROWS) if size % 128 == 0 else 0
    for _, rows in SMALL_ROWS[:n_vectors]:
        shapes.append(jax.ShapeDtypeStruct((rows * size,), F32))
    dma = pltpu.SemaphoreType.DMA
    tok, gt, *rest = pl.pallas_call(
        functools.partial(result_kernel, shards, n_vectors),
        in_specs=[vmem] + [anywhere] * 6,
        out_specs=[anywhere] * 6 + [vmem] * n_vectors,
        out_shape=shapes,
        scratch_shapes=[
            pltpu.VMEM((count, size, W), BF), pltpu.VMEM((count, size, W), F32),
            pltpu.VMEM(tok.shape, BF), pltpu.VMEM(gt.shape, F32), dma((count + 2,)), dma((count + 2,)),
        ],
        compiler_params=pltpu.CompilerParams(vmem_limit_bytes=63 * MIB),
    )(small, tok, gt, *grads)
    vectors = rest[4:]
    if not n_vectors:
        at = 0
        for _, rows in SMALL_ROWS:
            vectors.append(small[at : at + rows].reshape(-1))
            at += rows
    return tok, gt, rest[:4], vectors


def on_device(replicas, shards, tokens, qkv_weight, qv_bias, proj_weight, proj_bias, up_weight, up_bias,
              down_weight, down_bias, attn_gain, attn_shift, mlp_gain, mlp_shift, attn_scale, mlp_scale,
              cotangent, image_count):
    vectors = (qv_bias, proj_bias, up_bias, down_bias, attn_gain, attn_shift, mlp_gain, mlp_shift,
               attn_scale, mlp_scale)
    *grads, small, output, grad_tokens = layer(
        replicas, shards, vectors, image_count, tokens, cotangent,
        (qkv_weight, proj_weight, up_weight, down_weight),
    )
    output, grad_tokens, (down, up, proj, qkv), small = results(shards, small, output, grad_tokens, grads)
    qv_b, proj_b, up_b, down_b, *norms = small
    return (output, grad_tokens, qkv, qv_b, proj, proj_b, up, up_b, down, down_b, *norms)


def solution(mesh):
    rows, vector = P("shard", None), P("shard")
    image = P("replica", "shard", None)
    in_specs = (image, rows, vector, rows, vector, rows, vector, rows, vector, vector, vector, vector,
                vector, vector, vector, image, P())
    out_specs = (image, image, rows, vector, rows, vector, rows, vector, rows, vector, vector, vector,
                 vector, vector, vector, vector)
    return jax.shard_map(
        functools.partial(on_device, mesh.shape["replica"], mesh.shape["shard"]),
        mesh=mesh, in_specs=in_specs, out_specs=out_specs, check_vma=False,
    )
```

```python
import functools
import types

import jax
import jax.numpy as jnp
from jax import lax
from jax.experimental import pallas as pl
from jax.experimental.pallas import tpu as pltpu
from jax.sharding import PartitionSpec as P

HEAD_DIM = 64
EPS = 1e-06
BF = jnp.bfloat16
F32 = jnp.float32
MESH = pl.DeviceIdType.MESH
MIB = 1024 * 1024
SLOTS = 6
PAIR_SLOTS = 4
CORE_SLOTS = 4
LAG = 2


def matmul(left, right, dims=((1,), (0,))):
    return lax.dot_general(left, right, (dims, ((), ())), preferred_element_type=F32)


class Place:
    def __init__(self, replicas, shards):
        self.Z, self.Y = replicas // 2, shards // 2
        self.shards = shards
        replica, shard = lax.axis_index("replica"), lax.axis_index("shard")
        self.x, self.z = lax.rem(replica, 2), lax.div(replica, 2)
        self.c, self.y = lax.rem(shard, 2), lax.div(shard, 2)
        self.s = shard

    def part(self, y, c):
        return y * 2 + c

    def at(self, x=None, z=None, y=None, c=None):
        x = self.x if x is None else x
        z = self.z if z is None else z
        y = self.y if y is None else y
        c = self.c if c is None else c
        return (z * 2 + x, y * 2 + c)

    def near_z(self, k):
        z, bit = self.z, 1
        while bit < self.Z:
            if k & bit:
                z = z + bit - 2 * bit * lax.rem(lax.div(z, bit), 2)
            bit *= 2
        return z

    def z_order(self):
        return sorted(range(1, self.Z), key=lambda k: (-(k.bit_length()), k))

    def ahead_y(self, k):
        return lax.rem(self.y + k, self.Y)

    def behind_y(self, k):
        return lax.rem(self.y + self.Y - k, self.Y)

    def greet(self, extra=()):
        others = [self.at(c=1 - self.c), self.at(x=1 - self.x)]
        others += [self.at(y=self.ahead_y(k)) for k in range(1, self.Y)]
        others += [self.at(z=self.near_z(k)) for k in range(1, self.Z)]
        others += list(extra)
        barrier = pltpu.get_barrier_semaphore()
        for other in others:
            pl.semaphore_signal(barrier, inc=1, device_id=other, device_id_type=MESH)
        pl.semaphore_wait(barrier, len(others))


def send(src, dst, send_sem, recv_sem, device):
    return pltpu.make_async_remote_copy(
        src_ref=src,
        dst_ref=dst,
        send_sem=send_sem,
        recv_sem=recv_sem,
        device_id=device,
        device_id_type=MESH,
    )


QV, PROJ_B, UP_B, DOWN_B, ATTN_GAIN, ATTN_SHIFT, MLP_GAIN, MLP_SHIFT, ATTN_SCALE, MLP_SCALE, LIVE = (
    0, 2, 3, 7, 8, 9, 10, 11, 12, 13, 14)
SMALL_ROWS = ((QV, 2), (PROJ_B, 1), (UP_B, 4), (DOWN_B, 1), (ATTN_GAIN, 1), (ATTN_SHIFT, 1), (MLP_GAIN, 1),
              (MLP_SHIFT, 1), (ATTN_SCALE, 1), (MLP_SCALE, 1))
QKV, PROJ, UP, DOWN = range(4)


def norm_parts(values):
    centre = values - jnp.mean(values, axis=-1, keepdims=True)
    scale = lax.rsqrt(jnp.mean(centre * centre, axis=-1, keepdims=True) + EPS)
    return centre * scale, scale


def norm_back(grad, unit, scale, gain):
    inner = grad * gain
    return scale * (
        inner
        - jnp.mean(inner, axis=-1, keepdims=True)
        - unit * jnp.mean(inner * unit, axis=-1, keepdims=True)
    )


BW = 128


FIRST = 6
TAIL = 4
EARLY = 2
PACE = (5, 6, 7, 8, 9, 10, 11, 12, 14)


def gather_items(replicas, shards, width, hidden):
    Z = replicas // 2
    step = max(512, 128 * Z)
    size, down = width // shards, hidden // shards
    halves = width // step
    items = [(QKV, 0, size, n * width + h * step, step) for h in range(halves) for n in (1, 2, 0)]
    items += [(PROJ, 0, size, h * step, step) for h in range(halves)]
    upto, known = [], set()
    for b in range(down // BW):
        for p in range(shards):
            c = (p * down + b * BW) // step
            if c not in known:
                known.add(c)
                items.append((UP, 0, size, c * step, step))
        items.append((DOWN, b * BW, BW, 0, width))
        upto.append(len(items))
    straight = set(range(len(items) - TAIL, len(items)))
    straight |= set(range(upto[0] - EARLY, upto[0]))
    staged = [item for n, item in enumerate(items) if n not in straight]
    direct = [item for n, item in enumerate(items) if n in straight]
    need = []
    for n in upto:
        over = len([m for m in straight if m < n])
        need.append((n - over, over))
    return staged, direct, need


def layer_kernel(replicas, shards, multiples, names, *refs):
    vector_refs, refs = refs[: len(multiples)], refs[len(multiples) :]
    ref = types.SimpleNamespace(**dict(zip(names, refs)))
    place = Place(replicas, shards)
    Y, Z, s = place.Y, place.Z, place.s
    half = shards // 2
    part, crecv, ysum, yrecv = ref.part, ref.crecv, ref.ysum, ref.yrecv
    xsum, xrecv, zsum, zrecv = ref.xsum, ref.xrecv, ref.zsum, ref.zrecv
    out, small, vec, lse = ref.out, ref.small_buf, ref.vec, ref.lse
    CB, CW = part.shape[3], part.shape[4]
    rows, W = ref.gfeed.shape
    R = rows // 2
    keys = half * rows
    FF = ref.gpre.shape[1]
    down_rows, other_rows = FF // shards, W // shards
    n_blocks, blocks = down_rows // BW, other_rows // CB
    per_block = (BW // CB) * (W // CW)
    n_down, n_up = n_blocks * per_block, blocks * (FF // CW)
    n_proj, n_qkv = blocks * (W // CW), blocks * (3 * W // CW)
    total = n_down + n_up + n_proj + n_qkv
    mine = lax.div(s, half)
    j_half = lax.rem(s, half)
    replica = lax.axis_index("replica")
    kv, gpre, cot, gfeed, G = ref.kv, ref.gpre, ref.cot_s, ref.gfeed, ref.G
    second, first, query, x_s = ref.second_s, ref.first_s, ref.query_s, ref.x_s
    attended, branch, gbranch, gatt = ref.attended_s, ref.branch_s, ref.gbranch, ref.gatt
    TR, MT, QT, TM = min(128, R), min(256, rows), min(256, rows), min(256, R)
    pairs, tiles = W // 128, rows // QT

    def half_peer(k):
        return (replica, mine * half + lax.rem(j_half + k, half))

    swap_peer = (replica, lax.rem(s + half, shards))

    def load(src, dst, sem):
        return pltpu.make_async_copy(src, dst, sem)

    sources = (ref.qkv, ref.proj, ref.up, ref.down)
    weights = (ref.g_qkv, ref.g_proj, ref.g_up, ref.g_down)
    sizes = [source.shape[0] for source in sources]
    bounce = (G, gbranch, gpre, ref.proj_s)

    def own_rows(w):
        return weights[w].at[pl.ds(pl.multiple_of(s * sizes[w], sizes[w]), sizes[w])]

    own_loads = [load(sources[w], bounce[w].at[pl.ds(0, sizes[w])], ref.lsem.at[w]) for w in range(4)]
    own_stores = [load(bounce[w].at[pl.ds(0, sizes[w])], own_rows(w), ref.lsem.at[4 + w]) for w in range(4)]
    x_load = load(ref.tokens.at[mine], x_s.at[pl.ds(0, R)], ref.lsem.at[8])
    cot_load = load(ref.cotangent.at[mine], cot.at[pl.ds(0, R)], ref.lsem.at[9])
    x_load.start()
    for copy in own_loads:
        copy.start()
    cot_load.start()
    row = 0
    for vector_ref, count in zip(vector_refs, multiples):
        values = vector_ref[...].astype(F32).reshape(count, ref.small_s.shape[2])
        ref.small_s[s, row : row + count, :] = values
        row += count
    place.greet([(replica, lax.rem(s + k, shards)) for k in range(1, shards)])

    staged, direct, need = gather_items(replicas, shards, W, FF)
    items = staged + direct
    n_staged = len(staged)

    def piece(m, owner, whole_rows, whole_cols):
        w, row, size, col, width = items[m]
        at, cols = owner * sizes[w] + row, pl.ds(col, width)
        if not whole_rows:
            size //= 2
            at = at + place.x * size
        if not whole_cols:
            if size % (16 * Z):
                cols = pl.ds(pl.multiple_of(col + place.z * (width // Z), 128), width // Z)
            else:
                size //= Z
                at = at + place.z * size
        return pl.ds(pl.multiple_of(at, 16), size), cols

    def gy_copy(m, k):
        w, whole = items[m][0], m >= n_staged
        return send(sources[w].at[piece(m, 0, whole, whole)], weights[w].at[piece(m, s, whole, whole)],
                    ref.gys.at[m, k - 1], ref.gyr.at[m, k - 1], place.at(y=place.ahead_y(k)))

    def gathered(m, k, whole_rows, whole_cols):
        owner = place.part(place.behind_y(k), place.c)
        return weights[items[m][0]].at[piece(m, owner, whole_rows, whole_cols)]

    def gz_copy(m, k, j):
        b = gathered(m, k, False, False)
        return send(b, b, ref.gzs.at[m, k - 1, j - 1], ref.gzr.at[m, k - 1, j - 1],
                    place.at(z=place.near_z(j)))

    def gx_copy(m, k):
        b = gathered(m, k, False, True)
        return send(b, b, ref.gxs.at[m, k - 1], ref.gxr.at[m, k - 1], place.at(x=1 - place.x))

    def gc_copy(m, k):
        b = gathered(m, k, True, True)
        return send(b, b, ref.gcs.at[m, k - 1], ref.gcr.at[m, k - 1], place.at(c=1 - place.c))

    def gy_start(m):
        for k in range(1, Y):
            gy_copy(m, k).start()

    def direct_arrived(h):
        for k in range(1, Y):
            gy_copy(n_staged + h, k).wait()
            gc_copy(n_staged + h, k).start()

    def arrived(m):
        for k in range(1, Y):
            gc_copy(m, k).wait()

    halves = W // CW
    early = 3 * halves

    done = [0, 0, 0, 0]

    def gather_z(n):
        for m in range(done[0], min(n, n_staged)):
            for k in range(1, Y):
                gy_copy(m, k).wait()
                for j in place.z_order():
                    gz_copy(m, k, j).start()
            done[0] = m + 1

    def gather_x(n):
        gather_z(n)
        for m in range(done[1], min(n, n_staged)):
            for k in range(1, Y):
                for j in range(1, Z):
                    gz_copy(m, k, j).wait()
                gx_copy(m, k).start()
            done[1] = m + 1

    def gather_c(n):
        gather_x(n)
        for m in range(done[2], min(n, n_staged)):
            for k in range(1, Y):
                gx_copy(m, k).wait()
                gc_copy(m, k).start()
            done[2] = m + 1

    def gather_until(n):
        gather_c(n)
        for m in range(done[3], min(n, n_staged)):
            for k in range(1, Y):
                gc_copy(m, k).wait()
            done[3] = m + 1

    def gather_step(n):
        gather_c(n - 3)
        gather_x(n)
        gather_z(n + 3)
        gather_until(n - 5)

    def direct_step(h):
        for k in range(1, Y):
            gy_copy(n_staged + h, k).wait()
            gc_copy(n_staged + h, k).start()

    def direct_arrived(h):
        for k in range(1, Y):
            gc_copy(n_staged + h, k).wait()

    x_swap = send(ref.tokens.at[1 - mine], x_s.at[pl.ds(R, R)], ref.ts.at[2], ref.tr.at[2], swap_peer)
    cot_swap = send(ref.cotangent.at[1 - mine], cot.at[pl.ds(R, R)], ref.ts.at[3], ref.tr.at[3], swap_peer)
    small_sends = [
        send(ref.small_s.at[s], ref.small_s.at[s], ref.vs.at[k - 1], ref.vr.at[k - 1],
             (replica, lax.rem(s + k, shards)))
        for k in range(1, shards)
    ]
    own_sends = [send(sources[w], own_rows(w), ref.os.at[w], ref.orr.at[w], place.at(c=1 - place.c))
                 for w in range(4)]
    for copy in small_sends:
        copy.start()
    for m in range(min(FIRST, n_staged)):
        gy_start(m)
    x_swap.start()
    for m in range(FIRST, n_staged):
        gy_start(m)
    for copy in own_sends:
        copy.start()

    gather_z(3)

    for copy in small_sends:
        copy.wait()
    vec[...] = jnp.zeros_like(vec)
    row = 0
    for count in multiples:
        pieces = [ref.small_s[p, row + r : row + r + 1, :] for p in range(shards) for r in range(count)]
        for r in range(count):
            vec[row + r : row + r + 1, :] = jnp.concatenate(pieces[r * shards : (r + 1) * shards], axis=1)
        row += count
    live = (mine < ref.count[replica]).astype(F32)
    vec[LIVE : LIVE + 1, :] = jnp.full((1, W), live, F32)

    def vector(row):
        return vec[row : row + 1, :]

    def note(row, value):
        small[row : row + 1, :] += value

    def norm_tile(t, _):
        tile = pl.ds(pl.multiple_of(t * TR, TR), TR)
        unit, _ = norm_parts(x_s[tile, :].astype(F32))
        first[tile, :] = (unit * vector(ATTN_GAIN) + vector(ATTN_SHIFT)).astype(BF)
        return 0

    x_load.wait()
    lax.fori_loop(0, R // TR, norm_tile, 0)
    for w in range(4):
        own_loads[w].wait()
        own_stores[w].start()
    for m in range(3):
        gather_x(m + 1)
        gather_z(m + 4)
        gather_c(m)
    x_swap.wait()
    lax.fori_loop(R // TR, rows // TR, norm_tile, 0)
    own_stores[QKV].wait()
    own_sends[QKV].wait()

    def kv_copy(which, h, k):
        cols = pl.ds(h * CW, CW)
        return send(kv.at[which, pl.ds(0, rows), cols], kv.at[which, pl.ds((half - k) * rows, rows), cols],
                    ref.ks.at[which, h, k - 1], ref.kr.at[which, h, k - 1], half_peer(k))

    def qkv_slot(slot):
        if slot < 2:
            return ref.wu[slot, :, :CW]
        return ref.wq[...]

    def qkv_tile(n, h, slot):
        target = ref.wu.at[slot, :, pl.ds(0, CW)] if slot < 2 else ref.wq
        return load(ref.g_qkv.at[:, pl.ds(n * W + h * CW, CW)], target, ref.qsem.at[slot])

    def project(h, ready):
        here = slice(h * CW, (h + 1) * CW)
        tile_loads = [qkv_tile(1, h, 0), qkv_tile(2, h, 1), qkv_tile(0, h, 2)]
        for n in range(2):
            ready(n)
            tile_loads[n].start()
        for n in range(3):
            if n == 1:
                ready(2)
                tile_loads[2].start()
            tile_loads[n].wait()
            for t in range(rows // MT):
                tile = slice(t * MT, (t + 1) * MT)
                value = matmul(first[tile, :], qkv_slot(n))
                if n == 0:
                    kv[0, tile, here] = value.astype(BF)
                elif n == 1:
                    kv[1, tile, here] = (value + vector(QV + 1)[:, here]).astype(BF)
                else:
                    query[tile, here] = (value + vector(QV)[:, here]).astype(BF)
            if n < 2:
                for k in range(1, half):
                    kv_copy(n, h, k).start()

    def exchanged(h):
        for which in range(2):
            for k in range(1, half):
                kv_copy(which, h, k).wait()

    def first_ready(n):
        gather_until(n + 1)
        if n == 1:
            gather_x(4)
        elif n == 2:
            gather_z(8)
            gather_x(5)

    project(0, first_ready)
    cot_swap.start()
    for h in range(len(direct)):
        gy_start(n_staged + h)

    plan = {}

    def at_pair(p, act):
        plan.setdefault(p, []).append(act)

    for p in range(1, pairs):
        at_pair(p, lambda p=p: gather_step(PACE[p]))
    if halves > 1:
        def second_half():
            gather_until(early)
            project(1, lambda n: None)

        at_pair(pairs // 2 - 1, second_half)
        at_pair(pairs // 2, lambda: exchanged(1))

    proj_load = load(ref.g_proj, ref.proj_s, ref.lsem.at[10])

    def proj_ready():
        gather_until(early + halves)
        own_stores[PROJ].wait()
        own_stores[DOWN].wait()
        own_sends[PROJ].wait()
        proj_load.start()

    at_pair(pairs - 1, proj_ready)
    gather_step(PACE[0])
    exchanged(0)

    def both_heads(array, lane):
        return jnp.concatenate([jnp.where(lane < HEAD_DIM, array, BF(0)), jnp.where(lane >= HEAD_DIM, array, BF(0))])

    def own_heads(array):
        n = array.shape[1] // 2
        return jnp.concatenate([array[:HEAD_DIM, :n], array[HEAD_DIM:, n:]])

    def attend(p, _):
        for at in sorted(plan):
            @pl.when(p == at)
            def _(at=at):
                for act in plan[at]:
                    act()

        lane = lax.broadcasted_iota(jnp.int32, (1, 128), 1)
        cols = pl.ds(pl.multiple_of(p * 128, 128), 128)
        key, value_t = kv[0, :, cols], kv[1, :, cols].T
        scores = matmul(key, both_heads(query[:, cols] * BF(HEAD_DIM**-0.5), lane), ((1,), (1,)))
        highest = jnp.max(scores, axis=0, keepdims=True)
        expos = jnp.exp(scores - highest)
        denom = jnp.sum(expos, axis=0, keepdims=True)
        probs = (expos * (1.0 / denom)).astype(BF)
        lse[p] = highest + jnp.log(denom)
        attended[:, cols] = own_heads(matmul(value_t, probs)).T.astype(BF)
        return 0

    lax.fori_loop(0, pairs, attend, 0)

    cot_load.wait()
    cot_swap.wait()
    small[...] = jnp.zeros_like(small)

    def feed_tile(t, _):
        tile = pl.ds(pl.multiple_of(t * TR, TR), TR)
        value = (cot[tile, :].astype(F32) * vector(LIVE) * vector(MLP_SCALE)).astype(BF)
        gfeed[tile, :] = value
        note(DOWN_B, jnp.sum(value.astype(F32), axis=0, keepdims=True))
        return 0

    lax.fori_loop(0, rows // TR, feed_tile, 0)
    proj_load.wait()
    gather_step(PACE[-1])

    for w in (UP, DOWN):
        own_sends[w].wait()
    own_stores[UP].wait()

    def block_loads(b):
        slot = lax.rem(b, 2)
        copies = []
        for p in range(shards):
            at = pl.ds(pl.multiple_of(p * down_rows + b * BW, BW), BW)
            to = pl.ds(p * BW, BW)
            copies.append(load(ref.g_up.at[:, at], ref.wu.at[slot, :, to], ref.wsem.at[0, slot, p]))
            copies.append(load(ref.g_down.at[at], ref.wd.at[slot, to], ref.wsem.at[1, slot, p]))
        return copies

    gather_until(need[0][0])
    for h in range(need[0][1]):
        direct_step(h)
        direct_arrived(h)
    for copy in block_loads(0):
        copy.start()

    def branch_tile(t, _):
        tile = pl.ds(pl.multiple_of(t * MT, MT), MT)
        low = matmul(attended[tile, :], ref.proj_s[...]) + vector(PROJ_B)
        branch[tile, :] = low
        unit, _ = norm_parts(x_s[tile, :].astype(F32) + vector(ATTN_SCALE) * low)
        second[tile, :] = (unit * vector(MLP_GAIN) + vector(MLP_SHIFT)).astype(BF)
        return 0

    lax.fori_loop(0, rows // MT, branch_tile, 0)
    def core_copy(i):
        a = lax.rem(i, CORE_SLOTS)
        return send(part.at[lax.rem(i, 2), 1 - place.c], crecv.at[a], ref.cs.at[a], ref.cr.at[a],
                    place.at(c=1 - place.c))

    def y_copy(i, k):
        a = lax.rem(i, SLOTS)
        return send(ysum.at[a, place.ahead_y(k)], yrecv.at[a, k - 1], ref.ys.at[a, k - 1],
                    ref.yr.at[a, k - 1], place.at(y=place.ahead_y(k)))

    def x_copy(i):
        a = lax.rem(i, SLOTS)
        return send(xsum.at[a, 1 - place.x], xrecv.at[a], ref.xs.at[a], ref.xr.at[a],
                    place.at(x=1 - place.x))

    def z_copy(i, k):
        a = lax.rem(i, SLOTS)
        return send(zsum.at[a, place.near_z(k)], zrecv.at[a, k - 1], ref.zs.at[a, k - 1],
                    ref.zr.at[a, k - 1], place.at(z=place.near_z(k)))

    HB, WZ = CB // 2, CW // Z
    x_rows = pl.ds(pl.multiple_of(place.x * HB, HB), HB)
    z_cols = pl.ds(pl.multiple_of(place.z * WZ, WZ), WZ)

    def zg_copy(i, k):
        a = lax.rem(i, SLOTS)
        block = out.at[i, x_rows, z_cols]
        return send(block, block, ref.gs.at[a, k - 1], ref.gr.at[a, k - 1],
                    place.at(z=place.near_z(k)))

    def xg_copy(i):
        a = lax.rem(i, SLOTS)
        block = out.at[i, x_rows]
        return send(block, block, ref.hs.at[a], ref.hr.at[a], place.at(x=1 - place.x))

    def for_store(i, act):
        a = lax.rem(i, SLOTS)
        base = 0
        plan = ((ref.o_down, n_down, False), (ref.o_up, n_up, True), (ref.o_proj, n_proj, False),
                (ref.o_qkv, n_qkv, True))
        for target, count, rows_first in plan:
            u = i - base
            if rows_first:
                r, c = lax.rem(u, blocks), lax.div(u, blocks)
            else:
                r, c = lax.div(u, W // CW), lax.rem(u, W // CW)
            at = (pl.ds(pl.multiple_of(r * CB, CB), CB), pl.ds(pl.multiple_of(c * CW, CW), CW))

            @pl.when((u >= 0) & (u < count))
            def _(target=target, at=at):
                act(load(out.at[i], target.at[at], ref.osem.at[a]))

            base += count

    def add(*terms):
        if len(terms) == 2:
            return terms[0] + terms[1]
        whole = terms[0].astype(F32)
        for term in terms[1:]:
            whole = whole + term.astype(F32)
        return whole.astype(BF)

    def tick(i):
        def stage(lag):
            j = i - lag
            return j, (j >= 0) & (j < total)

        j1, ok1 = stage(1)

        @pl.when(ok1)
        def _():
            core_copy(j1).wait()
            a = lax.rem(j1, SLOTS)
            for y in range(Y):
                ysum[a, y] = add(part[lax.rem(j1, 2), place.c, y], crecv[lax.rem(j1, CORE_SLOTS), y])
            for k in range(1, Y):
                y_copy(j1, k).start()

        j2, ok2 = stage(1 + LAG)

        @pl.when(ok2)
        def _():
            a = lax.rem(j2, SLOTS)
            for k in range(1, Y):
                y_copy(j2, k).wait()
            for h in range(2):
                piece = slice(h * HB, (h + 1) * HB)
                xsum[a, h] = add(ysum[a, place.y, piece], *[yrecv[a, k - 1, piece] for k in range(1, Y)])
            x_copy(j2).start()

        j3, ok3 = stage(1 + 2 * LAG)

        @pl.when(ok3)
        def _():
            a = lax.rem(j3, SLOTS)
            x_copy(j3).wait()
            for z in range(Z):
                cols = slice(z * WZ, (z + 1) * WZ)
                zsum[a, z] = add(xsum[a, place.x, :, cols], xrecv[a, :, cols])
            for k in place.z_order():
                z_copy(j3, k).start()

        j4, ok4 = stage(1 + 3 * LAG)

        @pl.when(ok4)
        def _():
            a = lax.rem(j4, SLOTS)
            for k in range(1, Z):
                z_copy(j4, k).wait()
            out[j4, x_rows, z_cols] = add(zsum[a, place.z], *[zrecv[a, k - 1] for k in range(1, Z)])
            for k in place.z_order():
                zg_copy(j4, k).start()

        j5, ok5 = stage(1 + 4 * LAG)

        @pl.when(ok5)
        def _():
            for k in range(1, Z):
                zg_copy(j5, k).wait()
            xg_copy(j5).start()

        j6, ok6 = stage(1 + 5 * LAG)

        @pl.when(ok6)
        def _():
            xg_copy(j6).wait()
            for_store(j6, lambda copy: copy.start())

        j7, ok7 = stage(2 + 5 * LAG)

        @pl.when(ok7)
        def _():
            for_store(j7, lambda copy: copy.wait())

    def produce(i, left, offset, cols):
        slot = lax.rem(i, 2)
        for turn in range(2):
            c = 1 - place.c if turn == 0 else place.c
            for y in range(Y):
                first = offset(place.part(y, c))
                if CB % 128 == 0:
                    first = pl.multiple_of(first, 128)
                    value = matmul(left[:, pl.ds(first, CB)], cols, ((0,), (0,))).astype(BF)
                else:
                    start = pl.multiple_of(lax.div(first, 128) * 128, 128)
                    ref.tile[...] = matmul(left[:, pl.ds(start, 128)], cols, ((0,), (0,)))
                    value = ref.tile[pl.ds(pl.multiple_of(first - start, CB), CB)].astype(BF)
                part[slot, c, y] = value
            if turn == 0:
                core_copy(i).start()

    def columns(array, n):
        return array[:, pl.ds(pl.multiple_of(n * CW, CW), CW)]

    acc, gmid, act, slope = ref.acc, ref.gmid, ref.act_s, ref.slope_s
    spread = []
    for b in range(n_blocks):
        goal, over = need[min(b + 1, n_blocks - 1)]
        spread.append((goal, over, need[min(b + 2, n_blocks - 1)][1]))

    def block_step(b, _):
        slot = lax.rem(b, 2)
        for copy in block_loads(b):
            copy.wait()

        for at, (goal, over, soon) in enumerate(spread):
            @pl.when(b == at)
            def _(at=at, goal=goal, over=over, soon=soon):
                gather_until(goal)
                gather_step(done[1] + 3)
                for h in range(spread[at - 1][1] if at else need[0][1], over):
                    if at == 0:
                        direct_step(h)
                    direct_arrived(h)
                for h in range(spread[at - 1][2] if at else over, soon):
                    direct_step(h)

        @pl.when(b + 1 < n_blocks)
        def _():
            for copy in block_loads(b + 1):
                copy.start()

        spots = []
        for p in range(shards):
            row, col = UP_B + p * down_rows // W, p * down_rows % W
            spots.append((slice(row, row + 1), pl.ds(pl.multiple_of(col + b * BW, BW), BW)))
        bias = jnp.concatenate([vec[spot] for spot in spots], axis=1)
        for t in range(rows // MT):
            tile = slice(t * MT, (t + 1) * MT)
            hidden = matmul(second[tile, :], ref.wu[slot]) + bias
            gate = 0.5 * (1.0 + lax.erf(hidden * (0.5**0.5)))
            act[tile, :] = (hidden * gate).astype(BF)
            bell = jnp.exp(-0.5 * hidden * hidden) * 0.3989422804014327
            slope[tile, :] = gate + hidden * bell

        def chunk(n):
            r, c = n // (W // CW), n % (W // CW)
            produce(b * per_block + n, act, lambda p: p * BW + r * CB, columns(gfeed, c))
            tick(b * per_block + n)

        chunk(0)
        sums = [0.0] * shards
        for t in range(rows // MT):
            tile = slice(t * MT, (t + 1) * MT)
            pre = (matmul(gfeed[tile, :], ref.wd[slot], ((1,), (1,))) * slope[tile, :]).astype(BF)
            for p in range(shards):
                mid = pre[:, p * BW : (p + 1) * BW]
                gpre[tile, pl.ds(pl.multiple_of(p * down_rows + b * BW, BW), BW)] = mid
                sums[p] = sums[p] + jnp.sum(mid.astype(F32), axis=0, keepdims=True)
            more = matmul(pre, ref.wu[slot], ((1,), (1,)))
            feed = matmul(act[tile, :], ref.wd[slot])

            @pl.when(b == 0)
            def _():
                gmid[tile, :] = more
                acc[tile, :] = feed

            @pl.when(b > 0)
            def _():
                gmid[tile, :] += more
                acc[tile, :] += feed

            if t == 0:
                for n in range(1, per_block):
                    chunk(n)
        for p in range(shards):
            row, cols = spots[p]
            small[row, cols] = sums[p]
        return 0

    lax.fori_loop(0, n_blocks, block_step, 0)

    tok_out, tok_send, tok_own = ref.tok_out, ref.tok_send, ref.tok_own

    def to_owner(t, value, kept, given):
        if R >= TM:
            lower = pl.ds(pl.multiple_of(lax.rem(t * TM, R), TM), TM)

            @pl.when(t * TM < R)
            def _():
                kept[lower, :] = value.astype(kept.dtype)

            @pl.when(t * TM >= R)
            def _():
                given[lower, :] = value.astype(BF)
        else:
            kept[...] = value[:R].astype(kept.dtype)
            given[...] = value[R:].astype(BF)

    def middle_tile(t, _):
        tile = pl.ds(pl.multiple_of(t * TM, TM), TM)
        low = branch[tile, :]
        middle = x_s[tile, :].astype(F32) + vector(ATTN_SCALE) * low
        feed = acc[tile, :] + vector(DOWN_B)
        to_owner(t, (middle + vector(MLP_SCALE) * feed) * vector(LIVE), tok_own, tok_send)
        upstream = cot[tile, :].astype(F32) * vector(LIVE)
        note(MLP_SCALE, jnp.sum(upstream * feed, axis=0, keepdims=True))
        unit, scale = norm_parts(middle)
        grad = gmid[tile, :]
        note(MLP_GAIN, jnp.sum(grad * unit, axis=0, keepdims=True))
        note(MLP_SHIFT, jnp.sum(grad, axis=0, keepdims=True))
        grad = upstream + norm_back(grad, unit, scale, vector(MLP_GAIN))
        gmid[tile, :] = grad
        note(ATTN_SCALE, jnp.sum(grad * low, axis=0, keepdims=True))
        grad = (grad * vector(ATTN_SCALE)).astype(BF)
        gbranch[tile, :] = grad
        note(PROJ_B, jnp.sum(grad.astype(F32), axis=0, keepdims=True))
        gatt[tile, :] = matmul(grad, ref.proj_s[...], ((1,), (1,))).astype(BF)
        return 0

    def up_chunk(u):
        i = n_down + u
        b, n = lax.rem(u, blocks), lax.div(u, blocks)
        produce(i, second, lambda p: p * other_rows + b * CB, columns(gpre, n))
        tick(i)

    early_up = rows // TM if n_up >= 2 * pairs else 0

    def middle_step(t, _):
        if early_up:
            up_chunk(t)
        return middle_tile(t, 0)

    lax.fori_loop(0, rows // TM, middle_step, 0)
    tok_copy = send(tok_send, tok_out.at[mine], ref.ts.at[0], ref.tr.at[0], swap_peer)
    tok_store = load(tok_own, tok_out.at[mine], ref.lsem.at[11])
    tok_store.start()

    def qkv_load(n):
        slot = lax.rem(n, 2)
        return load(ref.g_qkv.at[:, pl.ds(pl.multiple_of(n * CW, CW), CW)], ref.wu.at[slot, :, pl.ds(0, CW)],
                    ref.qsem.at[slot])

    pown, psend, precv = ref.pown, ref.psend, ref.precv
    gk_acc, gv_acc = ref.gk_acc, ref.gv_acc

    def pair_copy(p, k):
        a = lax.rem(p, PAIR_SLOTS)
        return send(psend.at[a, k - 1], precv.at[a, k - 1], ref.ps.at[a, k - 1], ref.pr.at[a, k - 1],
                    half_peer(k))

    def pair_done(p):
        a = lax.rem(p, PAIR_SLOTS)
        for k in range(1, half):
            pair_copy(p, k).wait()
        for which in range(2):
            whole = pown[a, which]
            for k in range(1, half):
                whole = whole + precv[a, k - 1, which].astype(F32)
            cols = pl.ds(pl.multiple_of((which + 1) * W + p * 128, 128), 128)
            G[:, cols] = whole.astype(BF)

    per_pair = n_up // pairs

    def pair_step(p, _):
        if per_pair:
            for m in range(max(1, per_pair - tiles + 1)):
                @pl.when(p * per_pair + m >= early_up)
                def _(m=m):
                    up_chunk(p * per_pair + m)
        else:
            @pl.when(lax.rem(p, pairs // n_up) == 0)
            def _():
                up_chunk(lax.div(p, pairs // n_up))

        lane = lax.broadcasted_iota(jnp.int32, (1, 128), 1)
        cols = pl.ds(pl.multiple_of(p * 128, 128), 128)
        key, value = kv[0, :, cols], kv[1, :, cols]
        key_t = key.T
        for t in range(tiles):
            tile = slice(t * QT, (t + 1) * QT)
            own = both_heads(query[tile, cols] * BF(HEAD_DIM**-0.5), lane)
            own_grad = both_heads(gatt[tile, cols], lane)
            logs = jnp.concatenate([lse[p, :, tile], lse[p, :, rows + t * QT : rows + (t + 1) * QT]], axis=1)
            probs = jnp.exp(matmul(key, own, ((1,), (1,))) - logs)
            grad_probs = matmul(value, own_grad, ((1,), (1,)))
            centre = jnp.sum(grad_probs * probs, axis=0, keepdims=True)
            grad_scores = (probs * (grad_probs - centre)).astype(BF)
            gv = matmul(probs.astype(BF), own_grad)
            gk = matmul(grad_scores, own)
            if t == 0:
                gv_acc[...], gk_acc[...] = gv, gk
            else:
                gv_acc[...] += gv
                gk_acc[...] += gk
            G[tile, cols] = (own_heads(matmul(key_t, grad_scores)) * HEAD_DIM**-0.5).T.astype(BF)
            if per_pair and t < tiles - 1:
                u = p * per_pair + max(1, per_pair - tiles + 1) + t

                @pl.when(u >= early_up)
                def _(u=u):
                    up_chunk(u)
        a = lax.rem(p, PAIR_SLOTS)
        pown[a, 0], pown[a, 1] = gk_acc[:rows], gv_acc[:rows]
        for k in range(1, half):
            psend[a, k - 1, 0] = gk_acc[k * rows : (k + 1) * rows].astype(BF)
            psend[a, k - 1, 1] = gv_acc[k * rows : (k + 1) * rows].astype(BF)
            pair_copy(p, k).start()

        @pl.when(p >= 1)
        def _():
            pair_done(p - 1)
        return 0

    lax.fori_loop(0, pairs, pair_step, 0)

    qkv_load(0).start()

    def proj_step(u, _):
        i = n_down + n_up + u
        r, c = lax.div(u, W // CW), lax.rem(u, W // CW)
        produce(i, attended, lambda p: p * other_rows + r * CB, columns(gbranch, c))
        tick(i)

        @pl.when(u == 0)
        def _():
            pair_done(pairs - 1)
        return 0

    lax.fori_loop(0, n_proj, proj_step, 0)

    def qkv_step(n, _):
        cols = columns(G, n)
        for b in range(blocks):
            i = n_down + n_up + n_proj + n * blocks + b
            produce(i, first, lambda p: p * other_rows + b * CB, cols)
            tick(i)
            if b == 0:
                qkv_load(n).wait()

                @pl.when(n + 1 < 3 * W // CW)
                def _():
                    qkv_load(n + 1).start()

                for t in range(rows // MT):
                    tile = slice(t * MT, (t + 1) * MT)
                    term = matmul(cols[tile, :], ref.wu[lax.rem(n, 2), :, :CW], ((1,), (1,)))

                    @pl.when(n == 0)
                    def _():
                        acc[tile, :] = term

                    @pl.when(n > 0)
                    def _():
                        acc[tile, :] += term
        return 0

    lax.fori_loop(0, 3 * W // CW, qkv_step, 0)

    gt_own, gt_send = ref.gt_own_s, ref.gt_send

    def first_tile(t, _):
        tile = pl.ds(pl.multiple_of(t * TM, TM), TM)
        unit, scale = norm_parts(x_s[tile, :].astype(F32))
        grad = acc[tile, :]
        note(ATTN_GAIN, jnp.sum(grad * unit, axis=0, keepdims=True))
        note(ATTN_SHIFT, jnp.sum(grad, axis=0, keepdims=True))
        note(QV, jnp.sum(G[tile, :W].astype(F32), axis=0, keepdims=True))
        note(QV + 1, jnp.sum(G[tile, 2 * W :].astype(F32), axis=0, keepdims=True))
        to_owner(t, gmid[tile, :] + norm_back(grad, unit, scale, vector(ATTN_GAIN)), gt_own, gt_send)
        return 0

    lax.fori_loop(0, rows // TM, first_tile, 0)

    cw = W // shards
    packs = ref.packs
    for p in range(shards):
        at = 0
        for row, count in SMALL_ROWS:
            for r in range(count):
                t = p * count + r
                line, col = row + t // shards, t % shards * cw
                packs[p % 2, p // 2, at : at + 1, :] = small[line : line + 1, col : col + cw]
                at += 1

    sums = ref.sums
    core_small = send(packs.at[1 - place.c], ref.core_pack, ref.ss.at[0], ref.sr.at[0], place.at(c=1 - place.c))
    y_small = [send(packs.at[place.c, place.ahead_y(k)], sums.at[0, k], ref.ss.at[k], ref.sr.at[k],
                    place.at(y=place.ahead_y(k))) for k in range(1, Y)]
    x_small = [send(sums.at[1, 0], sums.at[1, 1], ref.ss.at[Y], ref.sr.at[Y], place.at(x=1 - place.x))]
    z_small = [send(sums.at[2, 0], sums.at[2, k], ref.ss.at[Y + k], ref.sr.at[Y + k],
                    place.at(z=place.near_z(k))) for k in range(1, Z)]

    def small_step(step):
        if step == 0:
            core_small.wait()
            for y in range(Y):
                packs[place.c, y] = packs[place.c, y] + ref.core_pack[y]
            for copy in y_small:
                copy.start()
            return
        copies = (y_small, x_small, z_small)[step - 1]
        for copy in copies:
            copy.wait()
        whole = packs[place.c, place.y] if step == 1 else sums[step - 1, 0]
        for k in range(len(copies)):
            whole = whole + sums[step - 1, k + 1]
        if step < 3:
            sums[step, 0] = whole
            for copy in (x_small, z_small)[step - 1]:
                copy.start()
        else:
            ref.small_out[...] = whole

    core_small.start()
    gt_copy = send(gt_send, ref.gt_low, ref.ts.at[1], ref.tr.at[1], swap_peer)
    gt_store = load(gt_own, ref.gt_own, ref.lsem.at[10])
    gt_store.start()
    depth = 3 + 5 * LAG
    small_after = {0: 0, 2 + LAG: 1, 2 + 2 * LAG: 2, 2 + 3 * LAG: 3}
    for lag in range(depth):
        tick(total + lag)
        if lag in small_after:
            small_step(small_after[lag])
        if lag == 0:
            gt_copy.start()
            tok_copy.start()
    for copy in (tok_store, gt_store, gt_copy, tok_copy):
        copy.wait()


def layer(replicas, shards, vectors, count, tokens, cotangent, weights):
    Y, Z, half = shards // 2, replicas // 2, shards // 2
    _, R, W = tokens.shape
    rows, keys = 2 * R, half * 2 * R
    FF = weights[UP].shape[1]
    CB, CW = min(128, W // shards), max(512, 128 * Z)
    HB, WZ = CB // 2, CW // Z
    total = (FF // shards // CB) * (W // CW) + (W // shards // CB) * ((FF + 4 * W) // CW)
    peers = max(Y, Z, 2)
    staged, direct, _ = gather_items(replicas, shards, W, FF)
    m = len(staged) + len(direct)
    multiples = tuple(v.shape[0] // (W // shards) for v in vectors)
    if (W // shards) % 128:
        vectors = [v.reshape(n, W // shards) for v, n in zip(vectors, multiples)]
    dma = pltpu.SemaphoreType.DMA
    vmem, anywhere = pl.BlockSpec(memory_space=pltpu.VMEM), pl.BlockSpec(memory_space=pl.ANY)
    inputs = dict(count=count, tokens=tokens, cotangent=cotangent, qkv=weights[QKV], proj=weights[PROJ],
                  up=weights[UP], down=weights[DOWN])
    scratch = dict(
        part=pltpu.VMEM((2, 2, Y, CB, CW), BF),
        crecv=pltpu.VMEM((CORE_SLOTS, Y, CB, CW), BF),
        ysum=pltpu.VMEM((SLOTS, Y, CB, CW), BF),
        yrecv=pltpu.VMEM((SLOTS, Y - 1, CB, CW), BF),
        xsum=pltpu.VMEM((SLOTS, 2, HB, CW), BF),
        xrecv=pltpu.VMEM((SLOTS, HB, CW), BF),
        zsum=pltpu.VMEM((SLOTS, Z, HB, WZ), BF),
        zrecv=pltpu.VMEM((SLOTS, Z - 1, HB, WZ), BF),
        out=pltpu.VMEM((total, CB, CW), BF),
        small_buf=pltpu.VMEM((16, W), F32),
        packs=pltpu.VMEM((2, Y, 16, W // shards), F32),
        core_pack=pltpu.VMEM((Y, 16, W // shards), F32),
        sums=pltpu.VMEM((3, peers, 16, W // shards), F32),
        kv=pltpu.VMEM((2, keys, W), BF),
        gpre=pltpu.VMEM((rows, FF), BF),
        act_s=pltpu.VMEM((rows, shards * BW), BF),
        slope_s=pltpu.VMEM((rows, shards * BW), F32),
        cot_s=pltpu.VMEM((rows, W), BF),
        gfeed=pltpu.VMEM((rows, W), BF),
        x_s=pltpu.VMEM((rows, W), BF),
        branch_s=pltpu.VMEM((rows, W), F32),
        second_s=pltpu.VMEM((rows, W), BF),
        attended_s=pltpu.VMEM((rows, W), BF),
        query_s=pltpu.VMEM((rows, W), BF),
        first_s=pltpu.VMEM((rows, W), BF),
        proj_s=pltpu.VMEM((W, W), BF),
        wd=pltpu.VMEM((2, shards * BW, W), BF),
        wu=pltpu.VMEM((2, W, shards * BW), BF),
        wq=pltpu.VMEM((W, CW), BF),
        acc=pltpu.VMEM((rows, W), F32),
        gmid=pltpu.VMEM((rows, W), F32),
        gbranch=pltpu.VMEM((rows, W), BF),
        gatt=pltpu.VMEM((rows, W), BF),
        G=pltpu.VMEM((rows, 3 * W), BF),
        pown=pltpu.VMEM((PAIR_SLOTS, 2, rows, 128), F32),
        psend=pltpu.VMEM((PAIR_SLOTS, half - 1, 2, rows, 128), BF),
        precv=pltpu.VMEM((PAIR_SLOTS, half - 1, 2, rows, 128), BF),
        gk_acc=pltpu.VMEM((keys, 128), F32),
        gv_acc=pltpu.VMEM((keys, 128), F32),
        tok_send=pltpu.VMEM((R, W), BF),
        gt_send=pltpu.VMEM((R, W), BF),
        tok_own=pltpu.VMEM((R, W), BF),
        gt_own_s=pltpu.VMEM((R, W), F32),
        small_s=pltpu.VMEM((shards, 16, W // shards), F32),
        vec=pltpu.VMEM((16, W), F32),
        lse=pltpu.VMEM((W // 128, 1, 2 * rows), F32),
        lsem=dma((12,)), wsem=dma((2, 2, shards)), qsem=dma((3,)), osem=dma((SLOTS,)),
        gys=dma((m, Y - 1)), gyr=dma((m, Y - 1)),
        gzs=dma((m, Y - 1, Z - 1)), gzr=dma((m, Y - 1, Z - 1)),
        gxs=dma((m, Y - 1)), gxr=dma((m, Y - 1)),
        gcs=dma((m, Y - 1)), gcr=dma((m, Y - 1)),
        os=dma((4,)), orr=dma((4,)),
        vs=dma((shards - 1,)), vr=dma((shards - 1,)),
        ks=dma((2, W // CW, half - 1)), kr=dma((2, W // CW, half - 1)),
        cs=dma((CORE_SLOTS,)), cr=dma((CORE_SLOTS,)),
        ys=dma((SLOTS, Y - 1)), yr=dma((SLOTS, Y - 1)),
        xs=dma((SLOTS,)), xr=dma((SLOTS,)),
        zs=dma((SLOTS, Z - 1)), zr=dma((SLOTS, Z - 1)),
        gs=dma((SLOTS, Z - 1)), gr=dma((SLOTS, Z - 1)),
        hs=dma((SLOTS,)), hr=dma((SLOTS,)),
        ps=dma((PAIR_SLOTS, half - 1)), pr=dma((PAIR_SLOTS, half - 1)),
        ss=dma((Y + Z,)), sr=dma((Y + Z,)),
        ts=dma((4,)), tr=dma((4,)),
    )
    if CB % 128:
        scratch["tile"] = pltpu.VMEM((128, CW), F32)
    outs = dict(
        o_down=jax.ShapeDtypeStruct((FF // shards, W), BF),
        o_up=jax.ShapeDtypeStruct((W // shards, FF), BF),
        o_proj=jax.ShapeDtypeStruct((W // shards, W), BF),
        o_qkv=jax.ShapeDtypeStruct((W // shards, 3 * W), BF),
        small_out=jax.ShapeDtypeStruct((16, W // shards), F32),
        tok_out=jax.ShapeDtypeStruct((2, R, W), BF),
        gt_own=jax.ShapeDtypeStruct((R, W), F32),
        gt_low=jax.ShapeDtypeStruct((R, W), BF),
        g_qkv=jax.ShapeDtypeStruct((W, 3 * W), BF),
        g_proj=jax.ShapeDtypeStruct((W, W), BF),
        g_up=jax.ShapeDtypeStruct((W, FF), BF),
        g_down=jax.ShapeDtypeStruct((FF, W), BF),
    )
    names = tuple(inputs) + tuple(outs) + tuple(scratch)
    results = pl.pallas_call(
        functools.partial(layer_kernel, replicas, shards, multiples, names),
        in_specs=[vmem] * len(vectors) + [pl.BlockSpec(memory_space=pltpu.SMEM)] + [anywhere] * 6,
        out_specs=[anywhere] * 4 + [vmem] + [anywhere] * 7,
        out_shape=list(outs.values()),
        scratch_shapes=list(scratch.values()),
        compiler_params=pltpu.CompilerParams(
            collective_id=0, has_side_effects=True, vmem_limit_bytes=63 * MIB
        ),
    )(*vectors, *inputs.values())
    return results[:8]


def result_kernel(shards, n_vectors, *refs):
    small, tok, gt_own, gt_low, *ins = refs[:8]
    tok_out, gt_out, *outs = refs[8:14]
    vectors = refs[14 : 14 + n_vectors]
    low, wide, tok_s, own_s, low_s, gt_s, in_sem, out_sem = refs[14 + n_vectors :]
    mine = lax.div(lax.axis_index("shard"), shards // 2)
    size, width = low.shape[1:]
    blocks = []
    for source, target in zip(ins, outs):
        for r in range(source.shape[0] // size):
            for c in range(source.shape[1] // width):
                at = (pl.ds(r * size, size), pl.ds(c * width, width))
                blocks.append((source.at[at], target.at[at]))
    n = len(blocks)
    loads = [pltpu.make_async_copy(src, low.at[i], in_sem.at[i]) for i, (src, _) in enumerate(blocks)]
    stores = [pltpu.make_async_copy(wide.at[i], dst, out_sem.at[i]) for i, (_, dst) in enumerate(blocks)]
    for i, (source, middle) in enumerate(((gt_low, low_s), (gt_own, own_s), (tok, tok_s))):
        loads.append(pltpu.make_async_copy(source, middle, in_sem.at[n + i]))
    stores += [
        pltpu.make_async_copy(gt_s, gt_out.at[1 - mine], out_sem.at[n]),
        pltpu.make_async_copy(own_s, gt_out.at[mine], out_sem.at[n + 1]),
        pltpu.make_async_copy(tok_s, tok_out, out_sem.at[n + 2]),
    ]
    for copy in loads:
        copy.start()
    at = 0
    for (_, count), vector in zip(SMALL_ROWS, vectors):
        pieces = [small[at + r : at + r + 1, :] for r in range(count)]
        vector[...] = jnp.concatenate(pieces, axis=1).reshape(vector.shape)
        at += count
    for i in range(n + 3):
        loads[i].wait()
        if i < n:
            wide[i] = low[i].astype(F32)
        elif i == n:
            gt_s[...] = low_s[...].astype(F32)
        stores[i].start()
    for copy in stores:
        copy.wait()


def results(shards, small, tok, gt_own, gt_low, grads):
    _, R, W = tok.shape
    size = W // shards
    count = sum(grad.shape[0] * grad.shape[1] for grad in grads) // (size * W)
    vmem, anywhere = pl.BlockSpec(memory_space=pltpu.VMEM), pl.BlockSpec(memory_space=pl.ANY)
    shapes = [jax.ShapeDtypeStruct(tok.shape, BF), jax.ShapeDtypeStruct(tok.shape, F32)]
    shapes += [jax.ShapeDtypeStruct(grad.shape, F32) for grad in grads]
    n_vectors = len(SMALL_ROWS) if size % 128 == 0 else 0
    for _, rows in SMALL_ROWS[:n_vectors]:
        shapes.append(jax.ShapeDtypeStruct((rows * size,), F32))
    dma = pltpu.SemaphoreType.DMA
    tok, gt, *rest = pl.pallas_call(
        functools.partial(result_kernel, shards, n_vectors),
        in_specs=[vmem] + [anywhere] * 7,
        out_specs=[anywhere] * 6 + [vmem] * n_vectors,
        out_shape=shapes,
        scratch_shapes=[
            pltpu.VMEM((count, size, W), BF), pltpu.VMEM((count, size, W), F32),
            pltpu.VMEM(tok.shape, BF), pltpu.VMEM((R, W), F32), pltpu.VMEM((R, W), BF), pltpu.VMEM((R, W), F32),
            dma((count + 3,)), dma((count + 3,)),
        ],
        compiler_params=pltpu.CompilerParams(vmem_limit_bytes=63 * MIB),
    )(small, tok, gt_own, gt_low, *grads)
    vectors = rest[4:]
    if not n_vectors:
        at = 0
        for _, rows in SMALL_ROWS:
            vectors.append(small[at : at + rows].reshape(-1))
            at += rows
    return tok, gt, rest[:4], vectors


def on_device(replicas, shards, tokens, qkv_weight, qv_bias, proj_weight, proj_bias, up_weight, up_bias,
              down_weight, down_bias, attn_gain, attn_shift, mlp_gain, mlp_shift, attn_scale, mlp_scale,
              cotangent, image_count):
    vectors = (qv_bias, proj_bias, up_bias, down_bias, attn_gain, attn_shift, mlp_gain, mlp_shift,
               attn_scale, mlp_scale)
    *grads, small, output, grad_own, grad_low = layer(
        replicas, shards, vectors, image_count, tokens, cotangent,
        (qkv_weight, proj_weight, up_weight, down_weight),
    )
    output, grad_tokens, (down, up, proj, qkv), small = results(
        shards, small, output, grad_own, grad_low, grads)
    qv_b, proj_b, up_b, down_b, *norms = small
    return (output, grad_tokens, qkv, qv_b, proj, proj_b, up, up_b, down, down_b, *norms)


def solution(mesh):
    rows, vector = P("shard", None), P("shard")
    image = P("replica", "shard", None)
    in_specs = (image, rows, vector, rows, vector, rows, vector, rows, vector, vector, vector, vector,
                vector, vector, vector, image, P())
    out_specs = (image, image, rows, vector, rows, vector, rows, vector, rows, vector, vector, vector,
                 vector, vector, vector, vector)
    return jax.shard_map(
        functools.partial(on_device, mesh.shape["replica"], mesh.shape["shard"]),
        mesh=mesh, in_specs=in_specs, out_specs=out_specs, check_vma=False,
    )
```

```python
import functools
import types

import jax
import jax.numpy as jnp
from jax import lax
from jax.experimental import pallas as pl
from jax.experimental.pallas import tpu as pltpu
from jax.sharding import PartitionSpec as P

HEAD_DIM = 64
EPS = 1e-06
BF = jnp.bfloat16
F32 = jnp.float32
MESH = pl.DeviceIdType.MESH
MIB = 1024 * 1024
SLOTS = 6
PAIR_SLOTS = 4
CORE_SLOTS = 4
LAG = 2


def matmul(left, right, dims=((1,), (0,))):
    return lax.dot_general(left, right, (dims, ((), ())), preferred_element_type=F32)


class Place:
    def __init__(self, replicas, shards):
        self.Z, self.Y = replicas // 2, shards // 2
        self.shards = shards
        replica, shard = lax.axis_index("replica"), lax.axis_index("shard")
        self.x, self.z = lax.rem(replica, 2), lax.div(replica, 2)
        self.c, self.y = lax.rem(shard, 2), lax.div(shard, 2)
        self.s = shard

    def part(self, y, c):
        return y * 2 + c

    def at(self, x=None, z=None, y=None, c=None):
        x = self.x if x is None else x
        z = self.z if z is None else z
        y = self.y if y is None else y
        c = self.c if c is None else c
        return (z * 2 + x, y * 2 + c)

    def near_z(self, k):
        z, bit = self.z, 1
        while bit < self.Z:
            if k & bit:
                z = z + bit - 2 * bit * lax.rem(lax.div(z, bit), 2)
            bit *= 2
        return z

    def z_order(self):
        return sorted(range(1, self.Z), key=lambda k: (-(k.bit_length()), k))

    def ahead_y(self, k):
        return lax.rem(self.y + k, self.Y)

    def behind_y(self, k):
        return lax.rem(self.y + self.Y - k, self.Y)

    def greet(self, extra=()):
        others = [self.at(c=1 - self.c), self.at(x=1 - self.x)]
        others += [self.at(y=self.ahead_y(k)) for k in range(1, self.Y)]
        others += [self.at(z=self.near_z(k)) for k in range(1, self.Z)]
        others += list(extra)
        barrier = pltpu.get_barrier_semaphore()
        for other in others:
            pl.semaphore_signal(barrier, inc=1, device_id=other, device_id_type=MESH)
        pl.semaphore_wait(barrier, len(others))


def send(src, dst, send_sem, recv_sem, device):
    return pltpu.make_async_remote_copy(
        src_ref=src,
        dst_ref=dst,
        send_sem=send_sem,
        recv_sem=recv_sem,
        device_id=device,
        device_id_type=MESH,
    )


QV, PROJ_B, UP_B, DOWN_B, ATTN_GAIN, ATTN_SHIFT, MLP_GAIN, MLP_SHIFT, ATTN_SCALE, MLP_SCALE, LIVE = (
    0, 2, 3, 7, 8, 9, 10, 11, 12, 13, 14)
SMALL_ROWS = ((QV, 2), (PROJ_B, 1), (UP_B, 4), (DOWN_B, 1), (ATTN_GAIN, 1), (ATTN_SHIFT, 1), (MLP_GAIN, 1),
              (MLP_SHIFT, 1), (ATTN_SCALE, 1), (MLP_SCALE, 1))
QKV, PROJ, UP, DOWN = range(4)


def norm_parts(values):
    centre = values - jnp.mean(values, axis=-1, keepdims=True)
    scale = lax.rsqrt(jnp.mean(centre * centre, axis=-1, keepdims=True) + EPS)
    return centre * scale, scale


def norm_back(grad, unit, scale, gain):
    inner = grad * gain
    return scale * (
        inner
        - jnp.mean(inner, axis=-1, keepdims=True)
        - unit * jnp.mean(inner * unit, axis=-1, keepdims=True)
    )


BW = 128


FIRST = 6
TAIL = 4
EARLY = 2
PACE = (5, 6, 7, 8, 9, 10, 11, 12, 14)


def gather_items(replicas, shards, width, hidden):
    Z = replicas // 2
    step = max(512, 128 * Z)
    size, down = width // shards, hidden // shards
    halves = width // step
    items = [(QKV, 0, size, n * width + h * step, step) for h in range(halves) for n in (1, 2, 0)]
    items += [(PROJ, 0, size, h * step, step) for h in range(halves)]
    upto, known = [], set()
    for b in range(down // BW):
        for p in range(shards):
            c = (p * down + b * BW) // step
            if c not in known:
                known.add(c)
                items.append((UP, 0, size, c * step, step))
        items.append((DOWN, b * BW, BW, 0, width))
        upto.append(len(items))
    straight = set(range(len(items) - TAIL, len(items)))
    straight |= set(range(upto[0] - EARLY, upto[0]))
    staged = [item for n, item in enumerate(items) if n not in straight]
    direct = [item for n, item in enumerate(items) if n in straight]
    need = []
    for n in upto:
        over = len([m for m in straight if m < n])
        need.append((n - over, over))
    return staged, direct, need


def layer_kernel(replicas, shards, multiples, names, *refs):
    vector_refs, refs = refs[: len(multiples)], refs[len(multiples) :]
    ref = types.SimpleNamespace(**dict(zip(names, refs)))
    place = Place(replicas, shards)
    Y, Z, s = place.Y, place.Z, place.s
    half = shards // 2
    part, crecv, ysum, yrecv = ref.part, ref.crecv, ref.ysum, ref.yrecv
    xsum, xrecv, zsum, zrecv = ref.xsum, ref.xrecv, ref.zsum, ref.zrecv
    out, small, vec, lse = ref.out, ref.small_buf, ref.vec, ref.lse
    CB, CW = part.shape[3], part.shape[4]
    rows, W = ref.gfeed.shape
    R = rows // 2
    keys = half * rows
    FF = ref.gpre.shape[1]
    down_rows, other_rows = FF // shards, W // shards
    n_blocks, blocks = down_rows // BW, other_rows // CB
    per_block = (BW // CB) * (W // CW)
    n_down, n_up = n_blocks * per_block, blocks * (FF // CW)
    n_proj, n_qkv = blocks * (W // CW), blocks * (3 * W // CW)
    total = n_down + n_up + n_proj + n_qkv
    mine = lax.div(s, half)
    j_half = lax.rem(s, half)
    replica = lax.axis_index("replica")
    kv, gpre, cot, gfeed, G = ref.kv, ref.gpre, ref.cot_s, ref.gfeed, ref.G
    second, first, query, x_s = ref.second_s, ref.first_s, ref.query_s, ref.x_s
    attended, branch, gbranch, gatt = ref.attended_s, ref.branch_s, ref.gbranch, ref.gatt
    TR, MT, QT, TM = min(128, R), min(512, rows), min(256, rows), min(256, R)
    pairs, tiles = W // 128, rows // QT

    def half_peer(k):
        return (replica, mine * half + lax.rem(j_half + k, half))

    swap_peer = (replica, lax.rem(s + half, shards))

    def load(src, dst, sem):
        return pltpu.make_async_copy(src, dst, sem)

    sources = (ref.qkv, ref.proj, ref.up, ref.down)
    weights = (ref.g_qkv, ref.g_proj, ref.g_up, ref.g_down)
    sizes = [source.shape[0] for source in sources]
    bounce = (G, gbranch, gpre, ref.proj_s)

    def own_rows(w):
        return weights[w].at[pl.ds(pl.multiple_of(s * sizes[w], sizes[w]), sizes[w])]

    own_loads = [load(sources[w], bounce[w].at[pl.ds(0, sizes[w])], ref.lsem.at[w]) for w in range(4)]
    own_stores = [load(bounce[w].at[pl.ds(0, sizes[w])], own_rows(w), ref.lsem.at[4 + w]) for w in range(4)]
    x_load = load(ref.tokens.at[mine], x_s.at[pl.ds(0, R)], ref.lsem.at[8])
    cot_load = load(ref.cotangent.at[mine], cot.at[pl.ds(0, R)], ref.lsem.at[9])
    x_load.start()
    for copy in own_loads:
        copy.start()
    cot_load.start()
    row = 0
    for vector_ref, count in zip(vector_refs, multiples):
        values = vector_ref[...].astype(F32).reshape(count, ref.small_s.shape[2])
        ref.small_s[s, row : row + count, :] = values
        row += count
    place.greet([(replica, lax.rem(s + k, shards)) for k in range(1, shards)])

    staged, direct, need = gather_items(replicas, shards, W, FF)
    items = staged + direct
    n_staged = len(staged)

    def piece(m, owner, whole_rows, whole_cols):
        w, row, size, col, width = items[m]
        at, cols = owner * sizes[w] + row, pl.ds(col, width)
        if not whole_rows:
            size //= 2
            at = at + place.x * size
        if not whole_cols:
            if size % (16 * Z):
                cols = pl.ds(pl.multiple_of(col + place.z * (width // Z), 128), width // Z)
            else:
                size //= Z
                at = at + place.z * size
        return pl.ds(pl.multiple_of(at, 16), size), cols

    def gy_copy(m, k):
        w, whole = items[m][0], m >= n_staged
        return send(sources[w].at[piece(m, 0, whole, whole)], weights[w].at[piece(m, s, whole, whole)],
                    ref.gys.at[m, k - 1], ref.gyr.at[m, k - 1], place.at(y=place.ahead_y(k)))

    def gathered(m, k, whole_rows, whole_cols):
        owner = place.part(place.behind_y(k), place.c)
        return weights[items[m][0]].at[piece(m, owner, whole_rows, whole_cols)]

    def gz_copy(m, k, j):
        b = gathered(m, k, False, False)
        return send(b, b, ref.gzs.at[m, k - 1, j - 1], ref.gzr.at[m, k - 1, j - 1],
                    place.at(z=place.near_z(j)))

    def gx_copy(m, k):
        b = gathered(m, k, False, True)
        return send(b, b, ref.gxs.at[m, k - 1], ref.gxr.at[m, k - 1], place.at(x=1 - place.x))

    def gc_copy(m, k):
        b = gathered(m, k, True, True)
        return send(b, b, ref.gcs.at[m, k - 1], ref.gcr.at[m, k - 1], place.at(c=1 - place.c))

    def gy_start(m):
        for k in range(1, Y):
            gy_copy(m, k).start()

    def direct_arrived(h):
        for k in range(1, Y):
            gy_copy(n_staged + h, k).wait()
            gc_copy(n_staged + h, k).start()

    def arrived(m):
        for k in range(1, Y):
            gc_copy(m, k).wait()

    halves = W // CW
    early = 3 * halves

    done = [0, 0, 0, 0]

    def gather_z(n):
        for m in range(done[0], min(n, n_staged)):
            for k in range(1, Y):
                gy_copy(m, k).wait()
                for j in place.z_order():
                    gz_copy(m, k, j).start()
            done[0] = m + 1

    def gather_x(n):
        gather_z(n)
        for m in range(done[1], min(n, n_staged)):
            for k in range(1, Y):
                for j in range(1, Z):
                    gz_copy(m, k, j).wait()
                gx_copy(m, k).start()
            done[1] = m + 1

    def gather_c(n):
        gather_x(n)
        for m in range(done[2], min(n, n_staged)):
            for k in range(1, Y):
                gx_copy(m, k).wait()
                gc_copy(m, k).start()
            done[2] = m + 1

    def gather_until(n):
        gather_c(n)
        for m in range(done[3], min(n, n_staged)):
            for k in range(1, Y):
                gc_copy(m, k).wait()
            done[3] = m + 1

    def gather_step(n):
        gather_c(n - 3)
        gather_x(n)
        gather_z(n + 3)
        gather_until(n - 5)

    def direct_step(h):
        for k in range(1, Y):
            gy_copy(n_staged + h, k).wait()
            gc_copy(n_staged + h, k).start()

    def direct_arrived(h):
        for k in range(1, Y):
            gc_copy(n_staged + h, k).wait()

    x_swap = send(ref.tokens.at[1 - mine], x_s.at[pl.ds(R, R)], ref.ts.at[2], ref.tr.at[2], swap_peer)
    cot_swap = send(ref.cotangent.at[1 - mine], cot.at[pl.ds(R, R)], ref.ts.at[3], ref.tr.at[3], swap_peer)
    small_sends = [
        send(ref.small_s.at[s], ref.small_s.at[s], ref.vs.at[k - 1], ref.vr.at[k - 1],
             (replica, lax.rem(s + k, shards)))
        for k in range(1, shards)
    ]
    own_sends = [send(sources[w], own_rows(w), ref.os.at[w], ref.orr.at[w], place.at(c=1 - place.c))
                 for w in range(4)]
    for copy in small_sends:
        copy.start()
    for m in range(min(FIRST, n_staged)):
        gy_start(m)
    x_swap.start()
    for m in range(FIRST, n_staged):
        gy_start(m)
    for copy in own_sends:
        copy.start()

    gather_z(3)

    for copy in small_sends:
        copy.wait()
    vec[...] = jnp.zeros_like(vec)
    row = 0
    for count in multiples:
        pieces = [ref.small_s[p, row + r : row + r + 1, :] for p in range(shards) for r in range(count)]
        for r in range(count):
            vec[row + r : row + r + 1, :] = jnp.concatenate(pieces[r * shards : (r + 1) * shards], axis=1)
        row += count
    live = (mine < ref.count[replica]).astype(F32)
    vec[LIVE : LIVE + 1, :] = jnp.full((1, W), live, F32)

    def vector(row):
        return vec[row : row + 1, :]

    def note(row, value):
        small[row : row + 1, :] += value

    def norm_tile(t, _):
        tile = pl.ds(pl.multiple_of(t * TR, TR), TR)
        unit, _ = norm_parts(x_s[tile, :].astype(F32))
        first[tile, :] = (unit * vector(ATTN_GAIN) + vector(ATTN_SHIFT)).astype(BF)
        return 0

    x_load.wait()
    lax.fori_loop(0, R // TR, norm_tile, 0)
    for w in range(4):
        own_loads[w].wait()
        own_stores[w].start()
    for m in range(3):
        gather_x(m + 1)
        gather_z(m + 4)
        gather_c(m)
    x_swap.wait()
    lax.fori_loop(R // TR, rows // TR, norm_tile, 0)
    own_stores[QKV].wait()
    own_sends[QKV].wait()

    def kv_copy(which, h, k):
        cols = pl.ds(h * CW, CW)
        return send(kv.at[which, pl.ds(0, rows), cols], kv.at[which, pl.ds((half - k) * rows, rows), cols],
                    ref.ks.at[which, h, k - 1], ref.kr.at[which, h, k - 1], half_peer(k))

    def qkv_slot(slot):
        if slot < 2:
            return ref.wu[slot, :, :CW]
        return ref.wq[...]

    def qkv_tile(n, h, slot):
        target = ref.wu.at[slot, :, pl.ds(0, CW)] if slot < 2 else ref.wq
        return load(ref.g_qkv.at[:, pl.ds(n * W + h * CW, CW)], target, ref.qsem.at[slot])

    def project(h, ready):
        here = slice(h * CW, (h + 1) * CW)
        tile_loads = [qkv_tile(1, h, 0), qkv_tile(2, h, 1), qkv_tile(0, h, 2)]
        for n in range(2):
            ready(n)
            tile_loads[n].start()
        for n in range(3):
            if n == 1:
                ready(2)
                tile_loads[2].start()
            tile_loads[n].wait()
            for t in range(rows // MT):
                tile = slice(t * MT, (t + 1) * MT)
                value = matmul(first[tile, :], qkv_slot(n))
                if n == 0:
                    kv[0, tile, here] = value.astype(BF)
                elif n == 1:
                    kv[1, tile, here] = (value + vector(QV + 1)[:, here]).astype(BF)
                else:
                    query[tile, here] = (value + vector(QV)[:, here]).astype(BF)
            if n < 2:
                for k in range(1, half):
                    kv_copy(n, h, k).start()

    def exchanged(h):
        for which in range(2):
            for k in range(1, half):
                kv_copy(which, h, k).wait()

    def first_ready(n):
        gather_until(n + 1)
        if n == 1:
            gather_x(4)
        elif n == 2:
            gather_z(8)
            gather_x(5)

    project(0, first_ready)
    cot_swap.start()
    for h in range(len(direct)):
        gy_start(n_staged + h)

    plan = {}

    def at_pair(p, act):
        plan.setdefault(p, []).append(act)

    for p in range(1, pairs):
        at_pair(p, lambda p=p: gather_step(PACE[p]))
    if halves > 1:
        def second_half():
            gather_until(early)
            project(1, lambda n: None)

        at_pair(pairs // 2 - 1, second_half)
        at_pair(pairs // 2, lambda: exchanged(1))

    proj_load = load(ref.g_proj, ref.proj_s, ref.lsem.at[10])

    def proj_ready():
        gather_until(early + halves)
        own_stores[PROJ].wait()
        own_stores[DOWN].wait()
        own_sends[PROJ].wait()
        proj_load.start()

    at_pair(pairs - 1, proj_ready)
    gather_step(PACE[0])
    exchanged(0)

    def both_heads(array, lane):
        return jnp.concatenate([jnp.where(lane < HEAD_DIM, array, BF(0)), jnp.where(lane >= HEAD_DIM, array, BF(0))])

    def own_heads(array):
        n = array.shape[1] // 2
        return jnp.concatenate([array[:HEAD_DIM, :n], array[HEAD_DIM:, n:]])

    def attend(p, _):
        for at in sorted(plan):
            @pl.when(p == at)
            def _(at=at):
                for act in plan[at]:
                    act()

        lane = lax.broadcasted_iota(jnp.int32, (1, 128), 1)
        cols = pl.ds(pl.multiple_of(p * 128, 128), 128)
        key, value_t = kv[0, :, cols], kv[1, :, cols].T
        scores = matmul(key, both_heads(query[:, cols] * BF(HEAD_DIM**-0.5), lane), ((1,), (1,)))
        highest = jnp.max(scores, axis=0, keepdims=True)
        expos = jnp.exp(scores - highest)
        denom = jnp.sum(expos, axis=0, keepdims=True)
        probs = (expos * (1.0 / denom)).astype(BF)
        lse[p] = highest + jnp.log(denom)
        attended[:, cols] = own_heads(matmul(value_t, probs)).T.astype(BF)
        return 0

    lax.fori_loop(0, pairs, attend, 0)

    cot_load.wait()
    cot_swap.wait()
    small[...] = jnp.zeros_like(small)

    def feed_tile(t, _):
        tile = pl.ds(pl.multiple_of(t * TR, TR), TR)
        value = (cot[tile, :].astype(F32) * vector(LIVE) * vector(MLP_SCALE)).astype(BF)
        gfeed[tile, :] = value
        note(DOWN_B, jnp.sum(value.astype(F32), axis=0, keepdims=True))
        return 0

    lax.fori_loop(0, rows // TR, feed_tile, 0)
    proj_load.wait()
    gather_step(PACE[-1])

    for w in (UP, DOWN):
        own_sends[w].wait()
    own_stores[UP].wait()

    def block_loads(b):
        slot = lax.rem(b, 2)
        copies = []
        for p in range(shards):
            at = pl.ds(pl.multiple_of(p * down_rows + b * BW, BW), BW)
            to = pl.ds(p * BW, BW)
            copies.append(load(ref.g_up.at[:, at], ref.wu.at[slot, :, to], ref.wsem.at[0, slot, p]))
            copies.append(load(ref.g_down.at[at], ref.wd.at[slot, to], ref.wsem.at[1, slot, p]))
        return copies

    gather_until(need[0][0])
    for h in range(need[0][1]):
        direct_step(h)
        direct_arrived(h)
    for copy in block_loads(0):
        copy.start()

    def branch_tile(t, _):
        tile = pl.ds(pl.multiple_of(t * MT, MT), MT)
        low = matmul(attended[tile, :], ref.proj_s[...]) + vector(PROJ_B)
        branch[tile, :] = low
        unit, _ = norm_parts(x_s[tile, :].astype(F32) + vector(ATTN_SCALE) * low)
        second[tile, :] = (unit * vector(MLP_GAIN) + vector(MLP_SHIFT)).astype(BF)
        return 0

    lax.fori_loop(0, rows // MT, branch_tile, 0)
    def core_copy(i):
        a = lax.rem(i, CORE_SLOTS)
        return send(part.at[lax.rem(i, 2), 1 - place.c], crecv.at[a], ref.cs.at[a], ref.cr.at[a],
                    place.at(c=1 - place.c))

    def y_copy(i, k):
        a = lax.rem(i, SLOTS)
        return send(ysum.at[a, place.ahead_y(k)], yrecv.at[a, k - 1], ref.ys.at[a, k - 1],
                    ref.yr.at[a, k - 1], place.at(y=place.ahead_y(k)))

    def x_copy(i):
        a = lax.rem(i, SLOTS)
        return send(xsum.at[a, 1 - place.x], xrecv.at[a], ref.xs.at[a], ref.xr.at[a],
                    place.at(x=1 - place.x))

    def z_copy(i, k):
        a = lax.rem(i, SLOTS)
        return send(zsum.at[a, place.near_z(k)], zrecv.at[a, k - 1], ref.zs.at[a, k - 1],
                    ref.zr.at[a, k - 1], place.at(z=place.near_z(k)))

    HB, WZ = CB // 2, CW // Z
    x_rows = pl.ds(pl.multiple_of(place.x * HB, HB), HB)
    z_cols = pl.ds(pl.multiple_of(place.z * WZ, WZ), WZ)

    def zg_copy(i, k):
        a = lax.rem(i, SLOTS)
        block = out.at[i, x_rows, z_cols]
        return send(block, block, ref.gs.at[a, k - 1], ref.gr.at[a, k - 1],
                    place.at(z=place.near_z(k)))

    def xg_copy(i):
        a = lax.rem(i, SLOTS)
        block = out.at[i, x_rows]
        return send(block, block, ref.hs.at[a], ref.hr.at[a], place.at(x=1 - place.x))

    def for_store(i, act):
        a = lax.rem(i, SLOTS)
        base = 0
        plan = ((ref.o_down, n_down, False), (ref.o_up, n_up, True), (ref.o_proj, n_proj, False),
                (ref.o_qkv, n_qkv, True))
        for target, count, rows_first in plan:
            u = i - base
            if rows_first:
                r, c = lax.rem(u, blocks), lax.div(u, blocks)
            else:
                r, c = lax.div(u, W // CW), lax.rem(u, W // CW)
            at = (pl.ds(pl.multiple_of(r * CB, CB), CB), pl.ds(pl.multiple_of(c * CW, CW), CW))

            @pl.when((u >= 0) & (u < count))
            def _(target=target, at=at):
                act(load(out.at[i], target.at[at], ref.osem.at[a]))

            base += count

    def add(*terms):
        if len(terms) == 2:
            return terms[0] + terms[1]
        whole = terms[0].astype(F32)
        for term in terms[1:]:
            whole = whole + term.astype(F32)
        return whole.astype(BF)

    def tick(i):
        def stage(lag):
            j = i - lag
            return j, (j >= 0) & (j < total)

        j1, ok1 = stage(1)

        @pl.when(ok1)
        def _():
            core_copy(j1).wait()
            a = lax.rem(j1, SLOTS)
            for y in range(Y):
                ysum[a, y] = add(part[lax.rem(j1, 2), place.c, y], crecv[lax.rem(j1, CORE_SLOTS), y])
            for k in range(1, Y):
                y_copy(j1, k).start()

        j2, ok2 = stage(1 + LAG)

        @pl.when(ok2)
        def _():
            a = lax.rem(j2, SLOTS)
            for k in range(1, Y):
                y_copy(j2, k).wait()
            for h in range(2):
                piece = slice(h * HB, (h + 1) * HB)
                xsum[a, h] = add(ysum[a, place.y, piece], *[yrecv[a, k - 1, piece] for k in range(1, Y)])
            x_copy(j2).start()

        j3, ok3 = stage(1 + 2 * LAG)

        @pl.when(ok3)
        def _():
            a = lax.rem(j3, SLOTS)
            x_copy(j3).wait()
            for z in range(Z):
                cols = slice(z * WZ, (z + 1) * WZ)
                zsum[a, z] = add(xsum[a, place.x, :, cols], xrecv[a, :, cols])
            for k in place.z_order():
                z_copy(j3, k).start()

        j4, ok4 = stage(1 + 3 * LAG)

        @pl.when(ok4)
        def _():
            a = lax.rem(j4, SLOTS)
            for k in range(1, Z):
                z_copy(j4, k).wait()
            out[j4, x_rows, z_cols] = add(zsum[a, place.z], *[zrecv[a, k - 1] for k in range(1, Z)])
            for k in place.z_order():
                zg_copy(j4, k).start()

        j5, ok5 = stage(1 + 4 * LAG)

        @pl.when(ok5)
        def _():
            for k in range(1, Z):
                zg_copy(j5, k).wait()
            xg_copy(j5).start()

        j6, ok6 = stage(1 + 5 * LAG)

        @pl.when(ok6)
        def _():
            xg_copy(j6).wait()
            for_store(j6, lambda copy: copy.start())

        j7, ok7 = stage(2 + 5 * LAG)

        @pl.when(ok7)
        def _():
            for_store(j7, lambda copy: copy.wait())

    def produce(i, left, offset, cols):
        slot = lax.rem(i, 2)
        for turn in range(2):
            c = 1 - place.c if turn == 0 else place.c
            for y in range(Y):
                first = offset(place.part(y, c))
                if CB % 128 == 0:
                    first = pl.multiple_of(first, 128)
                    value = matmul(left[:, pl.ds(first, CB)], cols, ((0,), (0,))).astype(BF)
                else:
                    start = pl.multiple_of(lax.div(first, 128) * 128, 128)
                    ref.tile[...] = matmul(left[:, pl.ds(start, 128)], cols, ((0,), (0,)))
                    value = ref.tile[pl.ds(pl.multiple_of(first - start, CB), CB)].astype(BF)
                part[slot, c, y] = value
            if turn == 0:
                core_copy(i).start()

    def columns(array, n):
        return array[:, pl.ds(pl.multiple_of(n * CW, CW), CW)]

    acc, gmid, act, slope = ref.acc, ref.gmid, ref.act_s, ref.slope_s
    spread = []
    for b in range(n_blocks):
        goal, over = need[min(b + 1, n_blocks - 1)]
        spread.append((goal, over, need[min(b + 2, n_blocks - 1)][1]))

    def block_step(b, _):
        slot = lax.rem(b, 2)
        for copy in block_loads(b):
            copy.wait()

        for at, (goal, over, soon) in enumerate(spread):
            @pl.when(b == at)
            def _(at=at, goal=goal, over=over, soon=soon):
                gather_until(goal)
                gather_step(done[1] + 3)
                for h in range(spread[at - 1][1] if at else need[0][1], over):
                    if at == 0:
                        direct_step(h)
                    direct_arrived(h)
                for h in range(spread[at - 1][2] if at else over, soon):
                    direct_step(h)

        @pl.when(b + 1 < n_blocks)
        def _():
            for copy in block_loads(b + 1):
                copy.start()

        spots = []
        for p in range(shards):
            row, col = UP_B + p * down_rows // W, p * down_rows % W
            spots.append((slice(row, row + 1), pl.ds(pl.multiple_of(col + b * BW, BW), BW)))
        bias = jnp.concatenate([vec[spot] for spot in spots], axis=1)
        for t in range(rows // MT):
            tile = slice(t * MT, (t + 1) * MT)
            hidden = matmul(second[tile, :], ref.wu[slot]) + bias
            gate = 0.5 * (1.0 + lax.erf(hidden * (0.5**0.5)))
            act[tile, :] = (hidden * gate).astype(BF)
            bell = jnp.exp(-0.5 * hidden * hidden) * 0.3989422804014327
            slope[tile, :] = gate + hidden * bell

        def chunk(n):
            r, c = n // (W // CW), n % (W // CW)
            produce(b * per_block + n, act, lambda p: p * BW + r * CB, columns(gfeed, c))
            tick(b * per_block + n)

        chunk(0)
        sums = [0.0] * shards
        for t in range(rows // MT):
            tile = slice(t * MT, (t + 1) * MT)
            pre = (matmul(gfeed[tile, :], ref.wd[slot], ((1,), (1,))) * slope[tile, :]).astype(BF)
            for p in range(shards):
                mid = pre[:, p * BW : (p + 1) * BW]
                gpre[tile, pl.ds(pl.multiple_of(p * down_rows + b * BW, BW), BW)] = mid
                sums[p] = sums[p] + jnp.sum(mid.astype(F32), axis=0, keepdims=True)
            more = matmul(pre, ref.wu[slot], ((1,), (1,)))
            feed = matmul(act[tile, :], ref.wd[slot])

            @pl.when(b == 0)
            def _():
                gmid[tile, :] = more
                acc[tile, :] = feed

            @pl.when(b > 0)
            def _():
                gmid[tile, :] += more
                acc[tile, :] += feed

            if t == 0:
                for n in range(1, per_block):
                    chunk(n)
        for p in range(shards):
            row, cols = spots[p]
            small[row, cols] = sums[p]
        return 0

    lax.fori_loop(0, n_blocks, block_step, 0)

    tok_out, tok_send, tok_own = ref.tok_out, ref.tok_send, ref.tok_own

    def to_owner(t, value, kept, given):
        if R >= TM:
            lower = pl.ds(pl.multiple_of(lax.rem(t * TM, R), TM), TM)

            @pl.when(t * TM < R)
            def _():
                kept[lower, :] = value.astype(kept.dtype)

            @pl.when(t * TM >= R)
            def _():
                given[lower, :] = value.astype(BF)
        else:
            kept[...] = value[:R].astype(kept.dtype)
            given[...] = value[R:].astype(BF)

    def middle_tile(t, _):
        tile = pl.ds(pl.multiple_of(t * TM, TM), TM)
        low = branch[tile, :]
        middle = x_s[tile, :].astype(F32) + vector(ATTN_SCALE) * low
        feed = acc[tile, :] + vector(DOWN_B)
        to_owner(t, (middle + vector(MLP_SCALE) * feed) * vector(LIVE), tok_own, tok_send)
        upstream = cot[tile, :].astype(F32) * vector(LIVE)
        note(MLP_SCALE, jnp.sum(upstream * feed, axis=0, keepdims=True))
        unit, scale = norm_parts(middle)
        grad = gmid[tile, :]
        note(MLP_GAIN, jnp.sum(grad * unit, axis=0, keepdims=True))
        note(MLP_SHIFT, jnp.sum(grad, axis=0, keepdims=True))
        grad = upstream + norm_back(grad, unit, scale, vector(MLP_GAIN))
        gmid[tile, :] = grad
        note(ATTN_SCALE, jnp.sum(grad * low, axis=0, keepdims=True))
        grad = (grad * vector(ATTN_SCALE)).astype(BF)
        gbranch[tile, :] = grad
        note(PROJ_B, jnp.sum(grad.astype(F32), axis=0, keepdims=True))
        gatt[tile, :] = matmul(grad, ref.proj_s[...], ((1,), (1,))).astype(BF)
        return 0

    def up_chunk(u):
        i = n_down + u
        b, n = lax.rem(u, blocks), lax.div(u, blocks)
        produce(i, second, lambda p: p * other_rows + b * CB, columns(gpre, n))
        tick(i)

    early_up = rows // TM if n_up >= 2 * pairs else 0

    def middle_step(t, _):
        if early_up:
            up_chunk(t)
        return middle_tile(t, 0)

    lax.fori_loop(0, rows // TM, middle_step, 0)
    tok_copy = send(tok_send, tok_out.at[mine], ref.ts.at[0], ref.tr.at[0], swap_peer)
    tok_store = load(tok_own, tok_out.at[mine], ref.lsem.at[11])
    tok_store.start()

    def qkv_load(n):
        slot = lax.rem(n, 2)
        return load(ref.g_qkv.at[:, pl.ds(pl.multiple_of(n * CW, CW), CW)], ref.wu.at[slot, :, pl.ds(0, CW)],
                    ref.qsem.at[slot])

    pown, psend, precv = ref.pown, ref.psend, ref.precv
    gk_acc, gv_acc = ref.gk_acc, ref.gv_acc

    def pair_copy(p, k):
        a = lax.rem(p, PAIR_SLOTS)
        return send(psend.at[a, k - 1], precv.at[a, k - 1], ref.ps.at[a, k - 1], ref.pr.at[a, k - 1],
                    half_peer(k))

    def pair_done(p):
        a = lax.rem(p, PAIR_SLOTS)
        for k in range(1, half):
            pair_copy(p, k).wait()
        for which in range(2):
            whole = pown[a, which]
            for k in range(1, half):
                whole = whole + precv[a, k - 1, which].astype(F32)
            cols = pl.ds(pl.multiple_of((which + 1) * W + p * 128, 128), 128)
            G[:, cols] = whole.astype(BF)

    per_pair = n_up // pairs

    def pair_step(p, _):
        if per_pair:
            for m in range(max(1, per_pair - tiles + 1)):
                @pl.when(p * per_pair + m >= early_up)
                def _(m=m):
                    up_chunk(p * per_pair + m)
        else:
            @pl.when(lax.rem(p, pairs // n_up) == 0)
            def _():
                up_chunk(lax.div(p, pairs // n_up))

        lane = lax.broadcasted_iota(jnp.int32, (1, 128), 1)
        cols = pl.ds(pl.multiple_of(p * 128, 128), 128)
        key, value = kv[0, :, cols], kv[1, :, cols]
        key_t = key.T
        for t in range(tiles):
            tile = slice(t * QT, (t + 1) * QT)
            own = both_heads(query[tile, cols] * BF(HEAD_DIM**-0.5), lane)
            own_grad = both_heads(gatt[tile, cols], lane)
            logs = jnp.concatenate([lse[p, :, tile], lse[p, :, rows + t * QT : rows + (t + 1) * QT]], axis=1)
            probs = jnp.exp(matmul(key, own, ((1,), (1,))) - logs)
            grad_probs = matmul(value, own_grad, ((1,), (1,)))
            centre = jnp.sum(grad_probs * probs, axis=0, keepdims=True)
            grad_scores = (probs * (grad_probs - centre)).astype(BF)
            gv = matmul(probs.astype(BF), own_grad)
            gk = matmul(grad_scores, own)
            if t == 0:
                gv_acc[...], gk_acc[...] = gv, gk
            else:
                gv_acc[...] += gv
                gk_acc[...] += gk
            G[tile, cols] = (own_heads(matmul(key_t, grad_scores)) * HEAD_DIM**-0.5).T.astype(BF)
            if per_pair and t < tiles - 1:
                u = p * per_pair + max(1, per_pair - tiles + 1) + t

                @pl.when(u >= early_up)
                def _(u=u):
                    up_chunk(u)
        a = lax.rem(p, PAIR_SLOTS)
        pown[a, 0], pown[a, 1] = gk_acc[:rows], gv_acc[:rows]
        for k in range(1, half):
            psend[a, k - 1, 0] = gk_acc[k * rows : (k + 1) * rows].astype(BF)
            psend[a, k - 1, 1] = gv_acc[k * rows : (k + 1) * rows].astype(BF)
            pair_copy(p, k).start()

        @pl.when(p >= 1)
        def _():
            pair_done(p - 1)
        return 0

    lax.fori_loop(0, pairs, pair_step, 0)

    qkv_load(0).start()

    def proj_step(u, _):
        i = n_down + n_up + u
        r, c = lax.div(u, W // CW), lax.rem(u, W // CW)
        produce(i, attended, lambda p: p * other_rows + r * CB, columns(gbranch, c))
        tick(i)

        @pl.when(u == 0)
        def _():
            pair_done(pairs - 1)
        return 0

    lax.fori_loop(0, n_proj, proj_step, 0)

    def qkv_step(n, _):
        cols = columns(G, n)
        for b in range(blocks):
            i = n_down + n_up + n_proj + n * blocks + b
            produce(i, first, lambda p: p * other_rows + b * CB, cols)
            tick(i)
            if b == 0:
                qkv_load(n).wait()

                @pl.when(n + 1 < 3 * W // CW)
                def _():
                    qkv_load(n + 1).start()

                for t in range(rows // MT):
                    tile = slice(t * MT, (t + 1) * MT)
                    term = matmul(cols[tile, :], ref.wu[lax.rem(n, 2), :, :CW], ((1,), (1,)))

                    @pl.when(n == 0)
                    def _():
                        acc[tile, :] = term

                    @pl.when(n > 0)
                    def _():
                        acc[tile, :] += term
        return 0

    lax.fori_loop(0, 3 * W // CW, qkv_step, 0)

    gt_own, gt_send = ref.gt_own_s, ref.gt_send

    def first_tile(t, _):
        tile = pl.ds(pl.multiple_of(t * TM, TM), TM)
        unit, scale = norm_parts(x_s[tile, :].astype(F32))
        grad = acc[tile, :]
        note(ATTN_GAIN, jnp.sum(grad * unit, axis=0, keepdims=True))
        note(ATTN_SHIFT, jnp.sum(grad, axis=0, keepdims=True))
        note(QV, jnp.sum(G[tile, :W].astype(F32), axis=0, keepdims=True))
        note(QV + 1, jnp.sum(G[tile, 2 * W :].astype(F32), axis=0, keepdims=True))
        to_owner(t, gmid[tile, :] + norm_back(grad, unit, scale, vector(ATTN_GAIN)), gt_own, gt_send)
        return 0

    lax.fori_loop(0, rows // TM, first_tile, 0)

    cw = W // shards
    packs = ref.packs
    for p in range(shards):
        at = 0
        for row, count in SMALL_ROWS:
            for r in range(count):
                t = p * count + r
                line, col = row + t // shards, t % shards * cw
                packs[p % 2, p // 2, at : at + 1, :] = small[line : line + 1, col : col + cw]
                at += 1

    sums = ref.sums
    core_small = send(packs.at[1 - place.c], ref.core_pack, ref.ss.at[0], ref.sr.at[0], place.at(c=1 - place.c))
    y_small = [send(packs.at[place.c, place.ahead_y(k)], sums.at[0, k], ref.ss.at[k], ref.sr.at[k],
                    place.at(y=place.ahead_y(k))) for k in range(1, Y)]
    x_small = [send(sums.at[1, 0], sums.at[1, 1], ref.ss.at[Y], ref.sr.at[Y], place.at(x=1 - place.x))]
    z_small = [send(sums.at[2, 0], sums.at[2, k], ref.ss.at[Y + k], ref.sr.at[Y + k],
                    place.at(z=place.near_z(k))) for k in range(1, Z)]

    def small_step(step):
        if step == 0:
            core_small.wait()
            for y in range(Y):
                packs[place.c, y] = packs[place.c, y] + ref.core_pack[y]
            for copy in y_small:
                copy.start()
            return
        copies = (y_small, x_small, z_small)[step - 1]
        for copy in copies:
            copy.wait()
        whole = packs[place.c, place.y] if step == 1 else sums[step - 1, 0]
        for k in range(len(copies)):
            whole = whole + sums[step - 1, k + 1]
        if step < 3:
            sums[step, 0] = whole
            for copy in (x_small, z_small)[step - 1]:
                copy.start()
        else:
            ref.small_out[...] = whole

    core_small.start()
    gt_copy = send(gt_send, ref.gt_low, ref.ts.at[1], ref.tr.at[1], swap_peer)
    gt_store = load(gt_own, ref.gt_own, ref.lsem.at[10])
    gt_store.start()
    depth = 3 + 5 * LAG
    small_after = {0: 0, 2 + LAG: 1, 2 + 2 * LAG: 2, 2 + 3 * LAG: 3}
    for lag in range(depth):
        tick(total + lag)
        if lag in small_after:
            small_step(small_after[lag])
        if lag == 0:
            gt_copy.start()
            tok_copy.start()
    for copy in (tok_store, gt_store, gt_copy, tok_copy):
        copy.wait()


def layer(replicas, shards, vectors, count, tokens, cotangent, weights):
    Y, Z, half = shards // 2, replicas // 2, shards // 2
    _, R, W = tokens.shape
    rows, keys = 2 * R, half * 2 * R
    FF = weights[UP].shape[1]
    CB, CW = min(128, W // shards), max(512, 128 * Z)
    HB, WZ = CB // 2, CW // Z
    total = (FF // shards // CB) * (W // CW) + (W // shards // CB) * ((FF + 4 * W) // CW)
    peers = max(Y, Z, 2)
    staged, direct, _ = gather_items(replicas, shards, W, FF)
    m = len(staged) + len(direct)
    multiples = tuple(v.shape[0] // (W // shards) for v in vectors)
    if (W // shards) % 128:
        vectors = [v.reshape(n, W // shards) for v, n in zip(vectors, multiples)]
    dma = pltpu.SemaphoreType.DMA
    vmem, anywhere = pl.BlockSpec(memory_space=pltpu.VMEM), pl.BlockSpec(memory_space=pl.ANY)
    inputs = dict(count=count, tokens=tokens, cotangent=cotangent, qkv=weights[QKV], proj=weights[PROJ],
                  up=weights[UP], down=weights[DOWN])
    scratch = dict(
        part=pltpu.VMEM((2, 2, Y, CB, CW), BF),
        crecv=pltpu.VMEM((CORE_SLOTS, Y, CB, CW), BF),
        ysum=pltpu.VMEM((SLOTS, Y, CB, CW), BF),
        yrecv=pltpu.VMEM((SLOTS, Y - 1, CB, CW), BF),
        xsum=pltpu.VMEM((SLOTS, 2, HB, CW), BF),
        xrecv=pltpu.VMEM((SLOTS, HB, CW), BF),
        zsum=pltpu.VMEM((SLOTS, Z, HB, WZ), BF),
        zrecv=pltpu.VMEM((SLOTS, Z - 1, HB, WZ), BF),
        out=pltpu.VMEM((total, CB, CW), BF),
        small_buf=pltpu.VMEM((16, W), F32),
        packs=pltpu.VMEM((2, Y, 16, W // shards), F32),
        core_pack=pltpu.VMEM((Y, 16, W // shards), F32),
        sums=pltpu.VMEM((3, peers, 16, W // shards), F32),
        kv=pltpu.VMEM((2, keys, W), BF),
        gpre=pltpu.VMEM((rows, FF), BF),
        act_s=pltpu.VMEM((rows, shards * BW), BF),
        slope_s=pltpu.VMEM((rows, shards * BW), F32),
        cot_s=pltpu.VMEM((rows, W), BF),
        gfeed=pltpu.VMEM((rows, W), BF),
        x_s=pltpu.VMEM((rows, W), BF),
        branch_s=pltpu.VMEM((rows, W), F32),
        second_s=pltpu.VMEM((rows, W), BF),
        attended_s=pltpu.VMEM((rows, W), BF),
        query_s=pltpu.VMEM((rows, W), BF),
        first_s=pltpu.VMEM((rows, W), BF),
        proj_s=pltpu.VMEM((W, W), BF),
        wd=pltpu.VMEM((2, shards * BW, W), BF),
        wu=pltpu.VMEM((2, W, shards * BW), BF),
        wq=pltpu.VMEM((W, CW), BF),
        acc=pltpu.VMEM((rows, W), F32),
        gmid=pltpu.VMEM((rows, W), F32),
        gbranch=pltpu.VMEM((rows, W), BF),
        gatt=pltpu.VMEM((rows, W), BF),
        G=pltpu.VMEM((rows, 3 * W), BF),
        pown=pltpu.VMEM((PAIR_SLOTS, 2, rows, 128), F32),
        psend=pltpu.VMEM((PAIR_SLOTS, half - 1, 2, rows, 128), BF),
        precv=pltpu.VMEM((PAIR_SLOTS, half - 1, 2, rows, 128), BF),
        gk_acc=pltpu.VMEM((keys, 128), F32),
        gv_acc=pltpu.VMEM((keys, 128), F32),
        tok_send=pltpu.VMEM((R, W), BF),
        gt_send=pltpu.VMEM((R, W), BF),
        tok_own=pltpu.VMEM((R, W), BF),
        gt_own_s=pltpu.VMEM((R, W), F32),
        small_s=pltpu.VMEM((shards, 16, W // shards), F32),
        vec=pltpu.VMEM((16, W), F32),
        lse=pltpu.VMEM((W // 128, 1, 2 * rows), F32),
        lsem=dma((12,)), wsem=dma((2, 2, shards)), qsem=dma((3,)), osem=dma((SLOTS,)),
        gys=dma((m, Y - 1)), gyr=dma((m, Y - 1)),
        gzs=dma((m, Y - 1, Z - 1)), gzr=dma((m, Y - 1, Z - 1)),
        gxs=dma((m, Y - 1)), gxr=dma((m, Y - 1)),
        gcs=dma((m, Y - 1)), gcr=dma((m, Y - 1)),
        os=dma((4,)), orr=dma((4,)),
        vs=dma((shards - 1,)), vr=dma((shards - 1,)),
        ks=dma((2, W // CW, half - 1)), kr=dma((2, W // CW, half - 1)),
        cs=dma((CORE_SLOTS,)), cr=dma((CORE_SLOTS,)),
        ys=dma((SLOTS, Y - 1)), yr=dma((SLOTS, Y - 1)),
        xs=dma((SLOTS,)), xr=dma((SLOTS,)),
        zs=dma((SLOTS, Z - 1)), zr=dma((SLOTS, Z - 1)),
        gs=dma((SLOTS, Z - 1)), gr=dma((SLOTS, Z - 1)),
        hs=dma((SLOTS,)), hr=dma((SLOTS,)),
        ps=dma((PAIR_SLOTS, half - 1)), pr=dma((PAIR_SLOTS, half - 1)),
        ss=dma((Y + Z,)), sr=dma((Y + Z,)),
        ts=dma((4,)), tr=dma((4,)),
    )
    if CB % 128:
        scratch["tile"] = pltpu.VMEM((128, CW), F32)
    outs = dict(
        o_down=jax.ShapeDtypeStruct((FF // shards, W), BF),
        o_up=jax.ShapeDtypeStruct((W // shards, FF), BF),
        o_proj=jax.ShapeDtypeStruct((W // shards, W), BF),
        o_qkv=jax.ShapeDtypeStruct((W // shards, 3 * W), BF),
        small_out=jax.ShapeDtypeStruct((16, W // shards), F32),
        tok_out=jax.ShapeDtypeStruct((2, R, W), BF),
        gt_own=jax.ShapeDtypeStruct((R, W), F32),
        gt_low=jax.ShapeDtypeStruct((R, W), BF),
        g_qkv=jax.ShapeDtypeStruct((W, 3 * W), BF),
        g_proj=jax.ShapeDtypeStruct((W, W), BF),
        g_up=jax.ShapeDtypeStruct((W, FF), BF),
        g_down=jax.ShapeDtypeStruct((FF, W), BF),
    )
    names = tuple(inputs) + tuple(outs) + tuple(scratch)
    results = pl.pallas_call(
        functools.partial(layer_kernel, replicas, shards, multiples, names),
        in_specs=[vmem] * len(vectors) + [pl.BlockSpec(memory_space=pltpu.SMEM)] + [anywhere] * 6,
        out_specs=[anywhere] * 4 + [vmem] + [anywhere] * 7,
        out_shape=list(outs.values()),
        scratch_shapes=list(scratch.values()),
        compiler_params=pltpu.CompilerParams(
            collective_id=0, has_side_effects=True, vmem_limit_bytes=63 * MIB
        ),
    )(*vectors, *inputs.values())
    return results[:8]


def result_kernel(shards, n_vectors, *refs):
    small, tok, gt_own, gt_low, *ins = refs[:8]
    tok_out, gt_out, *outs = refs[8:14]
    vectors = refs[14 : 14 + n_vectors]
    low, wide, tok_s, own_s, low_s, gt_s, in_sem, out_sem = refs[14 + n_vectors :]
    mine = lax.div(lax.axis_index("shard"), shards // 2)
    size, width = low.shape[1:]
    blocks = []
    for source, target in zip(ins, outs):
        for r in range(source.shape[0] // size):
            for c in range(source.shape[1] // width):
                at = (pl.ds(r * size, size), pl.ds(c * width, width))
                blocks.append((source.at[at], target.at[at]))
    n = len(blocks)
    loads = [pltpu.make_async_copy(src, low.at[i], in_sem.at[i]) for i, (src, _) in enumerate(blocks)]
    stores = [pltpu.make_async_copy(wide.at[i], dst, out_sem.at[i]) for i, (_, dst) in enumerate(blocks)]
    for i, (source, middle) in enumerate(((gt_low, low_s), (gt_own, own_s), (tok, tok_s))):
        loads.append(pltpu.make_async_copy(source, middle, in_sem.at[n + i]))
    stores += [
        pltpu.make_async_copy(gt_s, gt_out.at[1 - mine], out_sem.at[n]),
        pltpu.make_async_copy(own_s, gt_out.at[mine], out_sem.at[n + 1]),
        pltpu.make_async_copy(tok_s, tok_out, out_sem.at[n + 2]),
    ]
    for copy in loads:
        copy.start()
    at = 0
    for (_, count), vector in zip(SMALL_ROWS, vectors):
        pieces = [small[at + r : at + r + 1, :] for r in range(count)]
        vector[...] = jnp.concatenate(pieces, axis=1).reshape(vector.shape)
        at += count
    for i in range(n + 3):
        loads[i].wait()
        if i < n:
            wide[i] = low[i].astype(F32)
        elif i == n:
            gt_s[...] = low_s[...].astype(F32)
        stores[i].start()
    for copy in stores:
        copy.wait()


def results(shards, small, tok, gt_own, gt_low, grads):
    _, R, W = tok.shape
    size = W // shards
    count = sum(grad.shape[0] * grad.shape[1] for grad in grads) // (size * W)
    vmem, anywhere = pl.BlockSpec(memory_space=pltpu.VMEM), pl.BlockSpec(memory_space=pl.ANY)
    shapes = [jax.ShapeDtypeStruct(tok.shape, BF), jax.ShapeDtypeStruct(tok.shape, F32)]
    shapes += [jax.ShapeDtypeStruct(grad.shape, F32) for grad in grads]
    n_vectors = len(SMALL_ROWS) if size % 128 == 0 else 0
    for _, rows in SMALL_ROWS[:n_vectors]:
        shapes.append(jax.ShapeDtypeStruct((rows * size,), F32))
    dma = pltpu.SemaphoreType.DMA
    tok, gt, *rest = pl.pallas_call(
        functools.partial(result_kernel, shards, n_vectors),
        in_specs=[vmem] + [anywhere] * 7,
        out_specs=[anywhere] * 6 + [vmem] * n_vectors,
        out_shape=shapes,
        scratch_shapes=[
            pltpu.VMEM((count, size, W), BF), pltpu.VMEM((count, size, W), F32),
            pltpu.VMEM(tok.shape, BF), pltpu.VMEM((R, W), F32), pltpu.VMEM((R, W), BF), pltpu.VMEM((R, W), F32),
            dma((count + 3,)), dma((count + 3,)),
        ],
        compiler_params=pltpu.CompilerParams(vmem_limit_bytes=63 * MIB),
    )(small, tok, gt_own, gt_low, *grads)
    vectors = rest[4:]
    if not n_vectors:
        at = 0
        for _, rows in SMALL_ROWS:
            vectors.append(small[at : at + rows].reshape(-1))
            at += rows
    return tok, gt, rest[:4], vectors


def on_device(replicas, shards, tokens, qkv_weight, qv_bias, proj_weight, proj_bias, up_weight, up_bias,
              down_weight, down_bias, attn_gain, attn_shift, mlp_gain, mlp_shift, attn_scale, mlp_scale,
              cotangent, image_count):
    vectors = (qv_bias, proj_bias, up_bias, down_bias, attn_gain, attn_shift, mlp_gain, mlp_shift,
               attn_scale, mlp_scale)
    *grads, small, output, grad_own, grad_low = layer(
        replicas, shards, vectors, image_count, tokens, cotangent,
        (qkv_weight, proj_weight, up_weight, down_weight),
    )
    output, grad_tokens, (down, up, proj, qkv), small = results(
        shards, small, output, grad_own, grad_low, grads)
    qv_b, proj_b, up_b, down_b, *norms = small
    return (output, grad_tokens, qkv, qv_b, proj, proj_b, up, up_b, down, down_b, *norms)


def solution(mesh):
    rows, vector = P("shard", None), P("shard")
    image = P("replica", "shard", None)
    in_specs = (image, rows, vector, rows, vector, rows, vector, rows, vector, vector, vector, vector,
                vector, vector, vector, image, P())
    out_specs = (image, image, rows, vector, rows, vector, rows, vector, rows, vector, vector, vector,
                 vector, vector, vector, vector)
    return jax.shard_map(
        functools.partial(on_device, mesh.shape["replica"], mesh.shape["shard"]),
        mesh=mesh, in_specs=in_specs, out_specs=out_specs, check_vma=False,
    )
```
